128 devices in a mesh: section: 2 (over core), seq: 4 (over x), fsdp: 16 (over z, y).
Axes of the slice: x: 4, y: 4, z: 4, core: 2. Of those that a mesh axis runs over, the one named last changes fastest.
Arguments:
- block_in: bfloat16 [2, 16, 256, 1024], P(None, 'fsdp', 'seq'), may hold values from -6 to 6
- cotangent: bfloat16 [2, 16, 256, 1024], P(None, 'fsdp', 'seq'), may hold values from -6 to 6
- perm_rows: int32 [2, 16, 256], P(None, 'fsdp'), may hold values from 0 to 255, each once within a row
- doc_lengths: int32 [2, 16, 4], P(None, 'fsdp'), may hold values from 1 to 192, 256 in all within a row
- norm_in: float32 [2, 1024], P('section'), may hold values from 0.5 to 1.5
- w_qkv: bfloat16 [2, 1024, 3072], P('section', 'fsdp'), may hold values from -0.1875 to 0.1875
- w_beta: bfloat16 [2, 1024, 8], P('section', 'fsdp'), may hold values from -0.1875 to 0.1875
- conv_w: float32 [2, 4, 3, 1024], P('section'), may hold values from -3 to 3
- norm_head: float32 [2, 128], P('section'), may hold values from 0.5 to 1.5
- w_out: bfloat16 [2, 1024, 1024], P('section', 'fsdp'), may hold values from -0.1875 to 0.1875
- norm_ffn: float32 [2, 1024], P('section'), may hold values from 0.5 to 1.5
- w_ffn: bfloat16 [2, 2, 1024, 2816], P('section', None, None, 'fsdp'), may hold values from -0.1875 to 0.1875
- w_down: bfloat16 [2, 2816, 1024], P('section', 'fsdp'), may hold values from -0.109375 to 0.109375
Outputs:
- block_out: bfloat16 [2, 16, 256, 1024], P(None, 'fsdp', 'seq')
- input_grad: bfloat16 [2, 16, 256, 1024], P(None, 'fsdp', 'seq')
- grad_norm_in: float32 [2, 1024], P('section')
- grad_qkv: float32 [2, 1024, 3072], P('section', 'fsdp')
- grad_beta: float32 [2, 1024, 8], P('section', 'fsdp')
- grad_conv: float32 [2, 4, 3, 1024], P('section')
- grad_norm_head: float32 [2, 128], P('section')
- grad_out: float32 [2, 1024, 1024], P('section', 'fsdp')
- grad_norm_ffn: float32 [2, 1024], P('section')
- grad_ffn: float32 [2, 2, 1024, 2816], P('section', None, None, 'fsdp')
- grad_down: float32 [2, 2816, 1024], P('section', 'fsdp')
The draws below stay inside these ranges and needn't reach their ends.
Inputs may be any that keep to these rules, and one draw needn't show every extreme that they name: `perm_rows`: each pack's row is a permutation of its positions. `doc_lengths`: A pack's lengths sum to 256; its longest document has exactly 192 tokens.
All inputs are finite; a program needn't handle non-finite values.
Results may differ from the reference program's by a relative error of at most 0.029.
Values may be sent and summed in bfloat16 or wider, within the bound.
A program may use at most 192 MiB of HBM per device.

```python
import math
import jax
import jax.numpy as jnp
import numpy as np
from jax import lax

D = 1024
H = 8
HD = 128
FF = 2816
CONV = 4
SPAN = 64
MB = 2
NDOC = 4
LAYERS = 2
PACK = 256
DOC_MOST = 192
N_FSDP = 16


def block_scale(stream_key, shape, split, low, high):
    loudness, own = 1.0, jax.random.fold_in(stream_key, 6)
    for position, parts in split:
        draws = jnp.exp(jax.random.uniform(jax.random.fold_in(own, position), (parts,), jnp.float32, low / len(split), high / len(split)))
        loudness = loudness * jnp.repeat(draws, shape[position] // parts).reshape([-1 if axis == position else 1 for axis in range(len(shape))])
    return loudness


def split_up(count, total, bound, skew):
    weights = [(1 << 20) // math.isqrt(standing ** skew) + 1 for standing in range(2, count + 1)]
    surplus, given = total - bound - (count - 1), [1] * (count - 1)
    while surplus > 0:
        movable = [i for i in range(count - 1) if given[i] < bound]
        mass, budget = sum([weights[i] for i in movable]), surplus
        for i in movable:
            addition = min(bound - given[i], max(1, budget * weights[i] // mass), surplus)
            given[i] = given[i] + addition
            surplus = surplus - addition
    return np.array([bound] + given)


def uneven(rng, number_of, total, bound, skew):
    if number_of == 2:
        one = jax.random.randint(rng, (), max(1, total - bound), min(bound, total - 1) + 1)
        return jnp.stack([one, total - one])
    sizes = jnp.asarray(split_up(number_of, total, bound, skew), jnp.int32)
    pairs = (number_of - 1) // 2
    donor, receiver = sizes[1:1 + 2 * pairs:2], sizes[2:2 + 2 * pairs:2]
    room = jnp.minimum(donor - 1, bound - receiver)
    moved = jax.random.randint(jax.random.fold_in(rng, 1), (pairs,), 0, 1 << 20) % (room + 1)
    sizes = sizes.at[1:1 + 2 * pairs:2].set(donor - moved).at[2:2 + 2 * pairs:2].set(receiver + moved)
    return sizes[jax.random.permutation(jax.random.fold_in(rng, 2), number_of)]


def noise(key, dims, scale, limit, shards=(), held_as=jnp.bfloat16):
    loudness = block_scale(key, dims, shards, -0.22, 0.18) if shards else 1.0
    entries = jax.random.normal(key, dims, jnp.float32) * scale * loudness
    return jnp.minimum(jnp.maximum(entries, -limit), limit).astype(held_as)


def setup_inputs(seed: int = 0) -> dict:
    seeds = jax.random.split(jax.random.key(seed), 14)
    block_in = noise(seeds[0], (MB, N_FSDP, PACK, D), 1.0, 6.0, ((1, 16), (2, 4)))
    cotangent = noise(seeds[1], (MB, N_FSDP, PACK, D), 1.0, 6.0, ((1, 16), (2, 4)))
    perm_rows = jax.vmap(lambda own: jax.random.permutation(own, PACK))(jax.random.split(seeds[2], MB * N_FSDP)).reshape((MB, N_FSDP, PACK)).astype(jnp.int32)
    doc_lengths = jax.vmap(lambda own: uneven(own, NDOC, PACK, DOC_MOST, 2))(jax.random.split(seeds[3], MB * N_FSDP)).reshape((MB, N_FSDP, NDOC)).astype(jnp.int32)
    norm_in = jnp.clip(1.0 + 0.1 * jax.random.normal(seeds[4], (LAYERS, D), jnp.float32), 0.5, 1.5)
    w_qkv = noise(seeds[5], (LAYERS, D, 3 * D), D ** -0.5, 0.1875, ((0, 2), (1, 16)))
    w_beta = noise(seeds[6], (LAYERS, D, H), D ** -0.5, 0.1875, ((0, 2), (1, 16)))
    conv_w = noise(seeds[7], (LAYERS, CONV, 3, D), 0.5, 3.0, ((0, 2),), jnp.float32)
    norm_head = jnp.clip(1.0 + 0.1 * jax.random.normal(seeds[8], (LAYERS, HD), jnp.float32), 0.5, 1.5)
    w_out = noise(seeds[9], (LAYERS, D, D), D ** -0.5, 0.1875, ((0, 2), (1, 16)))
    norm_ffn = jnp.clip(1.0 + 0.1 * jax.random.normal(seeds[10], (LAYERS, D), jnp.float32), 0.5, 1.5)
    w_ffn = noise(seeds[11], (LAYERS, 2, D, FF), D ** -0.5, 0.1875, ((0, 2), (3, 16)))
    w_down = noise(seeds[12], (LAYERS, FF, D), FF ** -0.5, 0.109375, ((0, 2), (1, 16)))
    return {"block_in": block_in, "cotangent": cotangent, "perm_rows": perm_rows, "doc_lengths": doc_lengths, "norm_in": norm_in, "w_qkv": w_qkv, "w_beta": w_beta, "conv_w": conv_w, "norm_head": norm_head, "w_out": w_out, "norm_ffn": norm_ffn, "w_ffn": w_ffn, "w_down": w_down}


@jax.custom_vjp
def low(v):
    return lax.optimization_barrier(v.astype(jnp.bfloat16)).astype(jnp.float32)

@jax.custom_vjp
def low_back(v):
    return v

def low_keep(v):
    return (low(v), None)

def low_pass(kept, grad):
    return (grad,)

def back_keep(v):
    return (v, None)

def back_low(kept, grad):
    return (low(grad),)
low.defvjp(low_keep, low_pass)
low_back.defvjp(back_keep, back_low)

def highest_dot(left_side, right_side):
    return jnp.dot(left_side, right_side, precision=lax.Precision.HIGHEST)

def rms_rows(values, scale_by):
    return values * lax.rsqrt(lax.optimization_barrier(jnp.mean(values * values, axis=-1, keepdims=True)) + 1e-06) * scale_by

def unit_rows(values):
    return values * lax.rsqrt(lax.optimization_barrier(jnp.sum(values * values, axis=-1, keepdims=True)) + 1e-06)

def doc_index(doc_len, row_count):
    places = jnp.arange(row_count, dtype=jnp.int32)
    doc_ends = jnp.cumsum(doc_len).astype(jnp.int32)
    return lax.optimization_barrier(jnp.sum((places[:, None] >= doc_ends[None, :]).astype(jnp.int32), axis=1)).astype(jnp.int32)

def short_conv(series, kernel, doc_ids):
    row_count = series.shape[0]
    spread = (1,) * (series.ndim - 1)
    combined = series * kernel[0]
    for lag_step in range(1, kernel.shape[0]):
        padding = ((lag_step, 0),) + ((0, 0),) * (series.ndim - 1)
        shifted = jnp.pad(series, padding)[:row_count]
        earlier = jnp.pad(doc_ids, (lag_step, 0), constant_values=-1)[:row_count]
        within = (earlier == doc_ids).astype(series.dtype).reshape((row_count,) + spread)
        combined = combined + shifted * kernel[lag_step] * within
    return combined

def delta_scan(queries, key_rows, values, strengths, starts):
    row_count, head_count, head_width = queries.shape

    def token_step(memory, pieces):
        query_now, key_now, value_now, strength_now, start_now = pieces
        memory = memory * (1.0 - start_now)
        recall = jnp.einsum('hvk,hk->hv', memory, key_now, precision=lax.Precision.HIGHEST)
        memory = memory + strength_now[:, None, None] * (value_now - recall)[:, :, None] * key_now[:, None, :]
        return (memory, jnp.einsum('hvk,hk->hv', memory, query_now, precision=lax.Precision.HIGHEST))

    def block_step(memory, pieces):
        return lax.scan(token_step, memory, pieces)
    blocks = tuple((array.reshape((row_count // SPAN, SPAN) + array.shape[1:]) for array in (queries, key_rows, values, strengths, starts)))
    start_memory = jnp.zeros((head_count, head_width, head_width), queries.dtype)
    _, produced = lax.scan(jax.checkpoint(block_step), start_memory, blocks)
    return produced.reshape(row_count, head_count, head_width)

def head_part(projected, logits, kernel, head_gain, perm_row, doc_len):
    row_count, _, head_count, head_width = projected.shape
    places = jnp.arange(row_count, dtype=jnp.int32)
    inverse = jnp.zeros((row_count,), jnp.int32).at[perm_row].set(places)
    series = projected[inverse]
    strengths = jax.nn.sigmoid(logits[inverse][:, 0])
    doc_ids = doc_index(doc_len, row_count)
    earlier = jnp.pad(doc_ids, (1, 0), constant_values=-1)[:row_count]
    starts = (earlier != doc_ids).astype(projected.dtype)
    activated = jax.nn.silu(short_conv(series, kernel.reshape(kernel.shape[0], 3, head_count, head_width), doc_ids))
    queries = unit_rows(activated[:, 0]) * head_width ** (-0.5)
    key_rows = unit_rows(activated[:, 1])
    values = activated[:, 2]
    produced = delta_scan(queries, key_rows, values, strengths, starts)
    normed = produced * lax.rsqrt(lax.optimization_barrier(jnp.mean(produced * produced, axis=-1, keepdims=True)) + 1e-05) * head_gain
    return normed[perm_row]

def layer_pass(weights, rows_in, perm_row, doc_len):
    norm_in, w_qkv, w_beta, conv_w, norm_head, w_out, norm_ffn, w_ffn, w_down = weights
    row_count = rows_in.shape[0]
    normed_in = low(rms_rows(rows_in, norm_in))
    projected = low_back(low(highest_dot(normed_in, w_qkv)))
    logits = low_back(low(highest_dot(normed_in, w_beta)))
    mixed_out = head_part(projected.reshape(row_count, 3, H, HD), logits.reshape(row_count, 1, H), conv_w, norm_head, perm_row, doc_len)
    attended = low_back(low(mixed_out.reshape(row_count, D)))
    residual = rows_in + low_back(highest_dot(attended, w_out))
    normed_ffn = low(rms_rows(residual, norm_ffn))
    gate_pre = low_back(highest_dot(normed_ffn, w_ffn[0]))
    up_pre = low_back(highest_dot(normed_ffn, w_ffn[1]))
    hidden = low(jax.nn.silu(gate_pre) * up_pre)
    return residual + low_back(highest_dot(hidden, w_down))

def reference(block_in, cotangent, perm_rows, doc_lengths, norm_in, w_qkv, w_beta, conv_w, norm_head, w_out, norm_ffn, w_ffn, w_down):
    weights = tuple((member.astype(jnp.float32) for member in (norm_in, w_qkv, w_beta, conv_w, norm_head, w_out, norm_ffn, w_ffn, w_down)))
    inputs = block_in.astype(jnp.float32).reshape(MB * N_FSDP, PACK, D)
    perm_all = perm_rows.reshape(MB * N_FSDP, PACK)
    length_all = doc_lengths.reshape(MB * N_FSDP, NDOC)

    def forward(inputs, weights):

        def one_pack(pieces):
            rows_in, perm_row, doc_len = pieces
            first_out = layer_pass(tuple((member[0] for member in weights)), rows_in, perm_row, doc_len)
            middle = low_back(low(first_out))
            return layer_pass(tuple((member[1] for member in weights)), middle, perm_row, doc_len)
        return lax.map(jax.checkpoint(one_pack), (inputs, perm_all, length_all))
    outputs, pullback = jax.vjp(forward, inputs, weights)
    grad_inputs, grad_weights = pullback(cotangent.astype(jnp.float32).reshape(MB * N_FSDP, PACK, D))
    block_out = outputs.reshape(MB, N_FSDP, PACK, D).astype(jnp.bfloat16)
    input_grad = grad_inputs.reshape(MB, N_FSDP, PACK, D).astype(jnp.bfloat16)
    grads = [member.astype(jnp.float32) for member in grad_weights]
    return (block_out, input_grad, grads[0], grads[1], grads[2], grads[3], grads[4], grads[5], grads[6], grads[7], grads[8])
```

```python
import functools

import jax
import jax.numpy as jnp
from jax import lax
from jax.experimental import pallas as pl
from jax.experimental.pallas import tpu as pltpu
from jax.sharding import PartitionSpec as P

D = 1024
H = 8
HD = 128
PACK = 256
ROWS = 64
UNIT = 48
QW = 896
MESH = pl.DeviceIdType.MESH
F32, BF16 = jnp.float32, jnp.bfloat16
VMEM = pl.BlockSpec(memory_space=pltpu.VMEM)
SMEM = pl.BlockSpec(memory_space=pltpu.SMEM)
ANY = pl.BlockSpec(memory_space=pl.ANY)
VMEM_BYTES = 60 * 1024 * 1024


def sds(shape, dtype):
    return jax.ShapeDtypeStruct(shape, dtype)


def dot(left, right, dims):
    return lax.dot_general(left, right, (dims, ((), ())), preferred_element_type=F32)


NN = ((1,), (0,))
NT = ((1,), (1,))
TN = ((0,), (0,))


def halves(value):
    high = value.astype(BF16)
    return high, (value - high.astype(F32)).astype(BF16)


def dot3(left, right, dims):
    return dot(left[0], right[0], dims) + (
        dot(left[0], right[1], dims) + dot(left[1], right[0], dims)
    )


def place():
    fsdp = lax.axis_index("fsdp")
    return (
        lax.axis_index("section"),
        lax.axis_index("seq"),
        lax.div(fsdp, 4),
        lax.rem(fsdp, 4),
    )


def along_x(seq, step):
    return {"seq": lax.rem(seq + step, 4)}


def along_y(z, y, step):
    return {"fsdp": z * 4 + lax.rem(y + step, 4)}


def along_z(z, y, step):
    return {"fsdp": lax.rem(z + step, 4) * 4 + y}


def greet(peers):
    barrier = pltpu.get_barrier_semaphore()
    for peer in peers:
        pl.semaphore_signal(barrier, inc=1, device_id=peer, device_id_type=MESH)
    pl.semaphore_wait(barrier, len(peers))


def remote(source, target, send, recv, peer):
    return pltpu.make_async_remote_copy(
        src_ref=source,
        dst_ref=target,
        send_sem=send,
        recv_sem=recv,
        device_id=peer,
        device_id_type=MESH,
    )


class RingGather:
    def __init__(self, me, right, left, own, slot, send, recv):
        self.at_left, self.at_right = lax.rem(me + 3, 4), lax.rem(me + 1, 4)
        self.opposite = lax.rem(me + 2, 4)
        self.slot = slot

        def copy(index, half, source, peer, sem):
            return remote(source, slot(index, half), send.at[sem], recv.at[sem], peer)

        self.first = [
            copy(me, 0, own(0), right, 0),
            copy(me, 1, own(1), left, 1),
            copy(me, 1, own(1), right, 2),
            copy(me, 0, own(0), left, 3),
        ]
        self.second = [
            copy(self.at_left, 0, slot(self.at_left, 0), right, 4),
            copy(self.at_right, 1, slot(self.at_right, 1), left, 5),
        ]

    def start(self):
        for copy in self.first:
            copy.start()

    def middle(self):
        self.first[0].wait_recv()
        self.second[0].start()
        self.first[1].wait_recv()
        self.second[1].start()

    def near(self):
        self.first[2].wait_recv()
        self.first[3].wait_recv()

    def far(self):
        self.second[0].wait_recv()
        self.second[1].wait_recv()

    def finish(self):
        for copy in self.first + self.second:
            copy.wait_send()


class RingReduce:
    def __init__(self, me, right, left, part, near, from_left, from_right, send, recv):
        at_right, at_left = lax.rem(me + 1, 4), lax.rem(me + 3, 4)
        opposite = lax.rem(me + 2, 4)
        self.me, self.part, self.near = me, part, near
        self.from_left, self.from_right = from_left, from_right
        self.at_right, self.at_left = at_right, at_left

        def copy(source, target, peer, sem):
            return remote(source, target, send.at[sem], recv.at[sem], peer)

        self.first = [
            copy(part(opposite, 0), near(0), right, 0),
            copy(part(opposite, 1), near(1), left, 1),
            copy(part(at_right, 1), from_left(1), right, 2),
            copy(part(at_left, 0), from_right(0), left, 3),
        ]
        self.second = [
            copy(part(at_right, 0), from_left(0), right, 4),
            copy(part(at_left, 1), from_right(1), left, 5),
        ]

    def start(self):
        for copy in self.first:
            copy.start()

    def middle(self):
        for half, index in ((0, self.at_right), (1, self.at_left)):
            self.first[half].wait_recv()
            add_into(self.part(index, half), [self.near(half)])
            self.second[half].start()

    def arrive(self):
        for copy in (self.first[2], self.first[3], self.second[0], self.second[1]):
            copy.wait_recv()

    def finish(self):
        for copy in self.first + self.second:
            copy.wait_send()

    def total(self):
        for half in (0, 1):
            add_into(self.part(self.me, half), [self.from_left(half), self.from_right(half)])


def add_into(target, others):
    shape = target.shape
    if len(shape) == 2:
        rows = 16
        steps = shape[0] // rows

        def body(step, carry):
            at = pl.ds(pl.multiple_of(step * rows, rows), rows)
            value = target[at, :].astype(F32)
            for other in others:
                value = value + other[at, :].astype(F32)
            target[at, :] = value.astype(target.dtype)
            return carry

        lax.fori_loop(0, steps, body, 0)
    else:
        for index in range(shape[0]):
            add_into(target.at[index], [other.at[index] for other in others])


def spread_kernel(
    x_ref,
    cot_ref,
    small_ref,
    q_ref,
    f_ref,
    o_ref,
    x_out,
    cot_out,
    small_out,
    q_out,
    f_out,
    o_out,
    send,
    recv,
    local,
    o_send,
    o_recv,
    pair_send,
    pair_recv,
):
    core, seq, z, y = place()
    partner = {"section": 1 - core}
    greet(
        [along_x(seq, k) for k in (1, 3)]
        + [along_y(z, y, k) for k in (1, 3)]
        + [along_z(z, y, k) for k in (1, 2, 3)]
        + [partner]
    )

    def cut(half, low):
        return pl.ds(low * half, low)

    own_copies = [
        pltpu.make_async_copy(x_ref, x_out.at[seq], local.at[0]),
        pltpu.make_async_copy(cot_ref, cot_out.at[seq], local.at[1]),
        pltpu.make_async_copy(small_ref, small_out.at[core], local.at[2]),
        pltpu.make_async_copy(q_ref, q_out.at[core, z, y], local.at[3]),
        pltpu.make_async_copy(f_ref, f_out.at[core, :, z, y], local.at[4]),
    ]
    for copy in own_copies:
        copy.start()

    def x_ring(source, target, sem):
        return RingGather(
            seq,
            along_x(seq, 1),
            along_x(seq, 3),
            lambda half: source.at[cut(half, 32)],
            lambda index, half: target.at[index, cut(half, 32)],
            send.at[sem],
            recv.at[sem],
        )

    def y_ring(own, slot, sem):
        return RingGather(
            y, along_y(z, y, 1), along_y(z, y, 3), own, slot, send.at[sem], recv.at[sem]
        )

    def z_ring(own, slot, sem):
        return RingGather(
            z, along_z(z, y, 1), along_z(z, y, 3), own, slot, send.at[sem], recv.at[sem]
        )

    rows_ring = x_ring(x_ref, x_out, 0)
    cot_ring = x_ring(cot_ref, cot_out, 1)
    pair_small = remote(
        small_ref, small_out.at[core], pair_send.at[0], pair_recv.at[0], partner
    )
    o_copies = [
        remote(o_ref, o_out.at[core, y], o_send.at[k], o_recv.at[0], along_z(z, y, k + 1))
        for k in range(3)
    ]
    own_o = pltpu.make_async_copy(o_ref, o_out.at[core, y], local.at[5])

    q_one = z_ring(
        lambda half: q_ref.at[cut(half, 32)],
        lambda index, half: q_out.at[core, index, y, cut(half, 32)],
        2,
    )
    d_one = z_ring(
        lambda half: f_ref.at[2, pl.ds(32 * half, 32 - 16 * half)],
        lambda index, half: f_out.at[core, 2, index, y, pl.ds(32 * half, 32 - 16 * half)],
        3,
    )
    g_one = y_ring(
        lambda half: f_ref.at[half], lambda index, half: f_out.at[core, half, z, index], 4
    )
    q_two = y_ring(
        lambda half: q_out.at[core, cut(half, 2), y],
        lambda index, half: q_out.at[core, cut(half, 2), index],
        5,
    )
    d_two = y_ring(
        lambda half: f_out.at[core, 2, cut(half, 2), y],
        lambda index, half: f_out.at[core, 2, cut(half, 2), index],
        6,
    )
    g_two = z_ring(
        lambda half: f_out.at[core, half, z], lambda index, half: f_out.at[core, half, index], 7
    )
    o_two = y_ring(
        lambda half: o_out.at[core, y, cut(half, 32)],
        lambda index, half: o_out.at[core, index, cut(half, 32)],
        8,
    )

    pair_small.start()
    rows_ring.start()
    q_one.start()
    g_one.start()

    @pl.when(z == seq)
    def _():
        own_o.start()
        for copy in o_copies:
            copy.start()

    d_one.start()
    cot_ring.start()

    rows_ring.middle()
    q_one.middle()
    g_one.middle()
    d_one.middle()
    cot_ring.middle()

    for copy in own_copies:
        copy.wait()

    sent = []

    def to_partner(piece):
        index = len(sent) + 1
        copy = remote(piece, piece, pair_send.at[index], pair_recv.at[index], partner)
        copy.start()
        sent.append(copy)

    q_one.near()
    q_one.far()
    q_two.start()
    to_partner(q_out.at[core, :, y])
    g_one.near()
    g_one.far()
    g_two.start()
    to_partner(f_out.at[core, 0, z])
    to_partner(f_out.at[core, 1, z])

    @pl.when(z == seq)
    def _():
        own_o.wait()
        for copy in o_copies:
            copy.wait_send()

    @pl.when(z != seq)
    def _():
        o_copies[0].wait_recv()

    o_two.start()
    to_partner(o_out.at[core, y])
    d_one.near()
    d_one.far()
    d_two.start()
    to_partner(f_out.at[core, 2, :, y])

    two = [
        (q_two, lambda index, half: q_out.at[core, cut(half, 2), index]),
        (g_two, lambda index, half: f_out.at[core, half, index]),
        (o_two, lambda index, half: o_out.at[core, index, cut(half, 32)]),
        (d_two, lambda index, half: f_out.at[core, 2, cut(half, 2), index]),
    ]
    for ring, piece in two:
        ring.middle()
        to_partner(piece(ring.at_left, 0))
        to_partner(piece(ring.at_right, 1))
    for ring, piece in two:
        ring.near()
        to_partner(piece(ring.at_left, 1))
        to_partner(piece(ring.at_right, 0))
        ring.far()
        to_partner(piece(ring.opposite, 0))
        to_partner(piece(ring.opposite, 1))
    for ring in (rows_ring, cot_ring):
        ring.near()
        ring.far()
    for ring in (rows_ring, cot_ring, q_one, d_one, g_one, q_two, d_two, g_two, o_two):
        ring.finish()
    pair_small.wait()
    for copy in sent:
        copy.wait()


def spread(x, cot, small, q, f, o):
    return pl.pallas_call(
        spread_kernel,
        out_shape=[
            sds((4, ROWS, D), BF16),
            sds((4, ROWS, D), BF16),
            sds((2, 16, D), F32),
            sds((2, 4, 4, 64, QW), BF16),
            sds((2, 3, 4, 4, UNIT, D), BF16),
            sds((2, 4, 64, D), BF16),
        ],
        in_specs=[ANY] * 6,
        out_specs=[ANY] * 6,
        scratch_shapes=[
            pltpu.SemaphoreType.DMA((9, 6)),
            pltpu.SemaphoreType.DMA((9, 6)),
            pltpu.SemaphoreType.DMA((6,)),
            pltpu.SemaphoreType.DMA((3,)),
            pltpu.SemaphoreType.DMA((1,)),
            pltpu.SemaphoreType.DMA((30,)),
            pltpu.SemaphoreType.DMA((30,)),
        ],
        compiler_params=pltpu.CompilerParams(collective_id=1, has_side_effects=True),
        name="spread",
    )(x, cot, small, q, f, o)


def rms(value):
    return lax.rsqrt(jnp.mean(value * value, axis=-1, keepdims=True) + 1e-06)


def rms_back(grad, value, scale, gain):
    weighted = grad * gain
    inner = jnp.mean(weighted * value, axis=-1, keepdims=True)
    return (
        scale * weighted - value * (scale * scale * scale) * inner,
        jnp.sum(grad * value * scale, axis=0, keepdims=True),
    )


def seq_reduce(part, own, near, from_left, from_right, send, recv, seq):
    own[...] = part[...]
    ring = RingReduce(
        seq,
        along_x(seq, 1),
        along_x(seq, 3),
        lambda index, half: own.at[index, pl.ds(32 * half, 32)],
        lambda half: near.at[half],
        lambda half: from_left.at[pl.ds(32 * half, 32)],
        lambda half: from_right.at[pl.ds(32 * half, 32)],
        send,
        recv,
    )
    ring.start()
    ring.middle()
    ring.arrive()
    total = (
        own[seq].astype(F32) + from_left[...].astype(F32) + from_right[...].astype(F32)
    )
    return ring, total


def seq_gather(out, send, recv, seq):
    ring = RingGather(
        seq,
        along_x(seq, 1),
        along_x(seq, 3),
        lambda half: out.at[seq, pl.ds(32 * half, 32)],
        lambda index, half: out.at[index, pl.ds(32 * half, 32)],
        send,
        recv,
    )
    ring.start()
    ring.middle()
    ring.near()
    ring.far()
    ring.finish()


def attended_kernel(part, rows, small, residual_out, gathered, *scratch, layer):
    *bufs, send, recv = scratch
    seq = lax.axis_index("seq")
    greet([along_x(seq, 1), along_x(seq, 3)])
    ring, total = seq_reduce(part, *bufs, send.at[0], recv.at[0], seq)
    residual = rows[seq].astype(F32) + total
    residual_out[...] = residual
    gathered[seq] = (residual * rms(residual) * small[layer, 1:2, :]).astype(BF16)
    seq_gather(gathered, send.at[1], recv.at[1], seq)
    ring.finish()


def output_kernel(part, residual, gathered, *scratch):
    *bufs, send, recv = scratch
    seq = lax.axis_index("seq")
    greet([along_x(seq, 1), along_x(seq, 3)])
    ring, total = seq_reduce(part, *bufs, send.at[0], recv.at[0], seq)
    gathered[seq] = (residual[...] + total).astype(BF16)
    seq_gather(gathered, send.at[1], recv.at[1], seq)
    ring.finish()


def last_output_kernel(part, residual, out, *scratch):
    *bufs, send, recv = scratch
    seq = lax.axis_index("seq")
    greet([along_x(seq, 1), along_x(seq, 3)])
    ring, total = seq_reduce(part, *bufs, send.at[0], recv.at[0], seq)
    out[...] = (residual[...] + total).astype(BF16)
    ring.finish()


def back_ffn_kernel(part, outer, residual, small, grad_out, gathered, gain_out, *scratch, layer):
    *bufs, send, recv = scratch
    seq = lax.axis_index("seq")
    greet([along_x(seq, 1), along_x(seq, 3)])
    ring, total = seq_reduce(part, *bufs, send.at[0], recv.at[0], seq)
    value = residual[...]
    grad, gain = rms_back(total, value, rms(value), small[layer, 1:2, :])
    grad = outer[seq].astype(F32) + grad
    grad_out[...] = grad
    gathered[seq] = grad.astype(BF16)
    gain_out[...] = gain
    seq_gather(gathered, send.at[1], recv.at[1], seq)
    ring.finish()


def back_in_kernel(part, grad_ref, rows, small, gathered, gain_out, *scratch, layer, last):
    *bufs, send, recv = scratch
    seq = lax.axis_index("seq")
    greet([along_x(seq, 1), along_x(seq, 3)])
    ring, total = seq_reduce(part, *bufs, send.at[0], recv.at[0], seq)
    value = rows[seq].astype(F32)
    grad, gain = rms_back(total, value, rms(value), small[layer, 0:1, :])
    grad = (grad_ref[...] + grad).astype(BF16)
    gain_out[...] = gain
    if last:
        gathered[...] = grad
    else:
        gathered[seq] = grad
        seq_gather(gathered, send.at[1], recv.at[1], seq)
    ring.finish()


def seq_call(kernel, out_shape, collective_id, name, *operands):
    return pl.pallas_call(
        kernel,
        out_shape=out_shape,
        in_specs=[VMEM] * len(operands),
        out_specs=[VMEM] * len(out_shape),
        scratch_shapes=[
            pltpu.VMEM((4, ROWS, D), BF16),
            pltpu.VMEM((2, 32, D), BF16),
            pltpu.VMEM((ROWS, D), BF16),
            pltpu.VMEM((ROWS, D), BF16),
            pltpu.SemaphoreType.DMA((2, 6)),
            pltpu.SemaphoreType.DMA((2, 6)),
        ],
        compiler_params=pltpu.CompilerParams(
            collective_id=collective_id, has_side_effects=True, vmem_limit_bytes=VMEM_BYTES
        ),
        name=name,
    )(*operands)


def shifted(value, step):
    rows = value.shape[0]
    filler = jnp.zeros((abs(step), value.shape[1]), value.dtype)
    if step > 0:
        return jnp.concatenate([filler, value[: rows - step]], axis=0)
    return jnp.concatenate([value[-step:], filler], axis=0)


def doc_places(doc_len):
    col = lax.broadcasted_iota(jnp.int32, (PACK, 1), 0)
    row = lax.broadcasted_iota(jnp.int32, (1, PACK), 1)
    start_col, start_row = jnp.zeros_like(col), jnp.zeros_like(row)
    end = 0
    for doc in range(4):
        end = end + doc_len[doc]
        start_col = jnp.where(col >= end, end, start_col)
        start_row = jnp.where(row >= end, end, start_row)
    return col - start_col, start_col == start_row


def one_hot(column, row):
    return (column == row).astype(F32).astype(BF16)


def sigmoid(value):
    return 1.0 / (1.0 + jnp.exp(-value))


def conv_taps(small_ref, layer, tap, part):
    return small_ref[layer, 4 + tap * 3 + part : 5 + tap * 3 + part, 0:256]


def conv_part(series, small_ref, layer, part, offset):
    total = series * conv_taps(small_ref, layer, 0, part)
    for tap in range(1, 4):
        moved = jnp.where(offset >= tap, shifted(series, tap), 0.0)
        total = total + moved * conv_taps(small_ref, layer, tap, part)
    return total


def inverse(system):
    col = lax.broadcasted_iota(jnp.int32, (PACK, PACK), 0)
    row = lax.broadcasted_iota(jnp.int32, (PACK, PACK), 1)
    apart = col ^ row
    result = jnp.where(col == row, 1.0, 0.0) - jnp.where(apart == 1, system, 0.0)
    high, low = halves(system)
    for level in range(1, 8):
        mask = (apart >> level) == 1
        corner = halves(jnp.where(mask, system, 0.0))
        now = halves(result)
        inner = halves(dot3(corner, now, NN))
        result = result - dot3(now, inner, NN)
    return result


def unit(value):
    scale = lax.rsqrt(jnp.sum(value * value, axis=-1, keepdims=True) + 1e-06)
    return value * scale, scale


def mixer_kernel(
    rows, w_q, w_o, small, perm_row, perm_col, doc_len, part, proj_out, inv_out, u_out, o_out, att_out, n_out, *, layer
):
    x = rows[...].astype(F32)
    normed = (x * rms(x) * small[layer, 0:1, :]).astype(BF16)
    n_out[...] = normed
    proj = dot(normed, w_q[...], NN).astype(BF16)
    place_col = lax.broadcasted_iota(jnp.int32, (PACK, 1), 0)
    place_row = lax.broadcasted_iota(jnp.int32, (1, PACK), 1)
    proj = dot(one_hot(place_col, perm_row[...]), proj, NN)
    proj_out[...] = proj.astype(BF16)
    offset, same = doc_places(doc_len)
    activated = []
    for kind in range(3):
        pre = conv_part(proj[:, 256 * kind : 256 * kind + 256], small, layer, kind, offset)
        activated.append(pre * sigmoid(pre))
    col = lax.broadcasted_iota(jnp.int32, (PACK, PACK), 0)
    row = lax.broadcasted_iota(jnp.int32, (PACK, PACK), 1)
    strict = same & (col > row)
    tri = same & (col >= row)
    heads = []
    for head in range(2):
        lanes = slice(128 * head, 128 * head + 128)
        query = halves(unit(activated[0][:, lanes])[0] * HD**-0.5)
        key = halves(unit(activated[1][:, lanes])[0])
        value = activated[2][:, lanes]
        strength = sigmoid(proj[:, 768 + head : 769 + head])
        system = jnp.where(strict, strength * dot3(key, key, NT), 0.0)
        solved = inverse(system)
        inv_out[head] = solved
        fresh = dot3(halves(solved), halves(strength * value), NN)
        u_out[head] = fresh
        scores = jnp.where(tri, dot3(query, key, NT), 0.0)
        produced = dot3(halves(scores), halves(fresh), NN)
        o_out[head] = produced
        scale = lax.rsqrt(jnp.mean(produced * produced, axis=-1, keepdims=True) + 1e-05)
        heads.append((produced * scale * small[layer, 2:3, 0:128]).astype(BF16))
    mixed = jnp.concatenate(heads, axis=1)
    attended = dot(one_hot(perm_col[...], place_row), mixed, NN).astype(BF16)
    att_out[...] = attended
    part[...] = dot(attended, w_o[...], NN).astype(BF16)


def mixer(rows, w_q, w_o, small, perm_row, perm_col, doc_len, layer):
    return pl.pallas_call(
        functools.partial(mixer_kernel, layer=layer),
        out_shape=[
            sds((PACK, D), BF16),
            sds((PACK, QW), BF16),
            sds((2, PACK, PACK), F32),
            sds((2, PACK, HD), F32),
            sds((2, PACK, HD), F32),
            sds((PACK, 256), BF16),
            sds((PACK, D), BF16),
        ],
        in_specs=[VMEM] * 6 + [SMEM],
        out_specs=[VMEM] * 7,
        compiler_params=pltpu.CompilerParams(vmem_limit_bytes=VMEM_BYTES),
        name="mixer",
    )(rows, w_q, w_o, small, perm_row, perm_col, doc_len)


def mixer_back_kernel(
    grad,
    w_q,
    w_o,
    small,
    perm_row,
    perm_col,
    doc_len,
    proj_ref,
    inv_ref,
    u_ref,
    o_ref,
    att,
    normed,
    part,
    dw_q,
    dw_o,
    dsmall,
    *,
    layer,
):
    grad_att = dot(grad[...], w_o[...], NT).astype(BF16)
    dw_o[...] = dot(att[...], grad[...], TN).astype(BF16)
    place_col = lax.broadcasted_iota(jnp.int32, (PACK, 1), 0)
    place_row = lax.broadcasted_iota(jnp.int32, (1, PACK), 1)
    grad_att = dot(one_hot(place_col, perm_row[...]), grad_att, NN)
    proj = proj_ref[...].astype(F32)
    offset, same = doc_places(doc_len)
    pres, gates = [], []
    for kind in range(3):
        pre = conv_part(proj[:, 256 * kind : 256 * kind + 256], small, layer, kind, offset)
        pres.append(pre)
        gates.append(sigmoid(pre))
    col = lax.broadcasted_iota(jnp.int32, (PACK, PACK), 0)
    row = lax.broadcasted_iota(jnp.int32, (PACK, PACK), 1)
    strict = same & (col > row)
    tri = same & (col >= row)
    gain = small[layer, 2:3, 0:128]
    gain_grad = jnp.zeros((1, HD), F32)
    grads = [[], [], []]
    logit_grads = []
    for head in range(2):
        lanes = slice(128 * head, 128 * head + 128)
        act_q, act_k, value = [(pre * gate)[:, lanes] for pre, gate in zip(pres, gates)]
        query_f, scale_q = unit(act_q)
        key_f, scale_k = unit(act_k)
        query, key = halves(query_f * HD**-0.5), halves(key_f)
        strength = sigmoid(proj[:, 768 + head : 769 + head])
        produced = o_ref[head]
        scale = lax.rsqrt(jnp.mean(produced * produced, axis=-1, keepdims=True) + 1e-05)
        given = grad_att[:, lanes]
        weighted = given * gain
        inner = jnp.mean(weighted * produced, axis=-1, keepdims=True)
        grad_o = halves(scale * weighted - produced * (scale * scale * scale) * inner)
        gain_grad = gain_grad + jnp.sum(given * produced * scale, axis=0, keepdims=True)
        fresh = halves(u_ref[head])
        gram = dot3(key, key, NT)
        scores = halves(jnp.where(tri, dot3(query, key, NT), 0.0))
        grad_scores = halves(jnp.where(tri, dot3(grad_o, fresh, NT), 0.0))
        grad_fresh = halves(dot3(scores, grad_o, TN))
        grad_source = dot3(halves(inv_ref[head]), grad_fresh, TN)
        grad_system = jnp.where(strict, -dot3(halves(grad_source), fresh, NT), 0.0)
        grad_gram = halves(strength * grad_system)
        grad_query = dot3(grad_scores, key, NN)
        grad_key = (
            dot3(grad_scores, query, TN) + dot3(grad_gram, key, NN) + dot3(grad_gram, key, TN)
        )
        grad_value = strength * grad_source
        grad_strength = jnp.sum(grad_source * value, axis=-1, keepdims=True) + jnp.sum(
            grad_system * gram, axis=-1, keepdims=True
        )
        logit_grads.append(grad_strength * strength * (1.0 - strength))
        grads[0].append(
            HD**-0.5
            * (
                scale_q * grad_query
                - act_q
                * (scale_q * scale_q * scale_q)
                * jnp.sum(act_q * grad_query, axis=-1, keepdims=True)
            )
        )
        grads[1].append(
            scale_k * grad_key
            - act_k
            * (scale_k * scale_k * scale_k)
            * jnp.sum(act_k * grad_key, axis=-1, keepdims=True)
        )
        grads[2].append(grad_value)
    dsmall[...] = jnp.zeros_like(dsmall)
    dsmall[2:3, 0:128] = gain_grad
    pieces = []
    for kind in range(3):
        pre, gate = pres[kind], gates[kind]
        grad_pre = jnp.concatenate(grads[kind], axis=1) * gate * (1.0 + pre * (1.0 - gate))
        series = proj[:, 256 * kind : 256 * kind + 256]
        total = grad_pre * conv_taps(small, layer, 0, kind)
        dsmall[4 + kind : 5 + kind, 0:256] = jnp.sum(grad_pre * series, axis=0, keepdims=True)
        for tap in range(1, 4):
            kept = jnp.where(offset >= tap, grad_pre, 0.0)
            total = total + shifted(kept, -tap) * conv_taps(small, layer, tap, kind)
            dsmall[4 + tap * 3 + kind : 5 + tap * 3 + kind, 0:256] = jnp.sum(
                kept * shifted(series, tap), axis=0, keepdims=True
            )
        pieces.append(total.astype(BF16))
    lane = lax.broadcasted_iota(jnp.int32, (1, 128), 1)
    pieces.append(
        jnp.where(lane == 0, logit_grads[0], jnp.where(lane == 1, logit_grads[1], 0.0)).astype(BF16)
    )
    grad_proj = jnp.concatenate(pieces, axis=1)
    grad_proj = dot(one_hot(perm_col[...], place_row), grad_proj, NN).astype(BF16)
    part[...] = dot(grad_proj, w_q[...], NT).astype(BF16)
    dw_q[...] = dot(normed[...], grad_proj, TN).astype(BF16)


def mixer_back(grad, w_q, w_o, small, perm_row, perm_col, doc_len, saved, layer):
    return pl.pallas_call(
        functools.partial(mixer_back_kernel, layer=layer),
        out_shape=[
            sds((PACK, D), BF16),
            sds((D, QW), BF16),
            sds((256, D), BF16),
            sds((16, D), F32),
        ],
        in_specs=[VMEM] * 6 + [SMEM] + [VMEM] * 6,
        out_specs=[VMEM] * 4,
        compiler_params=pltpu.CompilerParams(vmem_limit_bytes=VMEM_BYTES),
        name="mixer_back",
    )(grad, w_q, w_o, small, perm_row, perm_col, doc_len, *saved)


def ffn_kernel(normed, weights, part, gate_out, up_out, total):
    step = pl.program_id(0)
    gate = dot(normed[...], weights[0], NT)
    up = dot(normed[...], weights[1], NT)
    gate_out[...] = gate
    up_out[...] = up
    hidden = (gate * sigmoid(gate) * up).astype(BF16)
    term = dot(hidden, weights[2], NN)

    @pl.when(step == 0)
    def _():
        total[...] = term

    @pl.when(step > 0)
    def _():
        total[...] += term

    @pl.when(step == 2)
    def _():
        part[...] = total[...].astype(BF16)


def ffn(normed, weights):
    return pl.pallas_call(
        ffn_kernel,
        grid=(3,),
        out_shape=[sds((PACK, D), BF16), sds((PACK, 768), F32), sds((PACK, 768), F32)],
        in_specs=[
            pl.BlockSpec((PACK, D), lambda i: (0, 0)),
            pl.BlockSpec((3, 256, D), lambda i: (0, i, 0)),
        ],
        out_specs=[
            pl.BlockSpec((PACK, D), lambda i: (0, 0)),
            pl.BlockSpec((PACK, 256), lambda i: (0, i)),
            pl.BlockSpec((PACK, 256), lambda i: (0, i)),
        ],
        scratch_shapes=[pltpu.VMEM((PACK, D), F32)],
        compiler_params=pltpu.CompilerParams(vmem_limit_bytes=VMEM_BYTES),
        name="ffn",
    )(normed, weights)


def ffn_back_kernel(grad, normed, weights, gate_ref, up_ref, part, dweights, total):
    step = pl.program_id(0)
    gate, up = gate_ref[...], up_ref[...]
    sig = sigmoid(gate)
    grad_hidden = dot(grad[...], weights[2], NT)
    grad_gate = (grad_hidden * up * sig * (1.0 + gate * (1.0 - sig))).astype(BF16)
    grad_up = (grad_hidden * gate * sig).astype(BF16)
    hidden = (gate * sig * up).astype(BF16)
    term = dot(grad_gate, weights[0], NN) + dot(grad_up, weights[1], NN)

    @pl.when(step == 0)
    def _():
        total[...] = term

    @pl.when(step > 0)
    def _():
        total[...] += term

    @pl.when(step == 2)
    def _():
        part[...] = total[...].astype(BF16)

    dweights[0] = dot(grad_gate, normed[...], TN).astype(BF16)
    dweights[1] = dot(grad_up, normed[...], TN).astype(BF16)
    dweights[2] = dot(hidden, grad[...], TN).astype(BF16)


def ffn_back(grad, normed, weights, gate, up):
    return pl.pallas_call(
        ffn_back_kernel,
        grid=(3,),
        out_shape=[sds((PACK, D), BF16), sds((3, 768, D), BF16)],
        in_specs=[
            pl.BlockSpec((PACK, D), lambda i: (0, 0)),
            pl.BlockSpec((PACK, D), lambda i: (0, 0)),
            pl.BlockSpec((3, 256, D), lambda i: (0, i, 0)),
            pl.BlockSpec((PACK, 256), lambda i: (0, i)),
            pl.BlockSpec((PACK, 256), lambda i: (0, i)),
        ],
        out_specs=[
            pl.BlockSpec((PACK, D), lambda i: (0, 0)),
            pl.BlockSpec((3, 256, D), lambda i: (0, i, 0)),
        ],
        scratch_shapes=[pltpu.VMEM((PACK, D), F32)],
        compiler_params=pltpu.CompilerParams(vmem_limit_bytes=VMEM_BYTES),
        name="ffn_back",
    )(grad, normed, weights, gate, up)


def collect_kernel(
    rows_ref,
    small_ref,
    q0_ref,
    q1_ref,
    f0_ref,
    f1_ref,
    o0_ref,
    o1_ref,
    rows_out,
    small_out,
    q_out,
    f_out,
    o_out,
    q_sum,
    f_sum,
    o_sum,
    q_in,
    f_in,
    o_in,
    g_near,
    g_left,
    g_right,
    d_near,
    d_left,
    d_right,
    q_near,
    q_left,
    q_right,
    o_near,
    o_left,
    o_right,
    o_far,
    small_sum,
    small_in,
    send,
    recv,
    pair_send,
    pair_recv,
    local,
    small_send,
    small_recv,
    o_send,
    o_recv,
):
    core, seq, z, y = place()
    partner = {"section": 1 - core}
    greet(
        [along_x(seq, k) for k in (1, 2, 3)]
        + [along_y(z, y, k) for k in (1, 2, 3)]
        + [along_z(z, y, k) for k in (1, 2, 3)]
        + [partner]
    )

    kept = []

    def pair(index, source, target):
        return remote(source, target, pair_send.at[index], pair_recv.at[index], partner)

    pair_small = pair(0, small_ref.at[1 - core], small_in.at[0])
    pair_small.start()
    layers = [
        (1, q0_ref, q1_ref, q_in, q_sum),
        (2, f0_ref, f1_ref, f_in, f_sum),
        (3, o0_ref, o1_ref, o_in, o_sum),
    ]
    keep = [pltpu.make_async_copy(rows_ref, rows_out.at[:, core], local.at[0])]
    pair_rows = pair(4, rows_ref, rows_out.at[:, core])
    for mine in (0, 1):

        @pl.when(core == mine)
        def _():
            for index, first, second, landing, total in layers:
                pair(index, (second, first)[mine], landing).start()
                pltpu.make_async_copy((first, second)[mine], total, local.at[index]).start()

    pair_rows.start()
    for copy in keep:
        copy.start()
    for index, first, second, landing, total in layers:
        pltpu.make_async_copy(first, total, local.at[index]).wait()
        pair(index, first, landing).wait()
        add_into(total, [landing])

    def half_rows(half):
        return pl.ds(32 * half, 32)

    def half_units(half):
        return pl.ds(32 * half, 32 - 16 * half)

    def half_planes(half):
        return pl.ds(2 * half, 2)

    def y_ring(sem, *refs):
        return RingReduce(
            y, along_y(z, y, 1), along_y(z, y, 3), *refs, send.at[sem], recv.at[sem]
        )

    def z_ring(sem, *refs):
        return RingReduce(
            z, along_z(z, y, 1), along_z(z, y, 3), *refs, send.at[sem], recv.at[sem]
        )

    g_one = z_ring(
        0,
        lambda index, half: f_sum.at[half, index],
        lambda half: g_near.at[half, pl.ds(0, 4)],
        lambda half: g_left.at[half, pl.ds(0, 4)],
        lambda half: g_right.at[half, pl.ds(0, 4)],
    )
    d_one = y_ring(
        1,
        lambda index, half: f_sum.at[2, half_planes(half), index],
        lambda half: d_near.at[half_planes(half)],
        lambda half: d_left.at[half_planes(half)],
        lambda half: d_right.at[half_planes(half)],
    )
    q_one = y_ring(
        2,
        lambda index, half: q_sum.at[half_planes(half), index],
        lambda half: q_near.at[half_planes(half)],
        lambda half: q_left.at[half_planes(half)],
        lambda half: q_right.at[half_planes(half)],
    )
    o_one = y_ring(
        3,
        lambda index, half: o_sum.at[index, half_rows(half)],
        lambda half: o_near.at[half_rows(half)],
        lambda half: o_left.at[half_rows(half)],
        lambda half: o_right.at[half_rows(half)],
    )
    g_two = y_ring(
        4,
        lambda index, half: f_sum.at[half, z, index],
        lambda half: g_near.at[half, 4],
        lambda half: g_left.at[half, 4],
        lambda half: g_right.at[half, 4],
    )
    d_two = z_ring(
        5,
        lambda index, half: f_sum.at[2, index, y, half_units(half)],
        lambda half: d_near.at[4, half_units(half)],
        lambda half: d_left.at[4, half_units(half)],
        lambda half: d_right.at[4, half_units(half)],
    )
    q_two = z_ring(
        6,
        lambda index, half: q_sum.at[index, y, half_rows(half)],
        lambda half: q_near.at[4, half_rows(half)],
        lambda half: q_left.at[4, half_rows(half)],
        lambda half: q_right.at[4, half_rows(half)],
    )
    first = [q_one, g_one, d_one, o_one]
    for ring in first:
        ring.start()

    pair_small.wait()
    small_sum[0] = small_ref[core] + small_in[0]
    stage = 0
    small_copies = []
    for axis in (along_y, along_z):
        copies = [
            remote(
                small_sum.at[stage],
                small_in.at[1 + 3 * stage + k],
                small_send.at[3 * stage + k],
                small_recv.at[3 * stage + k],
                axis(z, y, k + 1),
            )
            for k in range(3)
        ]
        for copy in copies:
            copy.start()
        small_copies += copies
        if stage == 0:
            for ring in first:
                ring.middle()
        for copy in copies:
            copy.wait_recv()
        small_sum[stage + 1] = (
            small_sum[stage]
            + small_in[1 + 3 * stage]
            + small_in[2 + 3 * stage]
            + small_in[3 + 3 * stage]
        )
        stage += 1
    small_out[seq] = small_sum[2]
    copies = [
        remote(
            small_sum.at[2],
            small_out.at[seq],
            small_send.at[6 + k],
            small_recv.at[6 + k],
            along_x(seq, k + 1),
        )
        for k in range(3)
    ]
    for copy in copies:
        copy.start()
    small_copies += copies

    for ring, follower in ((q_one, q_two), (g_one, g_two), (d_one, d_two), (o_one, None)):
        ring.arrive()
        ring.total()
        if follower is not None:
            follower.start()

    o_total = o_sum.at[y]
    o_copies = [
        remote(o_total, o_far.at[k], o_send.at[k], o_recv.at[k], along_z(z, y, 3 - k))
        for k in range(3)
    ]
    for k in range(3):

        @pl.when(lax.rem(z + 3 - k, 4) == seq)
        def _():
            o_copies[k].start()

    second = [q_two, g_two, d_two]
    for ring in second:
        ring.middle()
    for ring in second:
        ring.arrive()
        ring.total()

    def x_gather(sem, source, slot):
        return RingGather(
            seq, along_x(seq, 1), along_x(seq, 3), source, slot, send.at[sem], recv.at[sem]
        )

    third = [
        x_gather(
            7,
            lambda half: q_sum.at[z, y, half_rows(half)],
            lambda index, half: q_out.at[index, half_rows(half)],
        ),
        x_gather(
            8,
            lambda half: f_sum.at[half, z, y],
            lambda index, half: f_out.at[index, half],
        ),
        x_gather(
            9,
            lambda half: f_sum.at[2, z, y, half_units(half)],
            lambda index, half: f_out.at[index, 2, half_units(half)],
        ),
    ]
    for ring in third:
        ring.start()
    q_out[seq] = q_sum[z, y]
    f_out[seq] = f_sum[:, z, y]

    x_copies = [
        remote(o_out, o_out, o_send.at[3 + k], o_recv.at[3], along_x(seq, k + 1)) for k in range(3)
    ]

    @pl.when(z == seq)
    def _():
        for k in range(3):
            o_copies[k].wait_recv()
        o_out[...] = (
            o_sum[y].astype(F32)
            + o_far[0].astype(F32)
            + o_far[1].astype(F32)
            + o_far[2].astype(F32)
        ).astype(BF16)
        for copy in x_copies:
            copy.start()

    for ring in third:
        ring.middle()

    @pl.when(z == seq)
    def _():
        for copy in x_copies:
            copy.wait_send()

    @pl.when(z != seq)
    def _():
        x_copies[0].wait_recv()

    for k in range(3):

        @pl.when(lax.rem(z + 3 - k, 4) == seq)
        def _():
            o_copies[k].wait_send()

    for ring in third:
        ring.near()
        ring.far()
    for ring in first + second + third:
        ring.finish()
    for copy in copies:
        copy.wait_recv()
    for copy in small_copies:
        copy.wait_send()
    pair_rows.wait()
    for copy in keep:
        copy.wait()


def collect(rows, small, q, f, o):
    operands = (rows, small, *q, *f, *o)
    return pl.pallas_call(
        collect_kernel,
        out_shape=[
            sds((2, 2, ROWS, D), BF16),
            sds((4, 16, D), F32),
            sds((4, 64, QW), BF16),
            sds((4, 3, UNIT, D), BF16),
            sds((64, D), BF16),
        ],
        in_specs=[VMEM] * len(operands),
        out_specs=[VMEM] * 5,
        scratch_shapes=[
            pltpu.VMEM((4, 4, 64, QW), BF16),
            pltpu.VMEM((3, 4, 4, UNIT, D), BF16),
            pltpu.VMEM((4, 64, D), BF16),
            pltpu.VMEM((4, 4, 64, QW), BF16),
            pltpu.VMEM((3, 4, 4, UNIT, D), BF16),
            pltpu.VMEM((4, 64, D), BF16),
            pltpu.VMEM((2, 5, UNIT, D), BF16),
            pltpu.VMEM((2, 5, UNIT, D), BF16),
            pltpu.VMEM((2, 5, UNIT, D), BF16),
            pltpu.VMEM((5, UNIT, D), BF16),
            pltpu.VMEM((5, UNIT, D), BF16),
            pltpu.VMEM((5, UNIT, D), BF16),
            pltpu.VMEM((5, 64, QW), BF16),
            pltpu.VMEM((5, 64, QW), BF16),
            pltpu.VMEM((5, 64, QW), BF16),
            pltpu.VMEM((64, D), BF16),
            pltpu.VMEM((64, D), BF16),
            pltpu.VMEM((64, D), BF16),
            pltpu.VMEM((3, 64, D), BF16),
            pltpu.VMEM((3, 16, D), F32),
            pltpu.VMEM((7, 16, D), F32),
            pltpu.SemaphoreType.DMA((10, 6)),
            pltpu.SemaphoreType.DMA((10, 6)),
            pltpu.SemaphoreType.DMA((5,)),
            pltpu.SemaphoreType.DMA((5,)),
            pltpu.SemaphoreType.DMA((4,)),
            pltpu.SemaphoreType.DMA((9,)),
            pltpu.SemaphoreType.DMA((9,)),
            pltpu.SemaphoreType.DMA((6,)),
            pltpu.SemaphoreType.DMA((4,)),
        ],
        compiler_params=pltpu.CompilerParams(
            collective_id=2, has_side_effects=True, vmem_limit_bytes=VMEM_BYTES
        ),
        name="collect",
    )(*operands)


def local(
    block_in,
    cotangent,
    perm_rows,
    doc_lengths,
    norm_in,
    w_qkv,
    w_beta,
    conv_w,
    norm_head,
    w_out,
    norm_ffn,
    w_ffn,
    w_down,
):
    core, seq = lax.axis_index("section"), lax.axis_index("seq")

    def mine(array):
        return lax.dynamic_index_in_dim(array, core, 0, keepdims=False)[0]

    x, cot = mine(block_in), mine(cotangent)
    perm, doc_len = mine(perm_rows), mine(doc_lengths)
    perm_row, perm_col = perm[None, :], perm[:, None]
    heads = lax.dynamic_slice_in_dim(conv_w[0], seq * 256, 256, 2).reshape(12, 256)
    small = jnp.concatenate(
        [
            norm_in,
            norm_ffn,
            jnp.pad(norm_head, ((0, 1), (0, D - HD))),
            jnp.pad(heads, ((0, 0), (0, D - 256))),
        ],
        axis=0,
    )
    q = jnp.concatenate(
        [
            lax.dynamic_slice_in_dim(w_qkv[0].reshape(64, 3, D), seq * 256, 256, 2).reshape(64, 768),
            jnp.pad(lax.dynamic_slice_in_dim(w_beta[0], seq * 2, 2, 1), ((0, 0), (0, 126))),
        ],
        axis=1,
    )
    units = jnp.concatenate([jnp.swapaxes(w_ffn[0], 1, 2), w_down], axis=0)
    units = jnp.pad(units, ((0, 0), (0, 16), (0, 0)))
    units = lax.dynamic_slice_in_dim(units, seq * UNIT, UNIT, 1)
    x_all, cot_all, small_all, q_all, f_all, o_all = spread(x, cot, small, q, units, w_out[0])
    q_all = q_all.reshape(2, D, QW)
    f_all = f_all.reshape(2, 3, 768, D)
    o_all = o_all.reshape(2, 256, D)

    rows_in, residuals, normed_ffn, gates, ups, saved = [x_all], [], [], [], [], []
    block_row = None
    for layer in (0, 1):
        part, *kept = mixer(
            rows_in[layer].reshape(PACK, D),
            q_all[layer],
            o_all[layer],
            small_all,
            perm_row,
            perm_col,
            doc_len,
            layer,
        )
        saved.append(kept)
        residual, gathered = seq_call(
            functools.partial(attended_kernel, layer=layer),
            [sds((ROWS, D), F32), sds((4, ROWS, D), BF16)],
            3 + layer,
            "attended",
            part.reshape(4, ROWS, D),
            rows_in[layer],
            small_all,
        )
        residuals.append(residual)
        normed_ffn.append(gathered.reshape(PACK, D))
        part, gate, up = ffn(normed_ffn[layer], f_all[layer])
        gates.append(gate)
        ups.append(up)
        if layer == 0:
            (gathered,) = seq_call(
                output_kernel,
                [sds((4, ROWS, D), BF16)],
                5,
                "output",
                part.reshape(4, ROWS, D),
                residual,
            )
            rows_in.append(gathered)
        else:
            (block_row,) = seq_call(
                last_output_kernel,
                [sds((ROWS, D), BF16)],
                6,
                "last_output",
                part.reshape(4, ROWS, D),
                residual,
            )

    outer = cot_all
    dq, df, do, dsmall = [None] * 2, [None] * 2, [None] * 2, [None] * 2
    for layer in (1, 0):
        part, df[layer] = ffn_back(
            outer.reshape(PACK, D), normed_ffn[layer], f_all[layer], gates[layer], ups[layer]
        )
        grad, gathered, gain_ffn = seq_call(
            functools.partial(back_ffn_kernel, layer=layer),
            [sds((ROWS, D), F32), sds((4, ROWS, D), BF16), sds((1, D), F32)],
            7 + layer,
            "back_ffn",
            part.reshape(4, ROWS, D),
            outer,
            residuals[layer],
            small_all,
        )
        part, dq[layer], do[layer], grad_small = mixer_back(
            gathered.reshape(PACK, D),
            q_all[layer],
            o_all[layer],
            small_all,
            perm_row,
            perm_col,
            doc_len,
            saved[layer],
            layer,
        )
        outer, gain_in = seq_call(
            functools.partial(back_in_kernel, layer=layer, last=layer == 0),
            [sds((4, ROWS, D) if layer else (ROWS, D), BF16), sds((1, D), F32)],
            9 + layer,
            "back_in",
            part.reshape(4, ROWS, D),
            grad,
            rows_in[layer],
            small_all,
        )
        dsmall[layer] = jnp.concatenate([gain_in, gain_ffn, grad_small[2:]], axis=0)

    rows, small_sum, q_sum, f_sum, o_sum = collect(
        jnp.stack([block_row, outer]),
        jnp.stack(dsmall),
        [d.reshape(4, 4, 64, QW) for d in dq],
        [d.reshape(3, 4, 4, UNIT, D) for d in df],
        [d.reshape(4, 64, D) for d in do],
    )
    total = jnp.sum(small_sum, axis=0)
    grad_conv = jnp.transpose(small_sum[:, 4:, :256].reshape(4, 4, 3, 256), (1, 2, 0, 3))
    grad_qkv = jnp.transpose(q_sum[:, :, :768].reshape(4, 64, 3, 256), (1, 2, 0, 3))
    grad_beta = jnp.transpose(q_sum[:, :, 768:770], (1, 0, 2))
    grad_units = jnp.swapaxes(f_sum, 0, 1).reshape(3, 192, D)[:, :176].astype(F32)
    return (
        rows[0][:, None],
        rows[1][:, None],
        total[0:1],
        grad_qkv.reshape(1, 64, 3 * D).astype(F32),
        grad_beta.reshape(1, 64, H).astype(F32),
        grad_conv.reshape(1, 4, 3, D),
        total[2:3, :HD],
        o_sum[None].astype(F32),
        total[1:2],
        jnp.swapaxes(grad_units[:2], 1, 2)[None],
        grad_units[2][None],
    )


def solution(mesh):
    placed = (
        P(None, "fsdp", "seq", None),
        P(None, "fsdp", "seq", None),
        P(None, "fsdp", None),
        P(None, "fsdp", None),
        P("section", None),
        P("section", "fsdp", None),
        P("section", "fsdp", None),
        P("section", None, None, None),
        P("section", None),
        P("section", "fsdp", None),
        P("section", None),
        P("section", None, None, "fsdp"),
        P("section", "fsdp", None),
    )
    return jax.shard_map(
        local,
        mesh=mesh,
        in_specs=placed,
        out_specs=(
            P(None, "fsdp", "seq", None),
            P(None, "fsdp", "seq", None),
            P("section", None),
            P("section", "fsdp", None),
            P("section", "fsdp", None),
            P("section", None, None, None),
            P("section", None),
            P("section", "fsdp", None),
            P("section", None),
            P("section", None, None, "fsdp"),
            P("section", "fsdp", None),
        ),
        check_vma=False,
    )
```

```python
import functools

import jax
import jax.numpy as jnp
from jax import lax
from jax.experimental import pallas as pl
from jax.experimental.pallas import tpu as pltpu
from jax.sharding import PartitionSpec as P

D = 1024
H = 8
HD = 128
PACK = 256
ROWS = 64
UNIT = 48
QW = 896
MESH = pl.DeviceIdType.MESH
F32, BF16 = jnp.float32, jnp.bfloat16
VMEM = pl.BlockSpec(memory_space=pltpu.VMEM)
SMEM = pl.BlockSpec(memory_space=pltpu.SMEM)
ANY = pl.BlockSpec(memory_space=pl.ANY)
VMEM_BYTES = 60 * 1024 * 1024


def sds(shape, dtype):
    return jax.ShapeDtypeStruct(shape, dtype)


def dot(left, right, dims):
    return lax.dot_general(left, right, (dims, ((), ())), preferred_element_type=F32)


NN = ((1,), (0,))
NT = ((1,), (1,))
TN = ((0,), (0,))


def halves(value):
    high = value.astype(BF16)
    return high, (value - high.astype(F32)).astype(BF16)


def dot3(left, right, dims):
    return dot(left[0], right[0], dims) + (
        dot(left[0], right[1], dims) + dot(left[1], right[0], dims)
    )


def place():
    fsdp = lax.axis_index("fsdp")
    return (
        lax.axis_index("section"),
        lax.axis_index("seq"),
        lax.div(fsdp, 4),
        lax.rem(fsdp, 4),
    )


def along_x(seq, step):
    return {"seq": lax.rem(seq + step, 4)}


def along_y(z, y, step):
    return {"fsdp": z * 4 + lax.rem(y + step, 4)}


def along_z(z, y, step):
    return {"fsdp": lax.rem(z + step, 4) * 4 + y}


def greet(peers):
    barrier = pltpu.get_barrier_semaphore()
    for peer in peers:
        pl.semaphore_signal(barrier, inc=1, device_id=peer, device_id_type=MESH)
    pl.semaphore_wait(barrier, len(peers))


def remote(source, target, send, recv, peer):
    return pltpu.make_async_remote_copy(
        src_ref=source,
        dst_ref=target,
        send_sem=send,
        recv_sem=recv,
        device_id=peer,
        device_id_type=MESH,
    )


class Direct:
    def __init__(self, sems, peers, source, target):
        self.copies = [sems.copy(source(k), target(k), peer) for k, peer in enumerate(peers)]

    def start(self):
        for copy in self.copies:
            copy.start()

    def arrive(self):
        for copy in self.copies:
            copy.wait_recv()

    def sent(self):
        for copy in self.copies:
            copy.wait_send()


class Semaphores:
    def __init__(self, send, recv):
        self.send, self.recv, self.used = send, recv, 0

    def copy(self, source, target, peer):
        index = self.used
        self.used += 1
        return remote(source, target, self.send.at[index], self.recv.at[index], peer)


def add_into(target, others):
    shape = target.shape
    if len(shape) == 2:
        value = target[...].astype(F32)
        for other in others:
            value = value + other[...].astype(F32)
        target[...] = value.astype(target.dtype)
        return

    def body(index, carry):
        add_into(target.at[index], [other.at[index] for other in others])
        return carry

    lax.fori_loop(0, shape[0], body, 0)


def rms(value):
    return lax.rsqrt(jnp.mean(value * value, axis=-1, keepdims=True) + 1e-06)


def rms_back(grad, value, scale, gain):
    weighted = grad * gain
    inner = jnp.mean(weighted * value, axis=-1, keepdims=True)
    return (
        scale * weighted - value * (scale * scale * scale) * inner,
        jnp.sum(grad * value * scale, axis=0, keepdims=True),
    )


def shifted(value, step):
    rows = value.shape[0]
    filler = jnp.zeros((abs(step), value.shape[1]), value.dtype)
    if step > 0:
        return jnp.concatenate([filler, value[: rows - step]], axis=0)
    return jnp.concatenate([value[-step:], filler], axis=0)


def doc_places(doc_len):
    col = lax.broadcasted_iota(jnp.int32, (PACK, 1), 0)
    row = lax.broadcasted_iota(jnp.int32, (1, PACK), 1)
    start_col, start_row = jnp.zeros_like(col), jnp.zeros_like(row)
    end = 0
    for doc in range(4):
        end = end + doc_len[doc]
        start_col = jnp.where(col >= end, end, start_col)
        start_row = jnp.where(row >= end, end, start_row)
    return col - start_col, start_col == start_row


def one_hot(column, row):
    return (column == row).astype(F32).astype(BF16)


def sigmoid(value):
    return 1.0 / (1.0 + jnp.exp(-value))


def conv_taps(small_ref, layer, tap, part):
    return small_ref[layer, 4 + tap * 3 + part : 5 + tap * 3 + part, 0:256]


def conv_part(series, small_ref, layer, part, offset):
    total = series * conv_taps(small_ref, layer, 0, part)
    for tap in range(1, 4):
        moved = jnp.where(offset >= tap, shifted(series, tap), 0.0)
        total = total + moved * conv_taps(small_ref, layer, tap, part)
    return total


def inverse(system):
    col = lax.broadcasted_iota(jnp.int32, (PACK, PACK), 0)
    row = lax.broadcasted_iota(jnp.int32, (PACK, PACK), 1)
    apart = col ^ row
    result = jnp.where(col == row, 1.0, 0.0) - jnp.where(apart == 1, system, 0.0)
    high, low = halves(system)
    for level in range(1, 8):
        mask = (apart >> level) == 1
        corner = halves(jnp.where(mask, system, 0.0))
        now = halves(result)
        inner = halves(dot3(corner, now, NN))
        result = result - dot3(now, inner, NN)
    return result


def unit(value):
    scale = lax.rsqrt(jnp.sum(value * value, axis=-1, keepdims=True) + 1e-06)
    return value * scale, scale


def masks():
    col = lax.broadcasted_iota(jnp.int32, (PACK, PACK), 0)
    row = lax.broadcasted_iota(jnp.int32, (PACK, PACK), 1)
    return col, row


def to_places(perm_row):
    return one_hot(lax.broadcasted_iota(jnp.int32, (PACK, 1), 0), perm_row[...])


def to_rows(perm_col):
    return one_hot(perm_col[...], lax.broadcasted_iota(jnp.int32, (1, PACK), 1))


def mixer_forward(s, perm_row, perm_col, doc_len, layer):
    small = s.small
    x = s.rows_in[layer].reshape(PACK, D).astype(F32)
    normed = (x * rms(x) * small[layer, 0:1, :]).astype(BF16)
    s.normed[layer] = normed
    proj = dot(normed, s.wq[layer].reshape(D, QW), NN).astype(BF16)
    proj = dot(to_places(perm_row), proj, NN)
    s.proj[layer] = proj.astype(BF16)
    offset, same = doc_places(doc_len)
    activated = []
    for kind in range(3):
        pre = conv_part(proj[:, 256 * kind : 256 * kind + 256], small, layer, kind, offset)
        activated.append(pre * sigmoid(pre))
    col, row = masks()
    strict = same & (col > row)
    tri = same & (col >= row)
    heads = []
    for head in range(2):
        lanes = slice(128 * head, 128 * head + 128)
        query = halves(unit(activated[0][:, lanes])[0] * HD**-0.5)
        key = halves(unit(activated[1][:, lanes])[0])
        value = activated[2][:, lanes]
        strength = sigmoid(proj[:, 768 + head : 769 + head])
        system = jnp.where(strict, strength * dot3(key, key, NT), 0.0)
        solved = inverse(system)
        s.solved[layer, head] = solved
        fresh = dot3(halves(solved), halves(strength * value), NN)
        s.fresh[layer, head] = fresh
        scores = jnp.where(tri, dot3(query, key, NT), 0.0)
        produced = dot3(halves(scores), halves(fresh), NN)
        s.produced[layer, head] = produced
        scale = lax.rsqrt(jnp.mean(produced * produced, axis=-1, keepdims=True) + 1e-05)
        heads.append((produced * scale * small[layer, 2:3, 0:128]).astype(BF16))
    mixed = jnp.concatenate(heads, axis=1)
    s.att[layer] = dot(to_rows(perm_col), mixed, NN).astype(BF16)


def mixer_backward(s, perm_row, perm_col, doc_len, layer):
    small = s.small
    grad = s.branch[layer].reshape(PACK, D)
    grad_att = dot(grad, s.wo[layer].reshape(256, D), NT).astype(BF16)
    grad_att = dot(to_places(perm_row), grad_att, NN)
    proj = s.proj[layer].astype(F32)
    offset, same = doc_places(doc_len)
    pres, gates = [], []
    for kind in range(3):
        pre = conv_part(proj[:, 256 * kind : 256 * kind + 256], small, layer, kind, offset)
        pres.append(pre)
        gates.append(sigmoid(pre))
    col, row = masks()
    strict = same & (col > row)
    tri = same & (col >= row)
    gain = small[layer, 2:3, 0:128]
    gain_grad = jnp.zeros((1, HD), F32)
    grads = [[], [], []]
    logit_grads = []
    for head in range(2):
        lanes = slice(128 * head, 128 * head + 128)
        act_q, act_k, value = [(pre * gate)[:, lanes] for pre, gate in zip(pres, gates)]
        query_f, scale_q = unit(act_q)
        key_f, scale_k = unit(act_k)
        query, key = halves(query_f * HD**-0.5), halves(key_f)
        strength = sigmoid(proj[:, 768 + head : 769 + head])
        produced = s.produced[layer, head]
        scale = lax.rsqrt(jnp.mean(produced * produced, axis=-1, keepdims=True) + 1e-05)
        given = grad_att[:, lanes]
        weighted = given * gain
        inner = jnp.mean(weighted * produced, axis=-1, keepdims=True)
        grad_o = halves(scale * weighted - produced * (scale * scale * scale) * inner)
        gain_grad = gain_grad + jnp.sum(given * produced * scale, axis=0, keepdims=True)
        fresh = halves(s.fresh[layer, head])
        gram = dot3(key, key, NT)
        scores = halves(jnp.where(tri, dot3(query, key, NT), 0.0))
        grad_scores = halves(jnp.where(tri, dot3(grad_o, fresh, NT), 0.0))
        grad_fresh = halves(dot3(scores, grad_o, TN))
        grad_source = dot3(halves(s.solved[layer, head]), grad_fresh, TN)
        grad_system = jnp.where(strict, -dot3(halves(grad_source), fresh, NT), 0.0)
        grad_gram = halves(strength * grad_system)
        grad_query = dot3(grad_scores, key, NN)
        grad_key = (
            dot3(grad_scores, query, TN) + dot3(grad_gram, key, NN) + dot3(grad_gram, key, TN)
        )
        grad_value = strength * grad_source
        grad_strength = jnp.sum(grad_source * value, axis=-1, keepdims=True) + jnp.sum(
            grad_system * gram, axis=-1, keepdims=True
        )
        logit_grads.append(grad_strength * strength * (1.0 - strength))
        grads[0].append(
            HD**-0.5
            * (
                scale_q * grad_query
                - act_q
                * (scale_q * scale_q * scale_q)
                * jnp.sum(act_q * grad_query, axis=-1, keepdims=True)
            )
        )
        grads[1].append(
            scale_k * grad_key
            - act_k
            * (scale_k * scale_k * scale_k)
            * jnp.sum(act_k * grad_key, axis=-1, keepdims=True)
        )
        grads[2].append(grad_value)
    dsmall = s.dsmall.at[layer]
    dsmall[...] = jnp.zeros((16, D), F32)
    dsmall[2:3, 0:128] = gain_grad
    pieces = []
    for kind in range(3):
        pre, gate = pres[kind], gates[kind]
        grad_pre = jnp.concatenate(grads[kind], axis=1) * gate * (1.0 + pre * (1.0 - gate))
        series = proj[:, 256 * kind : 256 * kind + 256]
        total = grad_pre * conv_taps(small, layer, 0, kind)
        dsmall[4 + kind : 5 + kind, 0:256] = jnp.sum(grad_pre * series, axis=0, keepdims=True)
        for tap in range(1, 4):
            kept = jnp.where(offset >= tap, grad_pre, 0.0)
            total = total + shifted(kept, -tap) * conv_taps(small, layer, tap, kind)
            dsmall[4 + tap * 3 + kind : 5 + tap * 3 + kind, 0:256] = jnp.sum(
                kept * shifted(series, tap), axis=0, keepdims=True
            )
        pieces.append(total.astype(BF16))
    lane = lax.broadcasted_iota(jnp.int32, (1, 128), 1)
    pieces.append(
        jnp.where(lane == 0, logit_grads[0], jnp.where(lane == 1, logit_grads[1], 0.0)).astype(BF16)
    )
    grad_proj = jnp.concatenate(pieces, axis=1)
    s.grad_proj[...] = dot(to_rows(perm_col), grad_proj, NN).astype(BF16)


def units(weights):
    return weights.reshape(768, D)


def ffn_forward(s, layer):
    normed = s.normed_ffn[layer].reshape(PACK, D)
    gate = dot(normed, units(s.wf[layer, 0]), NT)
    up = dot(normed, units(s.wf[layer, 1]), NT)
    s.gate[layer] = gate
    s.up[layer] = up
    hidden = (gate * sigmoid(gate) * up).astype(BF16)
    return dot(hidden, units(s.wf[layer, 2]), NN)


def ffn_backward(s, layer):
    grad = s.outer[layer].reshape(PACK, D)
    gate, up = s.gate[layer], s.up[layer]
    sig = sigmoid(gate)
    grad_hidden = dot(grad, units(s.wf[layer, 2]), NT)
    grad_gate = (grad_hidden * up * sig * (1.0 + gate * (1.0 - sig))).astype(BF16)
    grad_up = (grad_hidden * gate * sig).astype(BF16)
    s.unit_grads[0] = grad_gate
    s.unit_grads[1] = grad_up
    s.unit_grads[2] = (gate * sig * up).astype(BF16)
    return dot(grad_gate, units(s.wf[layer, 0]), NN) + dot(grad_up, units(s.wf[layer, 1]), NN)


def ffn_weights(s, layer):
    normed = s.normed_ffn[layer].reshape(PACK, D)
    grad = s.outer[layer].reshape(PACK, D)
    for kind in range(3):
        right = grad if kind == 2 else normed
        s.dwf[layer, kind] = (
            dot(s.unit_grads[kind], right, TN).astype(BF16).reshape(4, 4, UNIT, D)
        )


def mixer_weights(s, layer):
    s.dwo[layer] = (
        dot(s.att[layer], s.branch[layer].reshape(PACK, D), TN).astype(BF16).reshape(4, 64, D)
    )
    s.dwq[layer] = (
        dot(s.normed[layer], s.grad_proj[...], TN).astype(BF16).reshape(4, 4, 64, QW)
    )


SCRATCH = [
    ("rows_in", (2, 4, ROWS, D), BF16),
    ("outer", (2, 4, ROWS, D), BF16),
    ("normed_ffn", (2, 4, ROWS, D), BF16),
    ("branch", (2, 4, ROWS, D), BF16),
    ("small", (2, 16, D), F32),
    ("wq", (2, 4, 4, 64, QW), BF16),
    ("wf", (2, 3, 4, 4, UNIT, D), BF16),
    ("wo", (2, 4, 64, D), BF16),
    ("dwq", (2, 4, 4, 64, QW), BF16),
    ("dwf", (2, 3, 4, 4, UNIT, D), BF16),
    ("dwo", (2, 4, 64, D), BF16),
    ("normed", (2, PACK, D), BF16),
    ("proj", (2, PACK, QW), BF16),
    ("solved", (2, 2, PACK, PACK), F32),
    ("fresh", (2, 2, PACK, HD), F32),
    ("produced", (2, 2, PACK, HD), F32),
    ("att", (2, PACK, 256), BF16),
    ("gate", (2, PACK, 768), F32),
    ("up", (2, PACK, 768), F32),
    ("unit_grads", (3, PACK, 768), BF16),
    ("grad_proj", (PACK, QW), BF16),
    ("residual", (2, ROWS, D), F32),
    ("grad_residual", (ROWS, D), F32),
    ("part", (2, 4, ROWS, D), BF16),
    ("landing", (2, 3, ROWS, D), BF16),
    ("final", (2, ROWS, D), BF16),
    ("dsmall", (2, 16, D), F32),
    ("small_sum", (3, 16, D), F32),
    ("small_in", (7, 16, D), F32),
    ("q_in", (3, 4, 64, QW), BF16),
    ("g_in", (3, 2, 4, UNIT, D), BF16),
    ("d_in", (3, 4, UNIT, D), BF16),
    ("o_in", (3, 64, D), BF16),
    ("q_in2", (3, 64, QW), BF16),
    ("g_in2", (3, 2, UNIT, D), BF16),
    ("d_in2", (3, UNIT, D), BF16),
    ("o_in2", (3, 64, D), BF16),
]
N_SEM = 260


class Refs:
    pass


def program_kernel(*refs):
    (x_ref, cot_ref, small_ref, q_ref, f_ref, o_ref, perm_row, perm_col, doc_len) = refs[:9]
    rows_out, small_out, q_out, f_out, o_out = refs[9:14]
    s = Refs()
    for (name, _, _), ref in zip(SCRATCH, refs[14:]):
        setattr(s, name, ref)
    send, recv, local, credit = refs[14 + len(SCRATCH) :]
    sems = Semaphores(send, recv)
    core, seq, z, y = place()
    partner = {"section": 1 - core}
    x_peers = [along_x(seq, k) for k in (1, 2, 3)]
    y_peers = [along_y(z, y, k) for k in (1, 2, 3)]
    z_peers = [along_z(z, y, k) for k in (1, 2, 3)]
    perms = (perm_row, perm_col, doc_len)

    def gather(peers, source, target):
        return Direct(sems, peers, lambda k: source, lambda k: target)

    def owner(layer):
        return pl.when(core == layer)

    def other(layer):
        return pl.when(core != layer)

    greet(x_peers + y_peers + z_peers + [partner])

    own = [
        pltpu.make_async_copy(x_ref, s.rows_in.at[0, seq], local.at[0]),
        pltpu.make_async_copy(cot_ref, s.outer.at[1, seq], local.at[1]),
        pltpu.make_async_copy(small_ref, s.small.at[core], local.at[2]),
        pltpu.make_async_copy(q_ref, s.wq.at[core, z, y], local.at[3]),
        pltpu.make_async_copy(f_ref, s.wf.at[core, :, z, y], local.at[4]),
    ]
    own_o = pltpu.make_async_copy(o_ref, s.wo.at[core, y], local.at[5])
    x_gather = gather(x_peers, x_ref, s.rows_in.at[0, seq])
    cot_gather = gather(x_peers, cot_ref, s.outer.at[1, seq])
    pair_small = sems.copy(small_ref, s.small.at[core], partner)

    low, high = pl.ds(0, 32), pl.ds(32, 32)
    wq, wf, wo = s.wq.at[core], s.wf.at[core], s.wo.at[core]
    q_one = [
        gather(y_peers, q_ref.at[low], wq.at[z, y, low]),
        gather(z_peers, q_ref.at[high], wq.at[z, y, high]),
    ]
    q_two = [
        gather(z_peers, wq.at[z, :, low], wq.at[z, :, low]),
        gather(y_peers, wq.at[:, y, high], wq.at[:, y, high]),
    ]
    f_one = [
        gather(y_peers, f_ref.at[pl.ds(0, 2)], wf.at[pl.ds(0, 2), z, y]),
        gather(z_peers, f_ref.at[2], wf.at[2, z, y]),
    ]
    f_two = [
        gather(z_peers, wf.at[pl.ds(0, 2), z], wf.at[pl.ds(0, 2), z]),
        gather(y_peers, wf.at[2, :, y], wf.at[2, :, y]),
    ]
    o_copies = [sems.copy(o_ref, wo.at[y], peer) for peer in z_peers]
    o_two = gather(y_peers, wo.at[y], wo.at[y])

    def to_partner(piece):
        return sems.copy(piece, piece, partner)

    pair_q = [to_partner(wq.at[lax.rem(z + 4 - k, 4), :, low]) for k in range(4)] + [
        to_partner(wq.at[:, lax.rem(y + 4 - k, 4), high]) for k in range(4)
    ]
    pair_o = to_partner(wo)
    pair_f = [to_partner(wf.at[kind]) for kind in range(3)]

    def weights_first():
        for ring in q_one:
            ring.start()

        @pl.when(z == seq)
        def _():
            own_o.start()
            for copy in o_copies:
                copy.start()

        for ring in f_one:
            ring.start()

    def weights_second():
        own[3].wait()
        for half in (0, 1):
            q_one[half].arrive()
            q_two[half].start()
            pair_q[4 * half].start()

        @pl.when(z == seq)
        def _():
            own_o.wait()

        @pl.when(z != seq)
        def _():
            for k in range(3):

                @pl.when(lax.rem(seq + k + 1, 4) == z)
                def _():
                    o_copies[k].wait_recv()

        o_two.start()
        own[4].wait()
        for ring in f_one:
            ring.arrive()
        for ring in f_two:
            ring.start()

    def weights_third():
        for k in range(3):
            for half in (0, 1):
                q_two[half].copies[k].wait_recv()
                pair_q[4 * half + k + 1].start()
        o_two.arrive()
        pair_o.start()

    def weights_fourth():
        f_two[0].arrive()
        pair_f[0].start()
        pair_f[1].start()
        f_two[1].arrive()
        pair_f[2].start()

    def weights_sent():
        for ring in q_one + q_two + f_one + f_two + [o_two]:
            ring.sent()

        @pl.when(z == seq)
        def _():
            for copy in o_copies:
                copy.wait_send()

        for copy in pair_q + [pair_o] + pair_f:
            copy.wait_send()

    def pair_arrived(copies):
        for copy in copies:
            copy.wait_recv()

    def reduce_rows(turn):
        part, landing = s.part.at[turn % 2], s.landing.at[turn % 2]
        return [
            Direct(
                sems,
                x_peers,
                lambda k: part.at[lax.rem(seq + k + 1, 4), half],
                lambda k: landing.at[k, half],
            )
            for half in (low, high)
        ]

    def gather_rows(place_of):
        return [gather(x_peers, place_of.at[seq, half], place_of.at[seq, half]) for half in (low, high)]

    def exchange(turn, value, finish, place_of, during=None, between=None):
        s.part[turn % 2] = value.astype(BF16).reshape(4, ROWS, D)
        reduces = reduce_rows(turn)
        for ring in reduces:
            ring.start()
        if during is not None:
            during()
        gathers = gather_rows(place_of) if place_of is not None else []
        for index, half in enumerate((low, high)):
            reduces[index].arrive()
            total = s.part[turn % 2, seq, half].astype(F32)
            for k in range(3):
                total = total + s.landing[turn % 2, k, half].astype(F32)
            finish(total, half)
            if gathers:
                gathers[index].start()
        if between is not None:
            between()
        for ring in gathers:
            ring.arrive()
        for ring in reduces + gathers:
            ring.sent()

    def sum_over(ring, target, landing):
        ring.arrive()
        add_into(target, [landing.at[k] for k in range(3)])

    def scatter(peers, me, part, landing):
        return Direct(
            sems, peers, lambda k: part(lax.rem(me + k + 1, 4)), lambda k: landing.at[k]
        )

    class Gradients:
        def __init__(self, layer):
            self.layer = layer
            dq, df, do = s.dwq.at[layer], s.dwf.at[layer], s.dwo.at[layer]
            self.dq, self.df, self.do = dq, df, do
            self.pair_f = sems.copy(df, s.wf.at[layer], partner)
            self.pair_q = sems.copy(dq, s.wq.at[layer], partner)
            self.pair_o = sems.copy(do, s.wo.at[layer], partner)
            both = pl.ds(0, 2)
            self.f_one = [
                scatter(z_peers, z, lambda j: df.at[both, j], s.g_in),
                scatter(y_peers, y, lambda j: df.at[2, :, j], s.d_in),
            ]
            self.f_two = [
                scatter(y_peers, y, lambda j: df.at[both, z, j], s.g_in2),
                scatter(z_peers, z, lambda j: df.at[2, j, y], s.d_in2),
            ]
            self.q_one = [
                scatter(z_peers, z, lambda j: dq.at[j, :, low], s.q_in.at[:, :, low]),
                scatter(y_peers, y, lambda j: dq.at[:, j, high], s.q_in.at[:, :, high]),
            ]
            self.q_two = [
                scatter(y_peers, y, lambda j: dq.at[z, j, low], s.q_in2.at[:, low]),
                scatter(z_peers, z, lambda j: dq.at[j, y, high], s.q_in2.at[:, high]),
            ]
            self.o_one = scatter(y_peers, y, lambda j: do.at[j], s.o_in)
            self.o_two = [
                sems.copy(do.at[y], s.o_in2.at[k], along_z(z, y, 3 - k)) for k in range(3)
            ]
            self.q_three = gather(x_peers, dq.at[z, y], q_out.at[seq])
            self.f_three = gather(x_peers, df.at[:, z, y], f_out.at[seq])
            self.o_three = [sems.copy(do.at[y], o_out, peer) for peer in x_peers]
            self.keep = [
                pltpu.make_async_copy(dq.at[z, y], q_out.at[seq], local.at[6]),
                pltpu.make_async_copy(df.at[:, z, y], f_out.at[seq], local.at[7]),
                pltpu.make_async_copy(do.at[y], o_out, local.at[8]),
            ]

        def free_f(self):
            @owner(self.layer)
            def _():
                pl.semaphore_signal(credit.at[0], inc=1, device_id=partner, device_id_type=MESH)

        def free_q(self):
            @owner(self.layer)
            def _():
                pl.semaphore_signal(credit.at[1], inc=1, device_id=partner, device_id_type=MESH)

        def hand_f(self):
            @other(self.layer)
            def _():
                pl.semaphore_wait(credit.at[0], 1)
                self.pair_f.start()

        def hand_q(self):
            @other(self.layer)
            def _():
                pl.semaphore_wait(credit.at[1], 1)
                self.pair_q.start()
                self.pair_o.start()

        def f_first(self):
            @owner(self.layer)
            def _():
                self.pair_f.wait_recv()
                add_into(self.df, [s.wf.at[self.layer]])
                for ring in self.f_one:
                    ring.start()

        def q_first(self):
            @owner(self.layer)
            def _():
                self.pair_q.wait_recv()
                add_into(self.dq, [s.wq.at[self.layer]])
                for ring in self.q_one:
                    ring.start()
                self.pair_o.wait_recv()
                add_into(self.do, [s.wo.at[self.layer]])
                self.o_one.start()

        def f_second(self):
            @owner(self.layer)
            def _():
                sum_over(self.f_one[0], self.df.at[pl.ds(0, 2), z], s.g_in)
                self.f_two[0].start()
                sum_over(self.f_one[1], self.df.at[2, :, y], s.d_in)
                self.f_two[1].start()

        def q_second(self):
            @owner(self.layer)
            def _():
                sum_over(self.q_one[0], self.dq.at[z, :, low], s.q_in.at[:, :, low])
                self.q_two[0].start()
                sum_over(self.q_one[1], self.dq.at[:, y, high], s.q_in.at[:, :, high])
                self.q_two[1].start()
                sum_over(self.o_one, self.do.at[y], s.o_in)
                for k in range(3):

                    @pl.when(lax.rem(z + 3 - k, 4) == seq)
                    def _():
                        self.o_two[k].start()

        def f_third(self):
            @owner(self.layer)
            def _():
                sum_over(self.f_two[0], self.df.at[pl.ds(0, 2), z, y], s.g_in2)
                sum_over(self.f_two[1], self.df.at[2, z, y], s.d_in2)
                self.f_three.start()
                self.keep[1].start()

        def q_third(self):
            @owner(self.layer)
            def _():
                sum_over(self.q_two[0], self.dq.at[z, y, low], s.q_in2.at[:, low])
                sum_over(self.q_two[1], self.dq.at[z, y, high], s.q_in2.at[:, high])
                self.q_three.start()
                self.keep[0].start()

                @pl.when(z == seq)
                def _():
                    for k in range(3):
                        self.o_two[k].wait_recv()
                    add_into(self.do.at[y], [s.o_in2.at[k] for k in range(3)])
                    for copy in self.o_three:
                        copy.start()
                    self.keep[2].start()

        def end(self):
            @owner(self.layer)
            def _():
                self.f_three.arrive()
                self.q_three.arrive()
                for ring in self.f_one + self.f_two + self.q_one + self.q_two:
                    ring.sent()
                for ring in (self.o_one, self.q_three, self.f_three):
                    ring.sent()
                for k in range(3):

                    @pl.when(lax.rem(z + 3 - k, 4) == seq)
                    def _():
                        self.o_two[k].wait_send()

                self.keep[0].wait()
                self.keep[1].wait()

                @pl.when(z == seq)
                def _():
                    self.keep[2].wait()
                    for copy in self.o_three:
                        copy.wait_send()

                for k in range(3):

                    @pl.when(lax.rem(z + k + 1, 4) == seq)
                    def _():
                        self.o_three[k].wait_recv()

            @other(self.layer)
            def _():
                for copy in (self.pair_f, self.pair_q, self.pair_o):
                    copy.wait_send()

    grads = [Gradients(0), Gradients(1)]

    x_gather.start()
    pair_small.start()
    for copy in own:
        copy.start()

    @owner(0)
    def _():
        weights_first()

    cot_gather.start()
    own[0].wait()
    own[2].wait()

    @owner(0)
    def _():
        weights_second()

    x_gather.arrive()
    pair_small.wait_recv()

    @owner(0)
    def _():
        weights_third()

    @owner(1)
    def _():
        pair_arrived(pair_q)
        pair_arrived([pair_o])
        weights_first()

    for layer in (0, 1):
        mixer_forward(s, *perms, layer)

        def spread_on():
            if layer == 0:

                @owner(0)
                def _():
                    weights_fourth()

                @owner(1)
                def _():
                    weights_second()

        def attended(total, half):
            residual = s.rows_in[layer, seq, half].astype(F32) + total
            s.residual[layer, half] = residual
            s.normed_ffn[layer, seq, half] = (
                residual * rms(residual) * s.small[layer, 1:2, :]
            ).astype(BF16)

        exchange(
            2 * layer,
            dot(s.att[layer], s.wo[layer].reshape(256, D), NN),
            attended,
            s.normed_ffn.at[layer],
            spread_on,
        )

        @other(layer)
        def _():
            pair_arrived(pair_f)

        def hand_on():
            if layer == 0:

                @owner(1)
                def _():
                    weights_third()
                    weights_fourth()

        def leave(total, half):
            out = (s.residual[layer, half] + total).astype(BF16)
            if layer == 0:
                s.rows_in[1, seq, half] = out
            else:
                s.final[0, half] = out

        exchange(
            2 * layer + 1,
            ffn_forward(s, layer),
            leave,
            s.rows_in.at[1] if layer == 0 else None,
            hand_on,
        )
        if layer == 0:

            @owner(0)
            def _():
                pair_arrived(pair_q)
                pair_arrived([pair_o])

    weights_sent()
    own[1].wait()
    cot_gather.arrive()
    for layer in (1, 0):
        mine = grads[layer]

        def weights_of_ffn():
            mine.free_f()
            ffn_weights(s, layer)
            mine.hand_f()
            if layer == 0:
                grads[1].f_second()
                grads[1].q_first()

        def back_ffn(total, half):
            value = s.residual[layer, half]
            grad, gain = rms_back(total, value, rms(value), s.small[layer, 1:2, :])
            grad = s.outer[layer, seq, half].astype(F32) + grad
            s.grad_residual[half] = grad
            s.branch[layer, seq, half] = grad.astype(BF16)
            gains.append(gain)

        def after_ffn():
            if layer == 0:
                mine.f_first()

        gains = []
        exchange(
            8 - 2 * layer - 2,
            ffn_backward(s, layer),
            back_ffn,
            s.branch.at[layer],
            weights_of_ffn,
            after_ffn,
        )
        gain_ffn = gains[0] + gains[1]
        mixer_backward(s, *perms, layer)
        s.dsmall[layer, 1:2, :] = gain_ffn

        def weights_of_mixer():
            mine.free_q()
            mixer_weights(s, layer)
            mine.hand_q()
            if layer == 1:
                mine.f_first()
            else:
                grads[1].f_third()
                grads[1].q_second()
                mine.f_second()

        def back_in(total, half):
            value = s.rows_in[layer, seq, half].astype(F32)
            grad, gain = rms_back(total, value, rms(value), s.small[layer, 0:1, :])
            grad = (s.grad_residual[half] + grad).astype(BF16)
            gains.append(gain)
            if layer == 1:
                s.outer[0, seq, half] = grad
            else:
                s.final[1, half] = grad

        gains = []
        exchange(
            8 - 2 * layer - 1,
            dot(s.grad_proj[...], s.wq[layer].reshape(D, QW), NT),
            back_in,
            s.outer.at[0] if layer == 1 else None,
            weights_of_mixer,
        )
        s.dsmall[layer, 0:1, :] = gains[0] + gains[1]

    rows_copies = [
        pltpu.make_async_copy(s.final.at[k], rows_out.at[k, core], local.at[9 + k]) for k in (0, 1)
    ]
    pair_rows = [sems.copy(s.final.at[k], rows_out.at[k, core], partner) for k in (0, 1)]
    pair_gains = sems.copy(s.dsmall.at[1 - core], s.small_in.at[0], partner)
    pair_gains.start()
    for copy in rows_copies + pair_rows:
        copy.start()
    grads[0].q_first()
    pair_gains.wait_recv()
    s.small_sum[0] = s.dsmall[core] + s.small_in[0]
    small_y = Direct(sems, y_peers, lambda k: s.small_sum.at[0], lambda k: s.small_in.at[1 + k])
    small_z = Direct(sems, z_peers, lambda k: s.small_sum.at[1], lambda k: s.small_in.at[4 + k])
    small_x = gather(x_peers, s.small_sum.at[2], small_out.at[seq])
    small_y.start()
    grads[1].q_third()
    small_y.arrive()
    s.small_sum[1] = s.small_sum[0] + s.small_in[1] + s.small_in[2] + s.small_in[3]
    small_z.start()
    grads[0].f_third()
    grads[0].q_second()
    small_z.arrive()
    s.small_sum[2] = s.small_sum[1] + s.small_in[4] + s.small_in[5] + s.small_in[6]
    small_keep = pltpu.make_async_copy(s.small_sum.at[2], small_out.at[seq], local.at[11])
    small_x.start()
    small_keep.start()
    grads[0].q_third()
    grads[1].end()
    grads[0].end()
    small_x.arrive()
    for copy in pair_rows:
        copy.wait()
    pair_gains.wait_send()
    for ring in (small_y, small_z, small_x, x_gather, cot_gather):
        ring.sent()
    pair_small.wait_send()
    for copy in rows_copies + [small_keep]:
        copy.wait()


def whole_program(*operands):
    return pl.pallas_call(
        program_kernel,
        out_shape=[
            sds((2, 2, ROWS, D), BF16),
            sds((4, 16, D), F32),
            sds((4, 64, QW), BF16),
            sds((4, 3, UNIT, D), BF16),
            sds((64, D), BF16),
        ],
        in_specs=[ANY] * 6 + [VMEM] * 2 + [SMEM],
        out_specs=[ANY] * 5,
        scratch_shapes=[pltpu.VMEM(shape, dtype) for _, shape, dtype in SCRATCH]
        + [
            pltpu.SemaphoreType.DMA((N_SEM,)),
            pltpu.SemaphoreType.DMA((N_SEM,)),
            pltpu.SemaphoreType.DMA((12,)),
            pltpu.SemaphoreType.REGULAR((2,)),
        ],
        compiler_params=pltpu.CompilerParams(
            collective_id=1, has_side_effects=True, vmem_limit_bytes=VMEM_BYTES
        ),
        name="layers",
    )(*operands)


def local(
    block_in,
    cotangent,
    perm_rows,
    doc_lengths,
    norm_in,
    w_qkv,
    w_beta,
    conv_w,
    norm_head,
    w_out,
    norm_ffn,
    w_ffn,
    w_down,
):
    core, seq = lax.axis_index("section"), lax.axis_index("seq")

    def mine(array):
        return lax.dynamic_index_in_dim(array, core, 0, keepdims=False)[0]

    x, cot = mine(block_in), mine(cotangent)
    perm, doc_len = mine(perm_rows), mine(doc_lengths)
    heads = lax.dynamic_slice_in_dim(conv_w[0], seq * 256, 256, 2).reshape(12, 256)
    small = jnp.concatenate(
        [
            norm_in,
            norm_ffn,
            jnp.pad(norm_head, ((0, 1), (0, D - HD))),
            jnp.pad(heads, ((0, 0), (0, D - 256))),
        ],
        axis=0,
    )
    q = jnp.concatenate(
        [
            lax.dynamic_slice_in_dim(w_qkv[0].reshape(64, 3, D), seq * 256, 256, 2).reshape(64, 768),
            jnp.pad(lax.dynamic_slice_in_dim(w_beta[0], seq * 2, 2, 1), ((0, 0), (0, 126))),
        ],
        axis=1,
    )
    shard = jnp.concatenate([jnp.swapaxes(w_ffn[0], 1, 2), w_down], axis=0)
    shard = jnp.pad(shard, ((0, 0), (0, 16), (0, 0)))
    shard = lax.dynamic_slice_in_dim(shard, seq * UNIT, UNIT, 1)
    rows, small_sum, q_sum, f_sum, o_sum = whole_program(
        x, cot, small, q, shard, w_out[0], perm[None, :], perm[:, None], doc_len
    )
    total = jnp.sum(small_sum, axis=0)
    grad_conv = jnp.transpose(small_sum[:, 4:, :256].reshape(4, 4, 3, 256), (1, 2, 0, 3))
    grad_qkv = jnp.transpose(q_sum[:, :, :768].reshape(4, 64, 3, 256), (1, 2, 0, 3))
    grad_beta = jnp.transpose(q_sum[:, :, 768:770], (1, 0, 2))
    grad_units = jnp.swapaxes(f_sum, 0, 1).reshape(3, 192, D)[:, :176].astype(F32)
    return (
        rows[0][:, None],
        rows[1][:, None],
        total[0:1],
        grad_qkv.reshape(1, 64, 3 * D).astype(F32),
        grad_beta.reshape(1, 64, H).astype(F32),
        grad_conv.reshape(1, 4, 3, D),
        total[2:3, :HD],
        o_sum[None].astype(F32),
        total[1:2],
        jnp.swapaxes(grad_units[:2], 1, 2)[None],
        grad_units[2][None],
    )


def solution(mesh):
    placed = (
        P(None, "fsdp", "seq", None),
        P(None, "fsdp", "seq", None),
        P(None, "fsdp", None),
        P(None, "fsdp", None),
        P("section", None),
        P("section", "fsdp", None),
        P("section", "fsdp", None),
        P("section", None, None, None),
        P("section", None),
        P("section", "fsdp", None),
        P("section", None),
        P("section", None, None, "fsdp"),
        P("section", "fsdp", None),
    )
    return jax.shard_map(
        local,
        mesh=mesh,
        in_specs=placed,
        out_specs=(
            P(None, "fsdp", "seq", None),
            P(None, "fsdp", "seq", None),
            P("section", None),
            P("section", "fsdp", None),
            P("section", "fsdp", None),
            P("section", None, None, None),
            P("section", None),
            P("section", "fsdp", None),
            P("section", None),
            P("section", None, None, "fsdp"),
            P("section", "fsdp", None),
        ),
        check_vma=False,
    )
```

```python
import functools

import jax
import jax.numpy as jnp
from jax import lax
from jax.experimental import pallas as pl
from jax.experimental.pallas import tpu as pltpu
from jax.sharding import PartitionSpec as P

D = 1024
H = 8
HD = 128
PACK = 256
ROWS = 64
UNIT = 48
QW = 896
MESH = pl.DeviceIdType.MESH
F32, BF16 = jnp.float32, jnp.bfloat16
VMEM = pl.BlockSpec(memory_space=pltpu.VMEM)
SMEM = pl.BlockSpec(memory_space=pltpu.SMEM)
ANY = pl.BlockSpec(memory_space=pl.ANY)
VMEM_BYTES = 60 * 1024 * 1024


def sds(shape, dtype):
    return jax.ShapeDtypeStruct(shape, dtype)


def dot(left, right, dims):
    return lax.dot_general(left, right, (dims, ((), ())), preferred_element_type=F32)


NN = ((1,), (0,))
NT = ((1,), (1,))
TN = ((0,), (0,))


def halves(value):
    high = value.astype(BF16)
    return high, (value - high.astype(F32)).astype(BF16)


def dot3(left, right, dims):
    return dot(left[0], right[0], dims) + (
        dot(left[0], right[1], dims) + dot(left[1], right[0], dims)
    )


def place():
    fsdp = lax.axis_index("fsdp")
    return (
        lax.axis_index("section"),
        lax.axis_index("seq"),
        lax.div(fsdp, 4),
        lax.rem(fsdp, 4),
    )


def along_x(seq, step):
    return {"seq": lax.rem(seq + step, 4)}


def along_y(z, y, step):
    return {"fsdp": z * 4 + lax.rem(y + step, 4)}


def along_z(z, y, step):
    return {"fsdp": lax.rem(z + step, 4) * 4 + y}


def greet(peers):
    barrier = pltpu.get_barrier_semaphore()
    for peer in peers:
        pl.semaphore_signal(barrier, inc=1, device_id=peer, device_id_type=MESH)
    pl.semaphore_wait(barrier, len(peers))


def remote(source, target, send, recv, peer):
    return pltpu.make_async_remote_copy(
        src_ref=source,
        dst_ref=target,
        send_sem=send,
        recv_sem=recv,
        device_id=peer,
        device_id_type=MESH,
    )


CUT = 80


class Direct:
    def __init__(self, sems, peers, source, target):
        self.copies = [sems.copy(source(k), target(k), peer) for k, peer in enumerate(peers)]

    def start(self):
        for copy in self.copies:
            copy.start()

    def arrive(self):
        for copy in self.copies:
            copy.wait_recv()

    def sent(self):
        for copy in self.copies:
            copy.wait_send()


class Semaphores:
    def __init__(self, send, recv):
        self.send, self.recv, self.used = send, recv, 0

    def copy(self, source, target, peer):
        index = self.used
        self.used += 1
        return remote(source, target, self.send.at[index], self.recv.at[index], peer)


def add_into(target, others):
    shape = target.shape
    if len(shape) == 2:
        value = target[...].astype(F32)
        for other in others:
            value = value + other[...].astype(F32)
        target[...] = value.astype(target.dtype)
        return

    def body(index, carry):
        add_into(target.at[index], [other.at[index] for other in others])
        return carry

    lax.fori_loop(0, shape[0], body, 0)


def rms(value):
    return lax.rsqrt(jnp.mean(value * value, axis=-1, keepdims=True) + 1e-06)


def rms_back(grad, value, scale, gain):
    weighted = grad * gain
    inner = jnp.mean(weighted * value, axis=-1, keepdims=True)
    return (
        scale * weighted - value * (scale * scale * scale) * inner,
        jnp.sum(grad * value * scale, axis=0, keepdims=True),
    )


def shifted(value, step):
    rows = value.shape[0]
    filler = jnp.zeros((abs(step), value.shape[1]), value.dtype)
    if step > 0:
        return jnp.concatenate([filler, value[: rows - step]], axis=0)
    return jnp.concatenate([value[-step:], filler], axis=0)


def doc_places(doc_len):
    col = lax.broadcasted_iota(jnp.int32, (PACK, 1), 0)
    row = lax.broadcasted_iota(jnp.int32, (1, PACK), 1)
    start_col, start_row = jnp.zeros_like(col), jnp.zeros_like(row)
    end = 0
    for doc in range(4):
        end = end + doc_len[doc]
        start_col = jnp.where(col >= end, end, start_col)
        start_row = jnp.where(row >= end, end, start_row)
    return col - start_col, start_col == start_row


def one_hot(column, row):
    return (column == row).astype(F32).astype(BF16)


def sigmoid(value):
    return 1.0 / (1.0 + jnp.exp(-value))


def conv_taps(small_ref, layer, tap, part):
    return small_ref[layer, 4 + tap * 3 + part : 5 + tap * 3 + part, 0:256]


def conv_part(series, small_ref, layer, part, offset):
    total = series * conv_taps(small_ref, layer, 0, part)
    for tap in range(1, 4):
        moved = jnp.where(offset >= tap, shifted(series, tap), 0.0)
        total = total + moved * conv_taps(small_ref, layer, tap, part)
    return total


def inverse(system):
    col = lax.broadcasted_iota(jnp.int32, (PACK, PACK), 0)
    row = lax.broadcasted_iota(jnp.int32, (PACK, PACK), 1)
    apart = col ^ row
    result = jnp.where(col == row, 1.0, 0.0) - jnp.where(apart == 1, system, 0.0)
    high, low = halves(system)
    for level in range(1, 8):
        mask = (apart >> level) == 1
        corner = halves(jnp.where(mask, system, 0.0))
        now = halves(result)
        inner = halves(dot3(corner, now, NN))
        result = result - dot3(now, inner, NN)
    return result


def unit(value):
    scale = lax.rsqrt(jnp.sum(value * value, axis=-1, keepdims=True) + 1e-06)
    return value * scale, scale


def masks():
    col = lax.broadcasted_iota(jnp.int32, (PACK, PACK), 0)
    row = lax.broadcasted_iota(jnp.int32, (PACK, PACK), 1)
    return col, row


def to_places(perm_row):
    return one_hot(lax.broadcasted_iota(jnp.int32, (PACK, 1), 0), perm_row)


def norm_rows(s, layer):
    x = s.rows_in[layer].reshape(PACK, D).astype(F32)
    s.normed[layer] = (x * rms(x) * s.small[layer, 0:1, :]).astype(BF16)


def mixer_forward(s, perm_row, doc_len, layer, midway):
    small = s.small
    proj = dot(s.normed[layer], s.wq[layer].reshape(D, QW), NN).astype(BF16)
    places = to_places(perm_row)
    proj = dot(places, proj, NN)
    s.proj[layer] = proj.astype(BF16)
    offset, same = doc_places(doc_len)
    activated = []
    for kind in range(3):
        pre = conv_part(proj[:, 256 * kind : 256 * kind + 256], small, layer, kind, offset)
        activated.append(pre * sigmoid(pre))
    midway()
    col, row = masks()
    strict = same & (col > row)
    tri = same & (col >= row)
    heads = []
    for head in range(2):
        lanes = slice(128 * head, 128 * head + 128)
        query = halves(unit(activated[0][:, lanes])[0] * HD**-0.5)
        key = halves(unit(activated[1][:, lanes])[0])
        value = activated[2][:, lanes]
        strength = sigmoid(proj[:, 768 + head : 769 + head])
        system = jnp.where(strict, strength * dot3(key, key, NT), 0.0)
        solved = inverse(system)
        s.solved[layer, head] = solved
        fresh = dot3(halves(solved), halves(strength * value), NN)
        s.fresh[layer, head] = fresh
        scores = jnp.where(tri, dot3(query, key, NT), 0.0)
        produced = dot3(halves(scores), halves(fresh), NN)
        s.produced[layer, head] = produced
        scale = lax.rsqrt(jnp.mean(produced * produced, axis=-1, keepdims=True) + 1e-05)
        heads.append((produced * scale * small[layer, 2:3, 0:128]).astype(BF16))
    mixed = jnp.concatenate(heads, axis=1)
    s.att[layer] = dot(places, mixed, TN).astype(BF16)


def mixer_backward(s, perm_row, doc_len, layer):
    small = s.small
    grad = s.branch[layer].reshape(PACK, D)
    grad_att = dot(grad, s.wo[layer].reshape(256, D), NT).astype(BF16)
    places = to_places(perm_row)
    grad_att = dot(places, grad_att, NN)
    proj = s.proj[layer].astype(F32)
    offset, same = doc_places(doc_len)
    pres, gates = [], []
    for kind in range(3):
        pre = conv_part(proj[:, 256 * kind : 256 * kind + 256], small, layer, kind, offset)
        pres.append(pre)
        gates.append(sigmoid(pre))
    col, row = masks()
    strict = same & (col > row)
    tri = same & (col >= row)
    gain = small[layer, 2:3, 0:128]
    gain_grad = jnp.zeros((1, HD), F32)
    grads = [[], [], []]
    logit_grads = []
    for head in range(2):
        lanes = slice(128 * head, 128 * head + 128)
        act_q, act_k, value = [(pre * gate)[:, lanes] for pre, gate in zip(pres, gates)]
        query_f, scale_q = unit(act_q)
        key_f, scale_k = unit(act_k)
        query, key = halves(query_f * HD**-0.5), halves(key_f)
        strength = sigmoid(proj[:, 768 + head : 769 + head])
        produced = s.produced[layer, head]
        scale = lax.rsqrt(jnp.mean(produced * produced, axis=-1, keepdims=True) + 1e-05)
        given = grad_att[:, lanes]
        weighted = given * gain
        inner = jnp.mean(weighted * produced, axis=-1, keepdims=True)
        grad_o = halves(scale * weighted - produced * (scale * scale * scale) * inner)
        gain_grad = gain_grad + jnp.sum(given * produced * scale, axis=0, keepdims=True)
        fresh = halves(s.fresh[layer, head])
        gram = dot3(key, key, NT)
        scores = halves(jnp.where(tri, dot3(query, key, NT), 0.0))
        grad_scores = halves(jnp.where(tri, dot3(grad_o, fresh, NT), 0.0))
        grad_fresh = halves(dot3(scores, grad_o, TN))
        grad_source = dot3(halves(s.solved[layer, head]), grad_fresh, TN)
        grad_system = jnp.where(strict, -dot3(halves(grad_source), fresh, NT), 0.0)
        grad_gram = halves(strength * grad_system)
        grad_query = dot3(grad_scores, key, NN)
        grad_key = (
            dot3(grad_scores, query, TN) + dot3(grad_gram, key, NN) + dot3(grad_gram, key, TN)
        )
        grad_value = strength * grad_source
        grad_strength = jnp.sum(grad_source * value, axis=-1, keepdims=True) + jnp.sum(
            grad_system * gram, axis=-1, keepdims=True
        )
        logit_grads.append(grad_strength * strength * (1.0 - strength))
        grads[0].append(
            HD**-0.5
            * (
                scale_q * grad_query
                - act_q
                * (scale_q * scale_q * scale_q)
                * jnp.sum(act_q * grad_query, axis=-1, keepdims=True)
            )
        )
        grads[1].append(
            scale_k * grad_key
            - act_k
            * (scale_k * scale_k * scale_k)
            * jnp.sum(act_k * grad_key, axis=-1, keepdims=True)
        )
        grads[2].append(grad_value)
    dsmall = s.dsmall.at[layer]
    dsmall[...] = jnp.zeros((16, D), F32)
    dsmall[2:3, 0:128] = gain_grad
    pieces = []
    for kind in range(3):
        pre, gate = pres[kind], gates[kind]
        grad_pre = jnp.concatenate(grads[kind], axis=1) * gate * (1.0 + pre * (1.0 - gate))
        series = proj[:, 256 * kind : 256 * kind + 256]
        total = grad_pre * conv_taps(small, layer, 0, kind)
        dsmall[4 + kind : 5 + kind, 0:256] = jnp.sum(grad_pre * series, axis=0, keepdims=True)
        for tap in range(1, 4):
            kept = jnp.where(offset >= tap, grad_pre, 0.0)
            total = total + shifted(kept, -tap) * conv_taps(small, layer, tap, kind)
            dsmall[4 + tap * 3 + kind : 5 + tap * 3 + kind, 0:256] = jnp.sum(
                kept * shifted(series, tap), axis=0, keepdims=True
            )
        pieces.append(total.astype(BF16))
    lane = lax.broadcasted_iota(jnp.int32, (1, 128), 1)
    pieces.append(
        jnp.where(lane == 0, logit_grads[0], jnp.where(lane == 1, logit_grads[1], 0.0)).astype(BF16)
    )
    grad_proj = jnp.concatenate(pieces, axis=1)
    s.grad_proj[...] = dot(places, grad_proj, TN).astype(BF16)


def units(weights, layer, kind):
    return weights[layer, :, :, UNIT * kind : UNIT * kind + UNIT, :].reshape(768, D)


def ffn_forward(s, layer):
    normed = s.normed_ffn[layer].reshape(PACK, D)
    gate = dot(normed, units(s.wf, layer, 0), NT)
    up = dot(normed, units(s.wf, layer, 1), NT)
    s.gate[layer] = gate
    s.up[layer] = up
    hidden = (gate * sigmoid(gate) * up).astype(BF16)
    return dot(hidden, units(s.wf, layer, 2), NN)


def ffn_backward(s, layer):
    grad = s.outer[layer].reshape(PACK, D)
    gate, up = s.gate[layer], s.up[layer]
    sig = sigmoid(gate)
    grad_hidden = dot(grad, units(s.wf, layer, 2), NT)
    grad_gate = (grad_hidden * up * sig * (1.0 + gate * (1.0 - sig))).astype(BF16)
    grad_up = (grad_hidden * gate * sig).astype(BF16)
    s.unit_grads[0] = grad_gate
    s.unit_grads[1] = grad_up
    s.unit_grads[2] = (gate * sig * up).astype(BF16)
    return dot(grad_gate, units(s.wf, layer, 0), NN) + dot(grad_up, units(s.wf, layer, 1), NN)


def ffn_weights(s, layer, kind):
    right = (s.outer if kind == 2 else s.normed_ffn)[layer].reshape(PACK, D)
    s.dwf[layer, :, :, UNIT * kind : UNIT * kind + UNIT, :] = (
        dot(s.unit_grads[kind], right, TN).astype(BF16).reshape(4, 4, UNIT, D)
    )


def mixer_weights(s, layer):
    s.dwo[layer] = (
        dot(s.att[layer], s.branch[layer].reshape(PACK, D), TN).astype(BF16).reshape(4, 64, D)
    )
    s.dwq[layer] = (
        dot(s.normed[layer], s.grad_proj[...], TN).astype(BF16).reshape(4, 4, 64, QW)
    )


SCRATCH = [
    ("rows_in", (2, 4, ROWS, D), BF16),
    ("outer", (2, 4, ROWS, D), BF16),
    ("normed_ffn", (2, 4, ROWS, D), BF16),
    ("branch", (2, 4, ROWS, D), BF16),
    ("small", (2, 16, D), F32),
    ("wq", (2, 4, 4, 64, QW), BF16),
    ("wf", (2, 4, 4, 3 * UNIT, D), BF16),
    ("wo", (2, 4, 64, D), BF16),
    ("dwq", (2, 4, 4, 64, QW), BF16),
    ("dwf", (2, 4, 4, 3 * UNIT, D), BF16),
    ("dwo", (2, 4, 64, D), BF16),
    ("normed", (2, PACK, D), BF16),
    ("proj", (2, PACK, QW), BF16),
    ("solved", (2, 2, PACK, PACK), F32),
    ("fresh", (2, 2, PACK, HD), F32),
    ("produced", (2, 2, PACK, HD), F32),
    ("att", (2, PACK, 256), BF16),
    ("gate", (2, PACK, 768), F32),
    ("up", (2, PACK, 768), F32),
    ("unit_grads", (3, PACK, 768), BF16),
    ("grad_proj", (PACK, QW), BF16),
    ("residual", (2, ROWS, D), F32),
    ("grad_residual", (ROWS, D), F32),
    ("part", (2, 4, ROWS, D), BF16),
    ("landing", (2, 3, ROWS, D), BF16),
    ("final", (2, ROWS, D), BF16),
    ("dsmall", (2, 16, D), F32),
    ("small_sum", (3, 16, D), F32),
    ("small_in", (7, 16, D), F32),
    ("q_in", (3, 4, 64, QW), BF16),
    ("g_in", (3, 4, CUT, D), BF16),
    ("d_in", (3, 4, 3 * UNIT - CUT, D), BF16),
    ("o_in", (3, 64, D), BF16),
    ("q_in2", (3, 64, QW), BF16),
    ("g_in2", (3, CUT, D), BF16),
    ("d_in2", (3, 3 * UNIT - CUT, D), BF16),
    ("o_in2", (3, 64, D), BF16),
]
N_SEM = 280


class Refs:
    pass


def pick(rows, columns, first):
    row = lax.broadcasted_iota(jnp.int32, (rows, columns), 0)
    column = lax.broadcasted_iota(jnp.int32, (rows, columns), 1)
    return one_hot(column, row + first)


def pick_columns(count, first):
    row = lax.broadcasted_iota(jnp.int32, (count, 128), 0)
    column = lax.broadcasted_iota(jnp.int32, (count, 128), 1)
    return ((row == first + column) & (column < 2)).astype(F32).astype(BF16)


def program_kernel(*refs):
    (
        block_in,
        cotangent,
        perm_ref,
        doc_ref,
        norm_in,
        w_qkv,
        w_beta,
        conv_w,
        norm_head,
        w_out,
        norm_ffn,
        w_ffn,
        w_down,
    ) = refs[:13]
    rows_out, small_out, q_out, f_out, o_out = refs[13:18]
    s = Refs()
    for (name, _, _), ref in zip(SCRATCH, refs[18:]):
        setattr(s, name, ref)
    send, recv, local, credit = refs[18 + len(SCRATCH) :]
    sems = Semaphores(send, recv)
    core, seq, z, y = place()
    partner = {"section": 1 - core}
    x_peers = [along_x(seq, k) for k in (1, 2, 3)]
    y_peers = [along_y(z, y, k) for k in (1, 2, 3)]
    z_peers = [along_z(z, y, k) for k in (1, 2, 3)]
    perm_row = perm_ref[core]
    perms = (perm_row, [doc_ref[core, 0, k] for k in range(4)])
    x_ref, cot_ref, o_ref = block_in.at[core, 0], cotangent.at[core, 0], w_out.at[0]

    def gather(peers, source, target):
        return Direct(sems, peers, lambda k: source, lambda k: target)

    def owner(layer):
        return pl.when(core == layer)

    def other(layer):
        return pl.when(core != layer)

    low, high = pl.ds(0, 32), pl.ds(32, 32)
    f_low, f_high = pl.ds(0, CUT), pl.ds(CUT, 3 * UNIT - CUT)
    wq, wf, wo = s.wq.at[core], s.wf.at[core], s.wo.at[core]

    own_q = [
        pltpu.make_async_copy(
            w_qkv.at[0, :, pl.ds(pl.multiple_of(D * kind + 256 * seq, 256), 256)],
            wq.at[z, y, :, pl.ds(256 * kind, 256)],
            local.at[kind],
        )
        for kind in range(3)
    ]
    for copy in own_q:
        copy.start()
    own_x = pltpu.make_async_copy(x_ref, s.rows_in.at[0, seq], local.at[3])
    own_cot = pltpu.make_async_copy(cot_ref, s.outer.at[1, seq], local.at[4])
    own_o = pltpu.make_async_copy(o_ref, wo.at[y], local.at[5])
    own_x.start()
    own_cot.start()

    greet(x_peers + y_peers + z_peers + [partner])
    x_gather = gather(x_peers, x_ref, s.rows_in.at[0, seq])
    cot_gather = gather(x_peers, cot_ref, s.outer.at[1, seq])
    pair_small = sems.copy(s.small.at[core], s.small.at[core], partner)
    x_gather.start()

    q_one = [
        gather(y_peers, wq.at[z, y, low], wq.at[z, y, low]),
        gather(z_peers, wq.at[z, y, high], wq.at[z, y, high]),
    ]
    q_two = [
        gather(z_peers, wq.at[z, :, low], wq.at[z, :, low]),
        gather(y_peers, wq.at[:, y, high], wq.at[:, y, high]),
    ]
    f_one = [
        gather(y_peers, wf.at[z, y, f_low], wf.at[z, y, f_low]),
        gather(z_peers, wf.at[z, y, f_high], wf.at[z, y, f_high]),
    ]
    f_two = [
        gather(z_peers, wf.at[z, :, f_low], wf.at[z, :, f_low]),
        gather(y_peers, wf.at[:, y, f_high], wf.at[:, y, f_high]),
    ]
    o_copies = [sems.copy(o_ref, wo.at[y], peer) for peer in z_peers]
    o_two = gather(y_peers, wo.at[y], wo.at[y])

    def to_partner(piece):
        return sems.copy(piece, piece, partner)

    def pair_pieces(ref, first, second):
        return [to_partner(ref.at[lax.rem(z + 4 - k, 4), :, first]) for k in range(4)] + [
            to_partner(ref.at[:, lax.rem(y + 4 - k, 4), second]) for k in range(4)
        ]

    pair_q = pair_pieces(wq, low, high)
    pair_f = pair_pieces(wf, f_low, f_high)
    pair_o = to_partner(wo)

    def weights_first():
        for ring in q_one:
            ring.start()

        @pl.when(z == seq)
        def _():
            own_o.start()
            for copy in o_copies:
                copy.start()

    def weights_second():
        for half in (0, 1):
            q_one[half].arrive()
            q_two[half].start()
            pair_q[4 * half].start()

        @pl.when(z == seq)
        def _():
            own_o.wait()

        for k in range(3):

            @pl.when(lax.rem(seq + k + 1, 4) == z)
            def _():
                o_copies[k].wait_recv()

        o_two.start()

    def weights_third():
        for k in range(3):
            for half in (0, 1):
                q_two[half].copies[k].wait_recv()
                pair_q[4 * half + k + 1].start()
        o_two.arrive()
        pair_o.start()
        for ring in f_one:
            ring.start()

    def weights_next():
        for half in (0, 1):
            f_one[half].arrive()
            f_two[half].start()
            pair_f[4 * half].start()

    def weights_fourth():
        for k in range(3):
            for half in (0, 1):
                f_two[half].copies[k].wait_recv()
                pair_f[4 * half + k + 1].start()

    def weights_sent():
        for ring in q_one + q_two + f_one + f_two + [o_two]:
            ring.sent()

        @pl.when(z == seq)
        def _():
            for copy in o_copies:
                copy.wait_send()

        for copy in pair_q + pair_f + [pair_o]:
            copy.wait_send()

    def pair_arrived(copies):
        for copy in copies:
            copy.wait_recv()

    def reduce_rows(turn):
        part, landing = s.part.at[turn % 2], s.landing.at[turn % 2]
        return [
            Direct(
                sems,
                x_peers,
                lambda k: part.at[lax.rem(seq + k + 1, 4), half],
                lambda k: landing.at[k, half],
            )
            for half in (low, high)
        ]

    def gather_rows(place_of):
        return [gather(x_peers, place_of.at[seq, half], place_of.at[seq, half]) for half in (low, high)]

    def exchange(turn, value, finish, place_of, during=None, between=None):
        s.part[turn % 2] = value.astype(BF16).reshape(4, ROWS, D)
        reduces = reduce_rows(turn)
        for ring in reduces:
            ring.start()
        if during is not None:
            during()
        gathers = gather_rows(place_of) if place_of is not None else []
        for index, half in enumerate((low, high)):
            reduces[index].arrive()
            total = s.part[turn % 2, seq, half].astype(F32)
            for k in range(3):
                total = total + s.landing[turn % 2, k, half].astype(F32)
            finish(total, half)
            if gathers:
                gathers[index].start()
        if between is not None:
            between()
        for ring in gathers:
            ring.arrive()
        for ring in reduces + gathers:
            ring.sent()

    def sum_over(ring, target, landing):
        ring.arrive()
        add_into(target, [landing.at[k] for k in range(3)])

    def scatter(peers, me, part, landing):
        return Direct(
            sems, peers, lambda k: part(lax.rem(me + k + 1, 4)), lambda k: landing.at[k]
        )

    class Gradients:
        def __init__(self, layer):
            self.layer = layer
            dq, df, do = s.dwq.at[layer], s.dwf.at[layer], s.dwo.at[layer]
            self.dq, self.df, self.do = dq, df, do
            self.pair_f = [
                sems.copy(
                    df.at[:, :, pl.ds(UNIT * kind, UNIT)],
                    s.wf.at[layer, :, :, pl.ds(UNIT * kind, UNIT)],
                    partner,
                )
                for kind in range(3)
            ]
            self.pair_q = sems.copy(dq, s.wq.at[layer], partner)
            self.pair_o = sems.copy(do, s.wo.at[layer], partner)
            self.f_one = [
                scatter(z_peers, z, lambda j: df.at[j, :, f_low], s.g_in),
                scatter(y_peers, y, lambda j: df.at[:, j, f_high], s.d_in),
            ]
            self.f_two = [
                scatter(y_peers, y, lambda j: df.at[z, j, f_low], s.g_in2),
                scatter(z_peers, z, lambda j: df.at[j, y, f_high], s.d_in2),
            ]
            self.q_one = [
                scatter(z_peers, z, lambda j: dq.at[j, :, low], s.q_in.at[:, :, low]),
                scatter(y_peers, y, lambda j: dq.at[:, j, high], s.q_in.at[:, :, high]),
            ]
            self.q_two = [
                scatter(y_peers, y, lambda j: dq.at[z, j, low], s.q_in2.at[:, low]),
                scatter(z_peers, z, lambda j: dq.at[j, y, high], s.q_in2.at[:, high]),
            ]
            self.o_one = scatter(y_peers, y, lambda j: do.at[j], s.o_in)
            self.o_two = [
                sems.copy(do.at[y], s.o_in2.at[k], along_z(z, y, 3 - k)) for k in range(3)
            ]
            self.q_three = gather(x_peers, dq.at[z, y], q_out.at[seq])
            self.f_three = gather(x_peers, df.at[z, y], f_out.at[seq])
            self.o_three = [sems.copy(do.at[y], o_out, peer) for peer in x_peers]
            self.keep = [
                pltpu.make_async_copy(dq.at[z, y], q_out.at[seq], local.at[6]),
                pltpu.make_async_copy(df.at[z, y], f_out.at[seq], local.at[7]),
                pltpu.make_async_copy(do.at[y], o_out, local.at[8]),
            ]

        def free(self, index):
            @owner(self.layer)
            def _():
                pl.semaphore_signal(credit.at[index], inc=1, device_id=partner, device_id_type=MESH)

        def taken(self, index):
            @other(self.layer)
            def _():
                pl.semaphore_wait(credit.at[index], 1)

        def hand(self, *copies):
            @other(self.layer)
            def _():
                for copy in copies:
                    copy.start()

        def f_first(self):
            @owner(self.layer)
            def _():
                for copy in self.pair_f:
                    copy.wait_recv()
                add_into(self.df, [s.wf.at[self.layer]])
                for ring in self.f_one:
                    ring.start()

        def q_first(self):
            @owner(self.layer)
            def _():
                self.pair_q.wait_recv()
                add_into(self.dq, [s.wq.at[self.layer]])
                for ring in self.q_one:
                    ring.start()
                self.pair_o.wait_recv()
                add_into(self.do, [s.wo.at[self.layer]])
                self.o_one.start()

        def f_second(self):
            @owner(self.layer)
            def _():
                sum_over(self.f_one[0], self.df.at[z, :, f_low], s.g_in)
                self.f_two[0].start()
                sum_over(self.f_one[1], self.df.at[:, y, f_high], s.d_in)
                self.f_two[1].start()

        def q_second(self):
            @owner(self.layer)
            def _():
                sum_over(self.q_one[0], self.dq.at[z, :, low], s.q_in.at[:, :, low])
                self.q_two[0].start()
                sum_over(self.q_one[1], self.dq.at[:, y, high], s.q_in.at[:, :, high])
                self.q_two[1].start()
                sum_over(self.o_one, self.do.at[y], s.o_in)
                for k in range(3):

                    @pl.when(lax.rem(z + 3 - k, 4) == seq)
                    def _():
                        self.o_two[k].start()

        def f_third(self):
            @owner(self.layer)
            def _():
                sum_over(self.f_two[0], self.df.at[z, y, f_low], s.g_in2)
                sum_over(self.f_two[1], self.df.at[z, y, f_high], s.d_in2)
                self.f_three.start()
                self.keep[1].start()

        def q_third(self):
            @owner(self.layer)
            def _():
                sum_over(self.q_two[0], self.dq.at[z, y, low], s.q_in2.at[:, low])
                sum_over(self.q_two[1], self.dq.at[z, y, high], s.q_in2.at[:, high])
                self.q_three.start()
                self.keep[0].start()

                @pl.when(z == seq)
                def _():
                    for k in range(3):
                        self.o_two[k].wait_recv()
                    add_into(self.do.at[y], [s.o_in2.at[k] for k in range(3)])
                    for copy in self.o_three:
                        copy.start()
                    self.keep[2].start()

        def end(self):
            @owner(self.layer)
            def _():
                self.f_three.arrive()
                self.q_three.arrive()
                for ring in self.f_one + self.f_two + self.q_one + self.q_two:
                    ring.sent()
                for ring in (self.o_one, self.q_three, self.f_three):
                    ring.sent()
                for k in range(3):

                    @pl.when(lax.rem(z + 3 - k, 4) == seq)
                    def _():
                        self.o_two[k].wait_send()

                self.keep[0].wait()
                self.keep[1].wait()

                @pl.when(z == seq)
                def _():
                    self.keep[2].wait()
                    for copy in self.o_three:
                        copy.wait_send()

                for k in range(3):

                    @pl.when(lax.rem(z + k + 1, 4) == seq)
                    def _():
                        self.o_three[k].wait_recv()

            @other(self.layer)
            def _():
                for copy in self.pair_f + [self.pair_q, self.pair_o]:
                    copy.wait_send()

    grads = [Gradients(0), Gradients(1)]

    logit_columns = dot(w_beta[0], pick_columns(8, 2 * seq), TN)
    wq[z, y, :, 768:QW] = logit_columns.astype(BF16)
    for copy in own_q:
        copy.wait()

    @owner(0)
    def _():
        weights_first()

    own_small = s.small.at[core]
    own_small[0:1, :] = norm_in[...]
    own_small[1:2, :] = norm_ffn[...]
    own_small[2:3, 0:HD] = norm_head[...]
    for tap in range(4):
        for part in range(3):
            row = 4 + 3 * tap + part
            own_small[row : row + 1, 0:256] = conv_w[
                0, part, tap : tap + 1, pl.ds(pl.multiple_of(256 * seq, 256), 256)
            ]
    pair_small.start()
    mine_of = pick(UNIT, 176, UNIT * seq)
    for kind in range(2):
        wf[z, y, UNIT * kind : UNIT * kind + UNIT, :] = dot(mine_of, w_ffn[0, kind], NN).astype(BF16)
    wf[z, y, 2 * UNIT : 3 * UNIT, :] = dot(mine_of, w_down[0], NN).astype(BF16)

    @owner(0)
    def _():
        weights_second()

    own_x.wait()
    x_gather.arrive()
    pair_small.wait_recv()
    norm_rows(s, 0)

    @owner(0)
    def _():
        weights_third()

    @owner(1)
    def _():
        pair_arrived(pair_q)
        pair_arrived([pair_o])
        weights_first()

    cot_gather.start()
    for layer in (0, 1):
        if layer == 1:
            norm_rows(s, 1)

            @owner(0)
            def _():
                pair_arrived(pair_q)
                pair_arrived([pair_o])

        def midway():
            if layer == 0:

                @owner(0)
                def _():
                    weights_next()

        mixer_forward(s, *perms, layer, midway)
        if layer == 0:

            @owner(1)
            def _():
                weights_second()

        def spread_on():
            if layer == 0:

                @owner(0)
                def _():
                    weights_fourth()
            else:

                @owner(1)
                def _():
                    weights_fourth()

        def attended(total, half):
            residual = s.rows_in[layer, seq, half].astype(F32) + total
            s.residual[layer, half] = residual
            s.normed_ffn[layer, seq, half] = (
                residual * rms(residual) * s.small[layer, 1:2, :]
            ).astype(BF16)

        exchange(
            2 * layer,
            dot(s.att[layer], s.wo[layer].reshape(256, D), NN),
            attended,
            s.normed_ffn.at[layer],
            spread_on,
        )

        @other(layer)
        def _():
            pair_arrived(pair_f)

        def hand_on():
            if layer == 0:

                @owner(1)
                def _():
                    weights_third()

        def handed():
            if layer == 0:

                @owner(1)
                def _():
                    weights_next()

        def leave(total, half):
            out = (s.residual[layer, half] + total).astype(BF16)
            if layer == 0:
                s.rows_in[1, seq, half] = out
            else:
                s.final[0, half] = out

        exchange(
            2 * layer + 1,
            ffn_forward(s, layer),
            leave,
            s.rows_in.at[1] if layer == 0 else None,
            hand_on,
            handed,
        )

    weights_sent()
    own_cot.wait()
    cot_gather.arrive()
    for layer in (1, 0):
        mine = grads[layer]

        def weights_of_ffn():
            mine.free(0)
            for kind in range(3):
                ffn_weights(s, layer, kind)
                if kind == 0:
                    mine.taken(0)
                mine.hand(mine.pair_f[kind])
            if layer == 0:
                grads[1].q_first()

        def back_ffn(total, half):
            value = s.residual[layer, half]
            grad, gain = rms_back(total, value, rms(value), s.small[layer, 1:2, :])
            grad = s.outer[layer, seq, half].astype(F32) + grad
            s.grad_residual[half] = grad
            s.branch[layer, seq, half] = grad.astype(BF16)
            gains.append(gain)

        def after_ffn():
            if layer == 0:
                grads[1].f_second()
                mine.f_first()

        gains = []
        exchange(
            8 - 2 * layer - 2,
            ffn_backward(s, layer),
            back_ffn,
            s.branch.at[layer],
            weights_of_ffn,
            after_ffn,
        )
        gain_ffn = gains[0] + gains[1]
        mixer_backward(s, *perms, layer)
        s.dsmall[layer, 1:2, :] = gain_ffn

        def weights_of_mixer():
            mine.free(1)
            mixer_weights(s, layer)
            mine.taken(1)
            mine.hand(mine.pair_q, mine.pair_o)
            if layer == 1:
                mine.f_first()
            else:
                grads[1].q_second()
                grads[1].f_third()

        def back_in(total, half):
            value = s.rows_in[layer, seq, half].astype(F32)
            grad, gain = rms_back(total, value, rms(value), s.small[layer, 0:1, :])
            grad = (s.grad_residual[half] + grad).astype(BF16)
            gains.append(gain)
            if layer == 1:
                s.outer[0, seq, half] = grad
            else:
                s.final[1, half] = grad

        gains = []
        exchange(
            8 - 2 * layer - 1,
            dot(s.grad_proj[...], s.wq[layer].reshape(D, QW), NT),
            back_in,
            s.outer.at[0] if layer == 1 else None,
            weights_of_mixer,
        )
        s.dsmall[layer, 0:1, :] = gains[0] + gains[1]

    rows_copies = [
        pltpu.make_async_copy(s.final.at[k], rows_out.at[k, core], local.at[9 + k]) for k in (0, 1)
    ]
    pair_rows = [sems.copy(s.final.at[k], rows_out.at[k, core], partner) for k in (0, 1)]
    pair_gains = sems.copy(s.dsmall.at[1 - core], s.small_in.at[0], partner)
    pair_gains.start()
    for copy in rows_copies + pair_rows:
        copy.start()
    grads[0].q_first()
    pair_gains.wait_recv()
    s.small_sum[0] = s.dsmall[core] + s.small_in[0]
    small_y = Direct(sems, y_peers, lambda k: s.small_sum.at[0], lambda k: s.small_in.at[1 + k])
    small_z = Direct(sems, z_peers, lambda k: s.small_sum.at[1], lambda k: s.small_in.at[4 + k])
    small_x = gather(x_peers, s.small_sum.at[2], small_out.at[seq])
    small_y.start()
    grads[0].f_second()
    grads[1].q_third()
    small_y.arrive()
    s.small_sum[1] = s.small_sum[0] + s.small_in[1] + s.small_in[2] + s.small_in[3]
    small_z.start()
    grads[0].q_second()
    small_z.arrive()
    s.small_sum[2] = s.small_sum[1] + s.small_in[4] + s.small_in[5] + s.small_in[6]
    small_keep = pltpu.make_async_copy(s.small_sum.at[2], small_out.at[seq], local.at[11])
    small_x.start()
    small_keep.start()
    grads[0].f_third()
    grads[0].q_third()
    grads[1].end()
    grads[0].end()
    small_x.arrive()
    for copy in pair_rows:
        copy.wait()
    pair_gains.wait_send()
    for ring in (small_y, small_z, small_x, x_gather, cot_gather):
        ring.sent()
    pair_small.wait_send()
    for copy in rows_copies + [small_keep]:
        copy.wait()


def whole_program(*operands):
    return pl.pallas_call(
        program_kernel,
        out_shape=[
            sds((2, 2, ROWS, D), BF16),
            sds((4, 16, D), F32),
            sds((4, 64, QW), BF16),
            sds((4, 3 * UNIT, D), BF16),
            sds((64, D), BF16),
        ],
        in_specs=[ANY, ANY, VMEM, SMEM, VMEM, ANY, VMEM, VMEM, VMEM, ANY, VMEM, VMEM, VMEM],
        out_specs=[ANY] * 5,
        scratch_shapes=[pltpu.VMEM(shape, dtype) for _, shape, dtype in SCRATCH]
        + [
            pltpu.SemaphoreType.DMA((N_SEM,)),
            pltpu.SemaphoreType.DMA((N_SEM,)),
            pltpu.SemaphoreType.DMA((12,)),
            pltpu.SemaphoreType.REGULAR((2,)),
        ],
        compiler_params=pltpu.CompilerParams(
            collective_id=1, has_side_effects=True, vmem_limit_bytes=VMEM_BYTES
        ),
        name="layers",
    )(*operands)


def finish_kernel(
    rows,
    small,
    q,
    f,
    o,
    block_out,
    input_grad,
    grad_norm_in,
    grad_qkv,
    grad_beta,
    grad_conv,
    grad_norm_head,
    grad_out,
    grad_norm_ffn,
    grad_ffn,
    grad_down,
):
    block_out[:, 0] = rows[0]
    input_grad[:, 0] = rows[1]
    total = small[0] + small[1] + small[2] + small[3]
    grad_norm_in[...] = total[0:1]
    grad_norm_ffn[...] = total[1:2]
    grad_norm_head[...] = total[2:3, 0:HD]
    grad_out[0] = o[...].astype(F32)
    beta = jnp.zeros((8, 64), F32)
    for seq in range(4):
        lanes = slice(256 * seq, 256 * seq + 256)
        for tap in range(4):
            for part in range(3):
                row = 4 + 3 * tap + part
                grad_conv[0, part, tap : tap + 1, lanes] = small[seq, row : row + 1, 0:256]
        for part in range(3):
            grad_qkv[0, :, D * part + 256 * seq : D * part + 256 * seq + 256] = q[
                seq, :, 256 * part : 256 * part + 256
            ].astype(F32)
        beta = beta + dot(pick_columns(8, 2 * seq), q[seq, :, 768:QW], NT)
    grad_beta[0] = beta
    for kind in range(3):
        whole = f[:, UNIT * kind : UNIT * kind + UNIT, :].reshape(4 * UNIT, D)[:176].astype(F32)
        if kind < 2:
            grad_ffn[0, kind] = whole
        else:
            grad_down[0] = whole


def finish(*operands):
    shapes = [
        ((2, 1, ROWS, D), BF16),
        ((2, 1, ROWS, D), BF16),
        ((1, D), F32),
        ((1, 64, 3 * D), F32),
        ((1, H, 64), F32),
        ((1, 3, 4, D), F32),
        ((1, HD), F32),
        ((1, 64, D), F32),
        ((1, D), F32),
        ((1, 2, 176, D), F32),
        ((1, 176, D), F32),
    ]
    return pl.pallas_call(
        finish_kernel,
        out_shape=[sds(*shape) for shape in shapes],
        in_specs=[VMEM] * 5,
        out_specs=[VMEM] * 11,
        compiler_params=pltpu.CompilerParams(vmem_limit_bytes=VMEM_BYTES),
        name="finish",
    )(*operands)


def local(
    block_in,
    cotangent,
    perm_rows,
    doc_lengths,
    norm_in,
    w_qkv,
    w_beta,
    conv_w,
    norm_head,
    w_out,
    norm_ffn,
    w_ffn,
    w_down,
):
    results = list(finish(
        *whole_program(
            block_in,
            cotangent,
            perm_rows,
            doc_lengths,
            norm_in,
            w_qkv,
            jnp.swapaxes(w_beta, 1, 2),
            jnp.swapaxes(conv_w, 1, 2),
            norm_head,
            w_out,
            norm_ffn,
            jnp.swapaxes(w_ffn, 2, 3),
            w_down,
        )
    ))
    results[4] = jnp.swapaxes(results[4], 1, 2)
    results[5] = jnp.swapaxes(results[5], 1, 2)
    results[9] = jnp.swapaxes(results[9], 2, 3)
    return tuple(results)


def solution(mesh):
    placed = (
        P(None, "fsdp", "seq", None),
        P(None, "fsdp", "seq", None),
        P(None, "fsdp", None),
        P(None, "fsdp", None),
        P("section", None),
        P("section", "fsdp", None),
        P("section", "fsdp", None),
        P("section", None, None, None),
        P("section", None),
        P("section", "fsdp", None),
        P("section", None),
        P("section", None, None, "fsdp"),
        P("section", "fsdp", None),
    )
    return jax.shard_map(
        local,
        mesh=mesh,
        in_specs=placed,
        out_specs=(
            P(None, "fsdp", "seq", None),
            P(None, "fsdp", "seq", None),
            P("section", None),
            P("section", "fsdp", None),
            P("section", "fsdp", None),
            P("section", None, None, None),
            P("section", None),
            P("section", "fsdp", None),
            P("section", None),
            P("section", None, None, "fsdp"),
            P("section", "fsdp", None),
        ),
        check_vma=False,
    )
```

```python
import functools

import jax
import jax.numpy as jnp
from jax import lax
from jax.experimental import pallas as pl
from jax.experimental.pallas import tpu as pltpu
from jax.sharding import PartitionSpec as P

D = 1024
H = 8
HD = 128
PACK = 256
ROWS = 64
UNIT = 48
QW = 896
MESH = pl.DeviceIdType.MESH
F32, BF16 = jnp.float32, jnp.bfloat16
VMEM = pl.BlockSpec(memory_space=pltpu.VMEM)
SMEM = pl.BlockSpec(memory_space=pltpu.SMEM)
ANY = pl.BlockSpec(memory_space=pl.ANY)
VMEM_BYTES = 60 * 1024 * 1024


def sds(shape, dtype):
    return jax.ShapeDtypeStruct(shape, dtype)


def dot(left, right, dims):
    return lax.dot_general(left, right, (dims, ((), ())), preferred_element_type=F32)


NN = ((1,), (0,))
NT = ((1,), (1,))
TN = ((0,), (0,))


def halves(value):
    high = value.astype(BF16)
    return high, (value - high.astype(F32)).astype(BF16)


def dot3(left, right, dims):
    return dot(left[0], right[0], dims) + (
        dot(left[0], right[1], dims) + dot(left[1], right[0], dims)
    )


def place():
    fsdp = lax.axis_index("fsdp")
    return (
        lax.axis_index("section"),
        lax.axis_index("seq"),
        lax.div(fsdp, 4),
        lax.rem(fsdp, 4),
    )


def along_x(seq, step):
    return {"seq": lax.rem(seq + step, 4)}


def along_y(z, y, step):
    return {"fsdp": z * 4 + lax.rem(y + step, 4)}


def along_z(z, y, step):
    return {"fsdp": lax.rem(z + step, 4) * 4 + y}


def greet(peers):
    barrier = pltpu.get_barrier_semaphore()
    for peer in peers:
        pl.semaphore_signal(barrier, inc=1, device_id=peer, device_id_type=MESH)
    pl.semaphore_wait(barrier, len(peers))


def remote(source, target, send, recv, peer):
    return pltpu.make_async_remote_copy(
        src_ref=source,
        dst_ref=target,
        send_sem=send,
        recv_sem=recv,
        device_id=peer,
        device_id_type=MESH,
    )


CUT = 80


class Direct:
    def __init__(self, sems, peers, source, target):
        self.copies = [sems.copy(source(k), target(k), peer) for k, peer in enumerate(peers)]

    def start(self):
        for copy in self.copies:
            copy.start()

    def arrive(self):
        for copy in self.copies:
            copy.wait_recv()

    def sent(self):
        for copy in self.copies:
            copy.wait_send()


class Semaphores:
    def __init__(self, send, recv):
        self.send, self.recv, self.used = send, recv, 0

    def copy(self, source, target, peer):
        index = self.used
        self.used += 1
        return remote(source, target, self.send.at[index], self.recv.at[index], peer)


def add_into(target, others):
    shape = target.shape
    if len(shape) == 2:
        value = target[...].astype(F32)
        for other in others:
            value = value + other[...].astype(F32)
        target[...] = value.astype(target.dtype)
        return

    def body(index, carry):
        add_into(target.at[index], [other.at[index] for other in others])
        return carry

    lax.fori_loop(0, shape[0], body, 0)


def rms(value):
    return lax.rsqrt(jnp.mean(value * value, axis=-1, keepdims=True) + 1e-06)


def rms_back(grad, value, scale, gain):
    weighted = grad * gain
    inner = jnp.mean(weighted * value, axis=-1, keepdims=True)
    return (
        scale * weighted - value * (scale * scale * scale) * inner,
        jnp.sum(grad * value * scale, axis=0, keepdims=True),
    )


def shifted(value, step):
    rows = value.shape[0]
    filler = jnp.zeros((abs(step), value.shape[1]), value.dtype)
    if step > 0:
        return jnp.concatenate([filler, value[: rows - step]], axis=0)
    return jnp.concatenate([value[-step:], filler], axis=0)


def doc_places(doc_len):
    col = lax.broadcasted_iota(jnp.int32, (PACK, 1), 0)
    row = lax.broadcasted_iota(jnp.int32, (1, PACK), 1)
    start_col, start_row = jnp.zeros_like(col), jnp.zeros_like(row)
    end = 0
    for doc in range(4):
        end = end + doc_len[doc]
        start_col = jnp.where(col >= end, end, start_col)
        start_row = jnp.where(row >= end, end, start_row)
    return col - start_col, start_col == start_row


def one_hot(column, row):
    return (column == row).astype(F32).astype(BF16)


def sigmoid(value):
    return 1.0 / (1.0 + jnp.exp(-value))


def conv_taps(small_ref, layer, tap, part):
    return small_ref[layer, 4 + tap * 3 + part : 5 + tap * 3 + part, 0:256]


def conv_part(series, small_ref, layer, part, offset):
    total = series * conv_taps(small_ref, layer, 0, part)
    for tap in range(1, 4):
        moved = jnp.where(offset >= tap, shifted(series, tap), 0.0)
        total = total + moved * conv_taps(small_ref, layer, tap, part)
    return total


def unit(value):
    scale = lax.rsqrt(jnp.sum(value * value, axis=-1, keepdims=True) + 1e-06)
    return value * scale, scale


def inverse(system):
    col = lax.broadcasted_iota(jnp.int32, (PACK, PACK), 0)
    row = lax.broadcasted_iota(jnp.int32, (PACK, PACK), 1)
    apart = col ^ row
    identity = jnp.where(col == row, 1.0, 0.0)
    rough = (identity - jnp.where(apart == 1, system, 0.0)).astype(BF16)
    for level in range(1, 8):
        corner = jnp.where((apart >> level) == 1, system, 0.0).astype(BF16)
        inner = dot(corner, rough, NN).astype(BF16)
        rough = rough - dot(rough, inner, NN).astype(BF16)
    high, low = halves(system)
    left = identity - rough.astype(F32) - (dot(high, rough, NN) + dot(low, rough, NN))
    return rough.astype(F32) + dot(rough, left.astype(BF16), NN)


def masks():
    col = lax.broadcasted_iota(jnp.int32, (PACK, PACK), 0)
    row = lax.broadcasted_iota(jnp.int32, (PACK, PACK), 1)
    return col, row


def to_places(perm_row):
    return one_hot(lax.broadcasted_iota(jnp.int32, (PACK, 1), 0), perm_row)


def norm_rows(s, layer, half):
    x = s.rows_in[layer, :, half, :].reshape(PACK // 2, D).astype(F32)
    x = (x * rms(x) * s.small[layer, 0:1, :]).astype(BF16)
    s.normed[layer, :, half, :] = x.reshape(4, ROWS // 2, D)


def project(s, layer, half):
    normed = s.normed[layer, :, half, :].reshape(PACK // 2, D)
    proj = dot(normed, s.wq[layer].reshape(D, QW), NN).astype(BF16)
    s.stored[:, half, :] = proj.reshape(4, ROWS // 2, QW)


def mixer_forward(s, perm_row, doc_len, layer):
    small = s.small
    places = to_places(perm_row)
    proj = dot(places, s.stored[...].reshape(PACK, QW), NN)
    s.proj[layer] = proj.astype(BF16)
    offset, same = doc_places(doc_len)
    activated = []
    for kind in range(3):
        pre = conv_part(proj[:, 256 * kind : 256 * kind + 256], small, layer, kind, offset)
        activated.append(pre * sigmoid(pre))
    col, row = masks()
    strict = same & (col > row)
    tri = same & (col >= row)
    heads = []
    for head in range(2):
        lanes = slice(128 * head, 128 * head + 128)
        query = halves(unit(activated[0][:, lanes])[0] * HD**-0.5)
        key = halves(unit(activated[1][:, lanes])[0])
        value = activated[2][:, lanes]
        strength = sigmoid(proj[:, 768 + head : 769 + head])
        system = jnp.where(strict, strength * dot3(key, key, NT), 0.0)
        solved = inverse(system)
        s.solved[layer, head] = solved
        fresh = dot3(halves(solved), halves(strength * value), NN)
        s.fresh[layer, head] = fresh
        scores = jnp.where(tri, dot3(query, key, NT), 0.0)
        produced = dot3(halves(scores), halves(fresh), NN)
        s.produced[layer, head] = produced
        scale = lax.rsqrt(jnp.mean(produced * produced, axis=-1, keepdims=True) + 1e-05)
        heads.append((produced * scale * small[layer, 2:3, 0:128]).astype(BF16))
    mixed = jnp.concatenate(heads, axis=1)
    s.att[layer] = dot(places, mixed, TN).astype(BF16).reshape(4, ROWS, 256)


def mixer_backward(s, perm_row, doc_len, layer):
    small = s.small
    grad = s.branch[layer].reshape(PACK, D)
    grad_att = dot(grad, s.wo[layer].reshape(256, D), NT).astype(BF16)
    places = to_places(perm_row)
    grad_att = dot(places, grad_att, NN)
    proj = s.proj[layer].astype(F32)
    offset, same = doc_places(doc_len)
    pres, gates = [], []
    for kind in range(3):
        pre = conv_part(proj[:, 256 * kind : 256 * kind + 256], small, layer, kind, offset)
        pres.append(pre)
        gates.append(sigmoid(pre))
    col, row = masks()
    strict = same & (col > row)
    tri = same & (col >= row)
    gain = small[layer, 2:3, 0:128]
    gain_grad = jnp.zeros((1, HD), F32)
    grads = [[], [], []]
    logit_grads = []
    for head in range(2):
        lanes = slice(128 * head, 128 * head + 128)
        act_q, act_k, value = [(pre * gate)[:, lanes] for pre, gate in zip(pres, gates)]
        query_f, scale_q = unit(act_q)
        key_f, scale_k = unit(act_k)
        query, key = halves(query_f * HD**-0.5), halves(key_f)
        strength = sigmoid(proj[:, 768 + head : 769 + head])
        produced = s.produced[layer, head]
        scale = lax.rsqrt(jnp.mean(produced * produced, axis=-1, keepdims=True) + 1e-05)
        given = grad_att[:, lanes]
        weighted = given * gain
        inner = jnp.mean(weighted * produced, axis=-1, keepdims=True)
        grad_o = halves(scale * weighted - produced * (scale * scale * scale) * inner)
        gain_grad = gain_grad + jnp.sum(given * produced * scale, axis=0, keepdims=True)
        fresh = halves(s.fresh[layer, head])
        gram = dot3(key, key, NT)
        scores = halves(jnp.where(tri, dot3(query, key, NT), 0.0))
        grad_scores = halves(jnp.where(tri, dot3(grad_o, fresh, NT), 0.0))
        grad_fresh = halves(dot3(scores, grad_o, TN))
        grad_source = dot3(halves(s.solved[layer, head]), grad_fresh, TN)
        grad_system = jnp.where(strict, -dot3(halves(grad_source), fresh, NT), 0.0)
        grad_gram = halves(strength * grad_system)
        grad_query = dot3(grad_scores, key, NN)
        grad_key = (
            dot3(grad_scores, query, TN) + dot3(grad_gram, key, NN) + dot3(grad_gram, key, TN)
        )
        grad_value = strength * grad_source
        grad_strength = jnp.sum(grad_source * value, axis=-1, keepdims=True) + jnp.sum(
            grad_system * gram, axis=-1, keepdims=True
        )
        logit_grads.append(grad_strength * strength * (1.0 - strength))
        grads[0].append(
            HD**-0.5
            * (
                scale_q * grad_query
                - act_q
                * (scale_q * scale_q * scale_q)
                * jnp.sum(act_q * grad_query, axis=-1, keepdims=True)
            )
        )
        grads[1].append(
            scale_k * grad_key
            - act_k
            * (scale_k * scale_k * scale_k)
            * jnp.sum(act_k * grad_key, axis=-1, keepdims=True)
        )
        grads[2].append(grad_value)
    dsmall = s.dsmall.at[layer]
    dsmall[...] = jnp.zeros((16, D), F32)
    dsmall[2:3, 0:128] = gain_grad
    pieces = []
    for kind in range(3):
        pre, gate = pres[kind], gates[kind]
        grad_pre = jnp.concatenate(grads[kind], axis=1) * gate * (1.0 + pre * (1.0 - gate))
        series = proj[:, 256 * kind : 256 * kind + 256]
        total = grad_pre * conv_taps(small, layer, 0, kind)
        dsmall[4 + kind : 5 + kind, 0:256] = jnp.sum(grad_pre * series, axis=0, keepdims=True)
        for tap in range(1, 4):
            kept = jnp.where(offset >= tap, grad_pre, 0.0)
            total = total + shifted(kept, -tap) * conv_taps(small, layer, tap, kind)
            dsmall[4 + tap * 3 + kind : 5 + tap * 3 + kind, 0:256] = jnp.sum(
                kept * shifted(series, tap), axis=0, keepdims=True
            )
        pieces.append(total.astype(BF16))
    lane = lax.broadcasted_iota(jnp.int32, (1, 128), 1)
    pieces.append(
        jnp.where(lane == 0, logit_grads[0], jnp.where(lane == 1, logit_grads[1], 0.0)).astype(BF16)
    )
    grad_proj = jnp.concatenate(pieces, axis=1)
    s.grad_proj[...] = dot(places, grad_proj, TN).astype(BF16).reshape(4, ROWS, QW)


def units(weights, layer, kind):
    return weights[layer, :, :, UNIT * kind : UNIT * kind + UNIT, :].reshape(768, D)


def half_of(ref, layer, half):
    return ref[layer, :, half, :].reshape(PACK // 2, ref.shape[-1])


def put_half(ref, layer, half, value):
    ref[layer, :, half, :] = value.reshape(4, ROWS // 2, ref.shape[-1])


def ffn_forward(s, layer, half):
    normed = half_of(s.normed_ffn, layer, half)
    gate = dot(normed, units(s.wf, layer, 0), NT)
    up = dot(normed, units(s.wf, layer, 1), NT)
    put_half(s.gate, layer, half, gate)
    put_half(s.up, layer, half, up)
    hidden = (gate * sigmoid(gate) * up).astype(BF16)
    return dot(hidden, units(s.wf, layer, 2), NN)


def ffn_backward(s, layer, half):
    grad = half_of(s.outer, layer, half)
    gate, up = half_of(s.gate, layer, half), half_of(s.up, layer, half)
    sig = sigmoid(gate)
    grad_hidden = dot(grad, units(s.wf, layer, 2), NT)
    grad_gate = (grad_hidden * up * sig * (1.0 + gate * (1.0 - sig))).astype(BF16)
    grad_up = (grad_hidden * gate * sig).astype(BF16)
    put_half(s.unit_grads, 0, half, grad_gate)
    put_half(s.unit_grads, 1, half, grad_up)
    put_half(s.unit_grads, 2, half, (gate * sig * up).astype(BF16))
    return dot(grad_gate, units(s.wf, layer, 0), NN) + dot(grad_up, units(s.wf, layer, 1), NN)


def ffn_weights(s, layer, kind):
    right = (s.outer if kind == 2 else s.normed_ffn)[layer].reshape(PACK, D)
    s.dwf[layer, :, :, UNIT * kind : UNIT * kind + UNIT, :] = (
        dot(s.unit_grads[kind].reshape(PACK, 768), right, TN).astype(BF16).reshape(4, 4, UNIT, D)
    )


def mixer_weights(s, layer):
    s.dwo[layer] = (
        dot(s.att[layer].reshape(PACK, 256), s.branch[layer].reshape(PACK, D), TN).astype(BF16).reshape(4, 64, D)
    )
    s.dwq[layer] = (
        dot(s.normed[layer].reshape(PACK, D), s.grad_proj[...].reshape(PACK, QW), TN)
        .astype(BF16)
        .reshape(4, 4, 64, QW)
    )


SCRATCH = [
    ("rows_in", (2, 4, ROWS, D), BF16),
    ("outer", (2, 4, ROWS, D), BF16),
    ("normed_ffn", (2, 4, ROWS, D), BF16),
    ("branch", (2, 4, ROWS, D), BF16),
    ("small", (2, 16, D), F32),
    ("own_q", (64, QW), BF16),
    ("own_f", (3 * UNIT, D), BF16),
    ("wq", (2, 4, 4, 64, QW), BF16),
    ("wf", (2, 4, 4, 3 * UNIT, D), BF16),
    ("wo", (2, 4, 64, D), BF16),
    ("dwq", (2, 4, 4, 64, QW), BF16),
    ("dwf", (2, 4, 4, 3 * UNIT, D), BF16),
    ("dwo", (2, 4, 64, D), BF16),
    ("normed", (2, 4, ROWS, D), BF16),
    ("stored", (4, ROWS, QW), BF16),
    ("proj", (2, PACK, QW), BF16),
    ("solved", (2, 2, PACK, PACK), F32),
    ("fresh", (2, 2, PACK, HD), F32),
    ("produced", (2, 2, PACK, HD), F32),
    ("att", (2, 4, ROWS, 256), BF16),
    ("gate", (2, 4, ROWS, 768), F32),
    ("up", (2, 4, ROWS, 768), F32),
    ("unit_grads", (3, 4, ROWS, 768), BF16),
    ("grad_proj", (4, ROWS, QW), BF16),
    ("residual", (2, ROWS, D), F32),
    ("grad_residual", (ROWS, D), F32),
    ("part", (2, 4, ROWS, D), BF16),
    ("landing", (2, 3, ROWS, D), BF16),
    ("final", (2, ROWS, D), BF16),
    ("dsmall", (2, 16, D), F32),
    ("small_sum", (3, 16, D), F32),
    ("small_in", (7, 16, D), F32),
    ("q_in", (2, 3, 4, 32, QW), BF16),
    ("g_in", (3, 4, CUT, D), BF16),
    ("o_in", (2, 3, 64, D), BF16),
    ("q_in2", (3, 32, QW), BF16),
    ("g_in2", (3, CUT, D), BF16),
    ("o_in2", (3, 64, D), BF16),
]
N_SEM = 400


class Refs:
    pass


def pick(rows, columns, first):
    row = lax.broadcasted_iota(jnp.int32, (rows, columns), 0)
    column = lax.broadcasted_iota(jnp.int32, (rows, columns), 1)
    return one_hot(column, row + first)


def pick_columns(count, first):
    row = lax.broadcasted_iota(jnp.int32, (count, 128), 0)
    column = lax.broadcasted_iota(jnp.int32, (count, 128), 1)
    return ((row == first + column) & (column < 2)).astype(F32).astype(BF16)


def program_kernel(*refs):
    (
        block_in,
        cotangent,
        perm_ref,
        doc_ref,
        norm_in,
        w_qkv,
        w_beta,
        conv_w,
        norm_head,
        w_out,
        norm_ffn,
        w_ffn,
        w_down,
    ) = refs[:13]
    rows_out, small_out, q_out, f_out, o_out = refs[13:18]
    s = Refs()
    for (name, _, _), ref in zip(SCRATCH, refs[18:]):
        setattr(s, name, ref)
    send, recv, local, credit = refs[18 + len(SCRATCH) :]
    sems = Semaphores(send, recv)
    core, seq, z, y = place()
    partner = {"section": 1 - core}
    x_peers = [along_x(seq, k) for k in (1, 2, 3)]
    y_peers = [along_y(z, y, k) for k in (1, 2, 3)]
    z_peers = [along_z(z, y, k) for k in (1, 2, 3)]
    perm_row = perm_ref[core]
    perms = (perm_row, [doc_ref[core, 0, k] for k in range(4)])
    x_ref, cot_ref, o_ref = block_in.at[core, 0], cotangent.at[core, 0], w_out.at[0]

    def gather(peers, source, target):
        return Direct(sems, peers, lambda k: source, lambda k: target)

    low, high = pl.ds(0, 32), pl.ds(32, 32)
    f_low, f_high = pl.ds(0, CUT), pl.ds(CUT, 3 * UNIT - CUT)

    def on_core(which):
        return pl.when(core == which)

    def on(which, peers):
        return [{**peer, "section": which} for peer in peers]

    own_q = [
        pltpu.make_async_copy(
            w_qkv.at[0, :, pl.ds(pl.multiple_of(D * kind + 256 * seq, 256), 256)],
            s.own_q.at[:, pl.ds(256 * kind, 256)],
            local.at[kind],
        )
        for kind in range(3)
    ]
    for copy in own_q:
        copy.start()
    own_x = pltpu.make_async_copy(x_ref, s.rows_in.at[0, seq], local.at[3])
    own_cot = pltpu.make_async_copy(cot_ref, s.outer.at[1, seq], local.at[4])
    own_o = pltpu.make_async_copy(o_ref, s.wo.at[1, y], local.at[5])
    own_x.start()
    own_cot.start()

    greet(
        [partner]
        + [peer for peers in (x_peers, y_peers, z_peers) for c in (0, 1) for peer in on(c, peers)]
    )
    x_gather = gather(x_peers, x_ref, s.rows_in.at[0, seq])
    cot_gather = gather(x_peers, cot_ref, s.outer.at[1, seq])
    pair_small = sems.copy(s.small.at[core], s.small.at[core], partner)
    x_gather.start()

    class Weights:
        def __init__(self, layer):
            self.layer = layer
            wq, wf, wo = s.wq.at[layer], s.wf.at[layer], s.wo.at[layer]
            self.wo = wo
            axes = (y_peers, z_peers)

            def first(source, target, rows):
                return [
                    [
                        sems.copy(source.at[part], target.at[z, y, part], peer)
                        for peer in on(which, axes[which])
                        + ([partner] if which != layer else [])
                    ]
                    for which, part in enumerate(rows)
                ]

            def second(target, rows):
                return [
                    gather(z_peers, target.at[z, :, rows[0]], target.at[z, :, rows[0]]),
                    gather(y_peers, target.at[:, y, rows[1]], target.at[:, y, rows[1]]),
                ]

            def pairs(target, rows):
                pieces = [
                    [target.at[lax.rem(z + 4 - k, 4), :, rows[0]] for k in range(4)],
                    [target.at[:, lax.rem(y + 4 - k, 4), rows[1]] for k in range(4)],
                ]
                return [[sems.copy(piece, piece, partner) for piece in part] for part in pieces]

            q_rows, f_rows = (low, high), (f_low, f_high)
            self.q_one, self.q_two = first(s.own_q, wq, q_rows), second(wq, q_rows)
            self.f_one, self.f_two = first(s.own_f, wf, f_rows), second(wf, f_rows)
            self.pair_q, self.pair_f = pairs(wq, q_rows), pairs(wf, f_rows)
            self.o_one = [sems.copy(o_ref, wo.at[y], peer) for peer in on(1, z_peers)]
            if layer == 0:
                self.o_pair = sems.copy(o_ref, wo.at[y], partner)
            self.o_two = gather(y_peers, wo.at[y], wo.at[y])
            self.pair_o = sems.copy(wo, wo, partner)

        def first_q(self):
            @on_core(self.layer)
            def _():
                for copies in self.q_one:
                    for copy in copies:
                        copy.start()

        def first_f(self):
            @on_core(self.layer)
            def _():
                @pl.when(z == seq)
                def _():
                    for copy in self.o_one:
                        copy.start()
                    if self.layer == 0:
                        self.o_pair.start()
                    else:
                        own_o.start()

                for copies in self.f_one:
                    for copy in copies:
                        copy.start()

        def second_of(self, one, two, pair):
            for which in (0, 1):

                @on_core(which)
                def _():
                    for copy in one[which]:
                        copy.wait_recv()
                    two[which].start()
                    pair[which][0].start()

        def second_q(self):
            self.second_of(self.q_one, self.q_two, self.pair_q)

        def second_f(self):
            self.second_of(self.f_one, self.f_two, self.pair_f)

        def second_o(self):
            @on_core(1)
            def _():
                @pl.when(z == seq)
                def _():
                    if self.layer == 0:
                        self.o_pair.wait_recv()
                    else:
                        own_o.wait()

                for k in range(3):

                    @pl.when(lax.rem(seq + k + 1, 4) == z)
                    def _():
                        self.o_one[k].wait_recv()

                self.o_two.start()

        def third_of(self, two, pair):
            for which in (0, 1):

                @on_core(which)
                def _():
                    for k in range(3):
                        two[which].copies[k].wait_recv()
                        pair[which][k + 1].start()

        def third_q(self):
            self.third_of(self.q_two, self.pair_q)

        def third_f(self):
            self.third_of(self.f_two, self.pair_f)

        def third_o(self):
            @on_core(1)
            def _():
                self.o_two.arrive()
                self.pair_o.start()

        def arrived(self, pair, with_o):
            for which in (0, 1):

                @on_core(1 - which)
                def _():
                    for copy in pair[which]:
                        copy.wait_recv()
                    if with_o and which == 1:
                        self.pair_o.wait_recv()

        def arrived_q(self):
            self.arrived(self.pair_q, True)

        def arrived_f(self):
            self.arrived(self.pair_f, False)

        def sent(self):
            @on_core(self.layer)
            def _():
                for copies in self.q_one + self.f_one:
                    for copy in copies:
                        copy.wait_send()

                @pl.when(z == seq)
                def _():
                    for copy in self.o_one:
                        copy.wait_send()
                    if self.layer == 0:
                        self.o_pair.wait_send()

            for which in (0, 1):

                @on_core(which)
                def _():
                    for ring in (self.q_two[which], self.f_two[which]):
                        ring.sent()
                    for copy in self.pair_q[which] + self.pair_f[which]:
                        copy.wait_send()
                    if which == 1:
                        self.o_two.sent()
                        self.pair_o.wait_send()

    weights = [Weights(0), Weights(1)]

    both_halves = (low, high)

    def start_rows(turn, half, value):
        part, landing = s.part.at[turn % 2], s.landing.at[turn % 2]
        part[:, half, :] = value.astype(BF16).reshape(4, ROWS // 2, D)
        ring = Direct(
            sems,
            x_peers,
            lambda k: part.at[lax.rem(seq + k + 1, 4), half],
            lambda k: landing.at[k, half],
        )
        ring.start()
        return ring

    def rows_total(turn, half, ring):
        ring.arrive()
        total = s.part[turn % 2, seq, half].astype(F32)
        for k in range(3):
            total = total + s.landing[turn % 2, k, half].astype(F32)
        return total

    def send_rows(place_of, half):
        ring = gather(x_peers, place_of.at[seq, half], place_of.at[seq, half])
        ring.start()
        return ring

    def all_sent(rings):
        for ring in rings:
            ring.sent()

    def sum_over(ring, target, landing):
        ring.arrive()
        add_into(target, [landing.at[k] for k in range(3)])

    def scatter(peers, me, part, landing):
        return Direct(
            sems, peers, lambda k: part(lax.rem(me + k + 1, 4)), lambda k: landing.at[k]
        )

    class Gradients:
        def __init__(self, layer):
            self.layer = layer
            dq, df, do = s.dwq.at[layer], s.dwf.at[layer], s.dwo.at[layer]
            lq, lf, lo = s.wq.at[layer], s.wf.at[layer], s.wo.at[layer]
            self.dq, self.df, self.do = dq, df, do
            self.q_in, self.o_in = s.q_in.at[layer], s.o_in.at[layer]
            self.lq, self.lf, self.lo = lq, lf, lo
            self.q_rows, self.f_rows = (low, high), (f_low, f_high)

            def pair_f(first, count):
                rows = pl.ds(first, count)
                return sems.copy(df.at[:, :, rows], lf.at[:, :, rows], partner)

            self.pair_f = [
                [pair_f(0, UNIT), pair_f(UNIT, CUT - UNIT)],
                [pair_f(2 * UNIT, UNIT), pair_f(CUT, 2 * UNIT - CUT)],
            ]
            self.pair_q = [sems.copy(dq.at[:, :, half], lq.at[:, :, half], partner) for half in self.q_rows]
            self.pair_o = sems.copy(do, lo, partner)
            self.f_one = [
                scatter(z_peers, z, lambda j: df.at[j, :, f_low], s.g_in),
                scatter(y_peers, y, lambda j: df.at[:, j, f_high], s.g_in.at[:, :, pl.ds(0, 3 * UNIT - CUT)]),
            ]
            self.f_two = [
                scatter(y_peers, y, lambda j: df.at[z, j, f_low], s.g_in2),
                scatter(z_peers, z, lambda j: df.at[j, y, f_high], s.g_in2.at[:, pl.ds(0, 3 * UNIT - CUT)]),
            ]
            self.q_one = [
                scatter(z_peers, z, lambda j: dq.at[j, :, low], self.q_in),
                scatter(y_peers, y, lambda j: dq.at[:, j, high], self.q_in),
            ]
            self.q_two = [
                scatter(y_peers, y, lambda j: dq.at[z, j, low], s.q_in2),
                scatter(z_peers, z, lambda j: dq.at[j, y, high], s.q_in2),
            ]
            self.o_one = scatter(y_peers, y, lambda j: do.at[j], self.o_in)
            self.o_two = [
                sems.copy(do.at[y], s.o_in2.at[k], along_z(z, y, 3 - k)) for k in range(3)
            ]
            holders = [{**peer, "section": layer} for peer in x_peers]

            def to_holders(which, source, target, index):
                copies = [sems.copy(source, target, peer) for peer in holders]
                if which == layer:
                    return copies, pltpu.make_async_copy(source, target, local.at[index])
                return copies, sems.copy(source, target, partner)

            self.q_three = [
                to_holders(which, dq.at[z, y, half], q_out.at[seq, half], 6)
                for which, half in enumerate(self.q_rows)
            ]
            self.f_three = [
                to_holders(which, df.at[z, y, rows], f_out.at[seq, rows], 7)
                for which, rows in enumerate(self.f_rows)
            ]
            self.o_three = to_holders(1, do.at[y], o_out, 8)

        def free(self, index):
            pl.semaphore_signal(credit.at[index], inc=1, device_id=partner, device_id_type=MESH)

        def taken(self, index):
            pl.semaphore_wait(credit.at[index], 1)

        def hand_f(self, which, index):
            @on_core(1 - which)
            def _():
                self.pair_f[which][index].start()

        def hand_q(self):
            for which in (0, 1):

                @on_core(1 - which)
                def _():
                    self.pair_q[which].start()
                    if which == 1:
                        self.pair_o.start()

        def f_first(self):
            for which, rows in enumerate(self.f_rows):

                @on_core(which)
                def _():
                    for copy in self.pair_f[which]:
                        copy.wait_recv()
                    add_into(self.df.at[:, :, rows], [self.lf.at[:, :, rows]])
                    self.f_one[which].start()

        def q_first(self):
            for which, half in enumerate(self.q_rows):

                @on_core(which)
                def _():
                    self.pair_q[which].wait_recv()
                    add_into(self.dq.at[:, :, half], [self.lq.at[:, :, half]])
                    self.q_one[which].start()
                    if which == 1:
                        self.pair_o.wait_recv()
                        add_into(self.do, [self.lo])
                        self.o_one.start()

        def f_second(self):
            @on_core(0)
            def _():
                sum_over(self.f_one[0], self.df.at[z, :, f_low], s.g_in)
                self.f_two[0].start()

            @on_core(1)
            def _():
                sum_over(self.f_one[1], self.df.at[:, y, f_high], s.g_in.at[:, :, pl.ds(0, 3 * UNIT - CUT)])
                self.f_two[1].start()

        def q_second(self):
            @on_core(0)
            def _():
                sum_over(self.q_one[0], self.dq.at[z, :, low], self.q_in)
                self.q_two[0].start()

            @on_core(1)
            def _():
                sum_over(self.q_one[1], self.dq.at[:, y, high], self.q_in)
                self.q_two[1].start()
                sum_over(self.o_one, self.do.at[y], self.o_in)
                for k in range(3):

                    @pl.when(lax.rem(z + 3 - k, 4) == seq)
                    def _():
                        self.o_two[k].start()

        def f_third(self):
            for which, rows, landing in ((0, f_low, s.g_in2), (1, f_high, s.g_in2.at[:, pl.ds(0, 3 * UNIT - CUT)])):

                @on_core(which)
                def _():
                    sum_over(self.f_two[which], self.df.at[z, y, rows], landing)

        def f_out(self):
            for which in (0, 1):

                @on_core(which)
                def _():
                    copies, here = self.f_three[which]
                    for copy in copies + [here]:
                        copy.start()

        def q_third(self):
            for which, half in enumerate(self.q_rows):

                @on_core(which)
                def _():
                    sum_over(self.q_two[which], self.dq.at[z, y, half], s.q_in2)
                    if which == 1:

                        @pl.when(z == seq)
                        def _():
                            for k in range(3):
                                self.o_two[k].wait_recv()
                            add_into(self.do.at[y], [s.o_in2.at[k] for k in range(3)])

        def q_out(self):
            for which in (0, 1):

                @on_core(which)
                def _():
                    copies, here = self.q_three[which]
                    for copy in copies + [here]:
                        copy.start()
                    if which == 1:

                        @pl.when(z == seq)
                        def _():
                            copies, here = self.o_three
                            for copy in copies + [here]:
                                copy.start()

        def end(self):
            for which in (0, 1):

                @on_core(which)
                def _():
                    mine = self.layer == which
                    rings = [self.f_one, self.f_two, self.q_one, self.q_two]
                    for ring in rings:
                        ring[which].sent()
                    for copies, here in (self.q_three[which], self.f_three[which]):
                        for copy in copies:
                            copy.wait_send()
                        if mine:
                            here.wait()
                        else:
                            here.wait_send()
                    for copy in self.pair_f[1 - which] + [self.pair_q[1 - which]]:
                        copy.wait_send()
                    if which == 0:
                        self.pair_o.wait_send()
                    else:
                        self.o_one.sent()
                        for k in range(3):

                            @pl.when(lax.rem(z + 3 - k, 4) == seq)
                            def _():
                                self.o_two[k].wait_send()

                        @pl.when(z == seq)
                        def _():
                            copies, here = self.o_three
                            for copy in copies:
                                copy.wait_send()
                            if mine:
                                here.wait()
                            else:
                                here.wait_send()

                    if mine:
                        for source in (0, 1):
                            for copies, here in (self.q_three[source], self.f_three[source]):
                                for copy in copies:
                                    copy.wait_recv()
                                if source != which:
                                    here.wait_recv()
                        copies, here = self.o_three
                        for k in range(3):

                            @pl.when(lax.rem(z + k + 1, 4) == seq)
                            def _():
                                copies[k].wait_recv()

                        if which == 0:

                            @pl.when(z == seq)
                            def _():
                                here.wait_recv()

    grads = [Gradients(0), Gradients(1)]

    logit_columns = dot(w_beta[0], pick_columns(8, 2 * seq), TN)
    s.own_q[:, 768:QW] = logit_columns.astype(BF16)
    for copy in own_q:
        copy.wait()
    weights[0].first_q()

    for which, q_part, f_part in ((0, low, f_low), (1, high, f_high)):

        @on_core(which)
        def _():
            s.wq[which, z, y, q_part] = s.own_q[q_part]

    own_small = s.small.at[core]
    own_small[0:1, :] = norm_in[...]
    own_small[1:2, :] = norm_ffn[...]
    own_small[2:3, 0:HD] = norm_head[...]
    for tap in range(4):
        for part in range(3):
            row = 4 + 3 * tap + part
            own_small[row : row + 1, 0:256] = conv_w[
                0, part, tap : tap + 1, pl.ds(pl.multiple_of(256 * seq, 256), 256)
            ]
    pair_small.start()
    mine_of = pick(UNIT, 176, UNIT * seq)
    for kind in range(2):
        s.own_f[UNIT * kind : UNIT * kind + UNIT, :] = dot(mine_of, w_ffn[0, kind], NN).astype(BF16)
    s.own_f[2 * UNIT : 3 * UNIT, :] = dot(mine_of, w_down[0], NN).astype(BF16)
    weights[0].first_f()
    for which, f_part in ((0, f_low), (1, f_high)):

        @on_core(which)
        def _():
            s.wf[which, z, y, f_part] = s.own_f[f_part]

    weights[0].second_q()
    own_x.wait()
    x_gather.arrive()
    pair_small.wait_recv()
    for half in both_halves:
        norm_rows(s, 0, half)
    weights[0].second_o()
    weights[0].third_q()
    weights[0].second_f()
    weights[0].third_o()
    weights[1].first_q()
    weights[1].first_f()
    cot_gather.start()
    incoming = []
    for layer in (0, 1):
        weights[layer].arrived_q()
        for index, half in enumerate(both_halves):
            if layer == 1:
                incoming[index].arrive()
                norm_rows(s, 1, half)
            project(s, layer, half)

        mixer_forward(s, *perms, layer)
        turn = 2 * layer
        reduces = [
            start_rows(turn, half, dot(half_of(s.att, layer, half), s.wo[layer].reshape(256, D), NN))
            for half in both_halves
        ]
        if layer == 0:
            weights[1].second_q()
            weights[0].third_f()
            weights[1].second_o()
            weights[1].second_f()
        gathers = []
        for ring, half in zip(reduces, both_halves):
            total = rows_total(turn, half, ring)
            residual = s.rows_in[layer, seq, half].astype(F32) + total
            s.residual[layer, half] = residual
            s.normed_ffn[layer, seq, half] = (
                residual * rms(residual) * s.small[layer, 1:2, :]
            ).astype(BF16)
            gathers.append(send_rows(s.normed_ffn.at[layer], half))
        all_sent(incoming)

        weights[layer].arrived_f()
        turn = 2 * layer + 1
        more = []
        for ring, half in zip(gathers, both_halves):
            ring.arrive()
            more.append(start_rows(turn, half, ffn_forward(s, layer, half)))
        all_sent(reduces + gathers)
        if layer == 0:
            weights[1].third_q()
            weights[1].third_o()
        incoming = []
        for ring, half in zip(more, both_halves):
            out = (s.residual[layer, half] + rows_total(turn, half, ring)).astype(BF16)
            if layer == 0:
                s.rows_in[1, seq, half] = out
                incoming.append(send_rows(s.rows_in.at[1], half))
            else:
                s.final[0, half] = out
        if layer == 0:
            weights[1].third_f()
        all_sent(more)

    for each in weights:
        each.sent()
    own_cot.wait()
    cot_gather.arrive()
    for layer in (1, 0):
        mine = grads[layer]
        turn = 6 - 2 * layer
        reduces = []
        for index, half in enumerate(both_halves):
            if layer == 0:
                incoming[index].arrive()
            reduces.append(start_rows(turn, half, ffn_backward(s, layer, half)))
        all_sent(incoming)
        mine.free(0)
        ffn_weights(s, layer, 2)
        mine.taken(0)
        mine.hand_f(1, 0)
        ffn_weights(s, layer, 0)
        mine.hand_f(0, 0)
        ffn_weights(s, layer, 1)
        mine.hand_f(0, 1)
        mine.hand_f(1, 1)
        if layer == 0:
            grads[1].f_third()
            grads[1].q_second()
        gathers, gains = [], []
        for ring, half in zip(reduces, both_halves):
            value = s.residual[layer, half]
            grad, gain = rms_back(
                rows_total(turn, half, ring), value, rms(value), s.small[layer, 1:2, :]
            )
            grad = s.outer[layer, seq, half].astype(F32) + grad
            s.grad_residual[half] = grad
            s.branch[layer, seq, half] = grad.astype(BF16)
            gathers.append(send_rows(s.branch.at[layer], half))
            gains.append(gain)
        gain_ffn = gains[0] + gains[1]
        mine.f_first()
        if layer == 0:
            grads[1].q_third()
        for ring in gathers:
            ring.arrive()
        mixer_backward(s, *perms, layer)
        s.dsmall[layer, 1:2, :] = gain_ffn
        all_sent(reduces + gathers)

        turn = 7 - 2 * layer
        reduces = [
            start_rows(
                turn,
                half,
                dot(
                    s.grad_proj[:, half, :].reshape(PACK // 2, QW),
                    s.wq[layer].reshape(D, QW),
                    NT,
                ),
            )
            for half in both_halves
        ]
        mine.free(1)
        mixer_weights(s, layer)
        mine.taken(1)
        mine.hand_q()
        if layer == 0:
            mine.q_first()
        incoming, gains = [], []
        for ring, half in zip(reduces, both_halves):
            value = s.rows_in[layer, seq, half].astype(F32)
            grad, gain = rms_back(
                rows_total(turn, half, ring), value, rms(value), s.small[layer, 0:1, :]
            )
            grad = (s.grad_residual[half] + grad).astype(BF16)
            if layer == 1:
                s.outer[0, seq, half] = grad
                incoming.append(send_rows(s.outer.at[0], half))
            else:
                s.final[1, half] = grad
            gains.append(gain)
        s.dsmall[layer, 0:1, :] = gains[0] + gains[1]
        all_sent(reduces)
        if layer == 1:
            mine.f_second()
            mine.q_first()

    rows_copies = [
        pltpu.make_async_copy(s.final.at[k], rows_out.at[k, core], local.at[9 + k]) for k in (0, 1)
    ]
    pair_rows = [sems.copy(s.final.at[k], rows_out.at[k, core], partner) for k in (0, 1)]
    pair_gains = sems.copy(s.dsmall.at[1 - core], s.small_in.at[0], partner)
    pair_gains.start()
    for copy in rows_copies + pair_rows:
        copy.start()
    small_y = Direct(sems, y_peers, lambda k: s.small_sum.at[0], lambda k: s.small_in.at[1 + k])
    small_z = Direct(sems, z_peers, lambda k: s.small_sum.at[1], lambda k: s.small_in.at[4 + k])
    small_x = gather(x_peers, s.small_sum.at[2], small_out.at[seq])
    small_keep = pltpu.make_async_copy(s.small_sum.at[2], small_out.at[seq], local.at[11])
    pair_gains.wait_recv()
    s.small_sum[0] = s.dsmall[core] + s.small_in[0]
    small_y.start()
    grads[1].f_out()
    grads[1].q_out()
    grads[0].f_second()
    grads[0].f_third()
    grads[0].f_out()
    grads[0].q_second()
    small_y.arrive()
    s.small_sum[1] = s.small_sum[0] + s.small_in[1] + s.small_in[2] + s.small_in[3]
    small_z.start()
    grads[0].q_third()
    grads[0].q_out()
    small_z.arrive()
    s.small_sum[2] = s.small_sum[1] + s.small_in[4] + s.small_in[5] + s.small_in[6]
    small_x.start()
    small_keep.start()
    grads[1].end()
    grads[0].end()
    small_x.arrive()
    for copy in pair_rows:
        copy.wait()
    pair_gains.wait_send()
    for ring in (small_y, small_z, small_x, x_gather, cot_gather):
        ring.sent()
    pair_small.wait_send()
    for copy in rows_copies + [small_keep]:
        copy.wait()


def whole_program(*operands):
    return pl.pallas_call(
        program_kernel,
        out_shape=[
            sds((2, 2, ROWS, D), BF16),
            sds((4, 16, D), F32),
            sds((4, 64, QW), BF16),
            sds((4, 3 * UNIT, D), BF16),
            sds((64, D), BF16),
        ],
        in_specs=[ANY, ANY, VMEM, SMEM, VMEM, ANY, VMEM, VMEM, VMEM, ANY, VMEM, VMEM, VMEM],
        out_specs=[ANY] * 5,
        scratch_shapes=[pltpu.VMEM(shape, dtype) for _, shape, dtype in SCRATCH]
        + [
            pltpu.SemaphoreType.DMA((N_SEM,)),
            pltpu.SemaphoreType.DMA((N_SEM,)),
            pltpu.SemaphoreType.DMA((12,)),
            pltpu.SemaphoreType.REGULAR((2,)),
        ],
        compiler_params=pltpu.CompilerParams(
            collective_id=1, has_side_effects=True, vmem_limit_bytes=VMEM_BYTES
        ),
        name="layers",
    )(*operands)


def finish_kernel(
    rows,
    small,
    q,
    f,
    o,
    block_out,
    input_grad,
    grad_norm_in,
    grad_qkv,
    grad_beta,
    grad_conv,
    grad_norm_head,
    grad_out,
    grad_norm_ffn,
    grad_ffn,
    grad_down,
):
    block_out[:, 0] = rows[0]
    input_grad[:, 0] = rows[1]
    total = small[0] + small[1] + small[2] + small[3]
    grad_norm_in[...] = total[0:1]
    grad_norm_ffn[...] = total[1:2]
    grad_norm_head[...] = total[2:3, 0:HD]
    grad_out[0] = o[...].astype(F32)
    beta = jnp.zeros((8, 64), F32)
    for seq in range(4):
        lanes = slice(256 * seq, 256 * seq + 256)
        for tap in range(4):
            for part in range(3):
                row = 4 + 3 * tap + part
                grad_conv[0, part, tap : tap + 1, lanes] = small[seq, row : row + 1, 0:256]
        for part in range(3):
            grad_qkv[0, :, D * part + 256 * seq : D * part + 256 * seq + 256] = q[
                seq, :, 256 * part : 256 * part + 256
            ].astype(F32)
        beta = beta + dot(pick_columns(8, 2 * seq), q[seq, :, 768:QW], NT)
    grad_beta[0] = beta
    for kind in range(3):
        whole = f[:, UNIT * kind : UNIT * kind + UNIT, :].reshape(4 * UNIT, D)[:176].astype(F32)
        if kind < 2:
            grad_ffn[0, kind] = whole
        else:
            grad_down[0] = whole


def finish(*operands):
    shapes = [
        ((2, 1, ROWS, D), BF16),
        ((2, 1, ROWS, D), BF16),
        ((1, D), F32),
        ((1, 64, 3 * D), F32),
        ((1, H, 64), F32),
        ((1, 3, 4, D), F32),
        ((1, HD), F32),
        ((1, 64, D), F32),
        ((1, D), F32),
        ((1, 2, 176, D), F32),
        ((1, 176, D), F32),
    ]
    return pl.pallas_call(
        finish_kernel,
        out_shape=[sds(*shape) for shape in shapes],
        in_specs=[VMEM] * 5,
        out_specs=[VMEM] * 11,
        compiler_params=pltpu.CompilerParams(vmem_limit_bytes=VMEM_BYTES),
        name="finish",
    )(*operands)


def local(
    block_in,
    cotangent,
    perm_rows,
    doc_lengths,
    norm_in,
    w_qkv,
    w_beta,
    conv_w,
    norm_head,
    w_out,
    norm_ffn,
    w_ffn,
    w_down,
):
    results = list(finish(
        *whole_program(
            block_in,
            cotangent,
            perm_rows,
            doc_lengths,
            norm_in,
            w_qkv,
            jnp.swapaxes(w_beta, 1, 2),
            jnp.swapaxes(conv_w, 1, 2),
            norm_head,
            w_out,
            norm_ffn,
            jnp.swapaxes(w_ffn, 2, 3),
            w_down,
        )
    ))
    results[4] = jnp.swapaxes(results[4], 1, 2)
    results[5] = jnp.swapaxes(results[5], 1, 2)
    results[9] = jnp.swapaxes(results[9], 2, 3)
    return tuple(results)


def solution(mesh):
    placed = (
        P(None, "fsdp", "seq", None),
        P(None, "fsdp", "seq", None),
        P(None, "fsdp", None),
        P(None, "fsdp", None),
        P("section", None),
        P("section", "fsdp", None),
        P("section", "fsdp", None),
        P("section", None, None, None),
        P("section", None),
        P("section", "fsdp", None),
        P("section", None),
        P("section", None, None, "fsdp"),
        P("section", "fsdp", None),
    )
    return jax.shard_map(
        local,
        mesh=mesh,
        in_specs=placed,
        out_specs=(
            P(None, "fsdp", "seq", None),
            P(None, "fsdp", "seq", None),
            P("section", None),
            P("section", "fsdp", None),
            P("section", "fsdp", None),
            P("section", None, None, None),
            P("section", None),
            P("section", "fsdp", None),
            P("section", None),
            P("section", None, None, "fsdp"),
            P("section", "fsdp", None),
        ),
        check_vma=False,
    )
```

```python
import functools

import jax
import jax.numpy as jnp
from jax import lax
from jax.experimental import pallas as pl
from jax.experimental.pallas import tpu as pltpu
from jax.sharding import PartitionSpec as P

D = 1024
H = 8
HD = 128
PACK = 256
ROWS = 64
UNIT = 48
QW = 896
MESH = pl.DeviceIdType.MESH
F32, BF16 = jnp.float32, jnp.bfloat16
VMEM = pl.BlockSpec(memory_space=pltpu.VMEM)
SMEM = pl.BlockSpec(memory_space=pltpu.SMEM)
ANY = pl.BlockSpec(memory_space=pl.ANY)
VMEM_BYTES = 60 * 1024 * 1024


def sds(shape, dtype):
    return jax.ShapeDtypeStruct(shape, dtype)


def dot(left, right, dims):
    return lax.dot_general(left, right, (dims, ((), ())), preferred_element_type=F32)


NN = ((1,), (0,))
NT = ((1,), (1,))
TN = ((0,), (0,))


def halves(value):
    high = value.astype(BF16)
    return high, (value - high.astype(F32)).astype(BF16)


def dot3(left, right, dims):
    return dot(left[0], right[0], dims) + (
        dot(left[0], right[1], dims) + dot(left[1], right[0], dims)
    )


def place():
    fsdp = lax.axis_index("fsdp")
    return (
        lax.axis_index("section"),
        lax.axis_index("seq"),
        lax.div(fsdp, 4),
        lax.rem(fsdp, 4),
    )


def along_x(seq, step):
    return {"seq": lax.rem(seq + step, 4)}


def along_y(z, y, step):
    return {"fsdp": z * 4 + lax.rem(y + step, 4)}


def along_z(z, y, step):
    return {"fsdp": lax.rem(z + step, 4) * 4 + y}


def greet(peers):
    barrier = pltpu.get_barrier_semaphore()
    for peer in peers:
        pl.semaphore_signal(barrier, inc=1, device_id=peer, device_id_type=MESH)
    pl.semaphore_wait(barrier, len(peers))


def remote(source, target, send, recv, peer):
    return pltpu.make_async_remote_copy(
        src_ref=source,
        dst_ref=target,
        send_sem=send,
        recv_sem=recv,
        device_id=peer,
        device_id_type=MESH,
    )


CUT = 80


class Direct:
    def __init__(self, sems, peers, source, target):
        self.copies = [sems.copy(source(k), target(k), peer) for k, peer in enumerate(peers)]

    def start(self):
        for copy in self.copies:
            copy.start()

    def arrive(self):
        for copy in self.copies:
            copy.wait_recv()

    def sent(self):
        for copy in self.copies:
            copy.wait_send()


class RingReduce:
    def __init__(self, sems, me, right, left, part, near, from_left, from_right):
        at_right, at_left = lax.rem(me + 1, 4), lax.rem(me + 3, 4)
        opposite = lax.rem(me + 2, 4)
        self.me, self.part, self.near = me, part, near
        self.from_left, self.from_right = from_left, from_right
        self.at_right, self.at_left = at_right, at_left
        self.first = [
            sems.copy(part(opposite, 0), near(0), right),
            sems.copy(part(opposite, 1), near(1), left),
            sems.copy(part(at_right, 1), from_left(1), right),
            sems.copy(part(at_left, 0), from_right(0), left),
        ]
        self.second = [
            sems.copy(part(at_right, 0), from_left(0), right),
            sems.copy(part(at_left, 1), from_right(1), left),
        ]

    def start(self):
        for copy in self.first:
            copy.start()

    def middle(self):
        for half, index in ((0, self.at_right), (1, self.at_left)):
            self.first[half].wait_recv()
            add_into(self.part(index, half), [self.near(half)])
            self.second[half].start()

    def total(self):
        for copy in self.first[2:] + self.second:
            copy.wait_recv()
        for half in (0, 1):
            add_into(self.part(self.me, half), [self.from_left(half), self.from_right(half)])

    def sent(self):
        for copy in self.first + self.second:
            copy.wait_send()


class Semaphores:
    def __init__(self, send, recv):
        self.send, self.recv, self.used = send, recv, 0

    def copy(self, source, target, peer):
        index = self.used
        self.used += 1
        return remote(source, target, self.send.at[index], self.recv.at[index], peer)


def add_into(target, others):
    shape = target.shape
    if len(shape) == 2:
        value = target[...].astype(F32)
        for other in others:
            value = value + other[...].astype(F32)
        target[...] = value.astype(target.dtype)
        return

    def body(index, carry):
        add_into(target.at[index], [other.at[index] for other in others])
        return carry

    lax.fori_loop(0, shape[0], body, 0)


def rms(value):
    return lax.rsqrt(jnp.mean(value * value, axis=-1, keepdims=True) + 1e-06)


def rms_back(grad, value, scale, gain):
    weighted = grad * gain
    inner = jnp.mean(weighted * value, axis=-1, keepdims=True)
    return (
        scale * weighted - value * (scale * scale * scale) * inner,
        jnp.sum(grad * value * scale, axis=0, keepdims=True),
    )


def shifted(value, step):
    rows = value.shape[0]
    filler = jnp.zeros((abs(step), value.shape[1]), value.dtype)
    if step > 0:
        return jnp.concatenate([filler, value[: rows - step]], axis=0)
    return jnp.concatenate([value[-step:], filler], axis=0)


def doc_places(doc_len):
    col = lax.broadcasted_iota(jnp.int32, (PACK, 1), 0)
    row = lax.broadcasted_iota(jnp.int32, (1, PACK), 1)
    start_col, start_row = jnp.zeros_like(col), jnp.zeros_like(row)
    end = 0
    for doc in range(4):
        end = end + doc_len[doc]
        start_col = jnp.where(col >= end, end, start_col)
        start_row = jnp.where(row >= end, end, start_row)
    return col - start_col, start_col == start_row


def one_hot(column, row):
    return (column == row).astype(F32).astype(BF16)


def sigmoid(value):
    return 1.0 / (1.0 + jnp.exp(-value))


def conv_taps(small_ref, layer, tap, part):
    return small_ref[layer, 4 + tap * 3 + part : 5 + tap * 3 + part, 0:256]


def conv_part(series, small_ref, layer, part, offset):
    total = series * conv_taps(small_ref, layer, 0, part)
    for tap in range(1, 4):
        moved = jnp.where(offset >= tap, shifted(series, tap), 0.0)
        total = total + moved * conv_taps(small_ref, layer, tap, part)
    return total


def unit(value):
    scale = lax.rsqrt(jnp.sum(value * value, axis=-1, keepdims=True) + 1e-06)
    return value * scale, scale


def inverses(systems):
    col, row = masks()
    apart = col ^ row
    identity = jnp.where(col == row, 1.0, 0.0)
    rough = [(identity - jnp.where(apart == 1, system, 0.0)).astype(BF16) for system in systems]
    for level in range(1, 8):
        mask = (apart >> level) == 1
        corner = [jnp.where(mask, system, 0.0).astype(BF16) for system in systems]
        inner = [dot(c, r, NN).astype(BF16) for c, r in zip(corner, rough)]
        rough = [r - dot(r, i, NN).astype(BF16) for r, i in zip(rough, inner)]
    split = [halves(system) for system in systems]
    left = [
        identity - r.astype(F32) - (dot(high, r, NN) + dot(low, r, NN))
        for r, (high, low) in zip(rough, split)
    ]
    return [r.astype(F32) + dot(r, rest.astype(BF16), NN) for r, rest in zip(rough, left)]


def masks():
    col = lax.broadcasted_iota(jnp.int32, (PACK, PACK), 0)
    row = lax.broadcasted_iota(jnp.int32, (PACK, PACK), 1)
    return col, row


def to_places(perm_row):
    return one_hot(lax.broadcasted_iota(jnp.int32, (PACK, 1), 0), perm_row)


def norm_rows(s, layer, half):
    x = s.rows_in[layer, :, half, :].reshape(PACK // 2, D).astype(F32)
    x = (x * rms(x) * s.small[layer, 0:1, :]).astype(BF16)
    s.normed[layer, :, half, :] = x.reshape(4, ROWS // 2, D)


def project(s, layer, half):
    normed = s.normed[layer, :, half, :].reshape(PACK // 2, D)
    proj = dot(normed, s.wq[layer].reshape(D, QW), NN).astype(BF16)
    s.stored[:, half, :] = proj.reshape(4, ROWS // 2, QW)


def mixer_forward(s, perm_row, doc_len, layer):
    small = s.small
    places = to_places(perm_row)
    proj = dot(places, s.stored[...].reshape(PACK, QW), NN)
    s.proj[layer] = proj.astype(BF16)
    offset, same = doc_places(doc_len)
    activated = []
    for kind in range(3):
        pre = conv_part(proj[:, 256 * kind : 256 * kind + 256], small, layer, kind, offset)
        activated.append(pre * sigmoid(pre))
    col, row = masks()
    strict = same & (col > row)
    tri = same & (col >= row)
    lanes = [slice(128 * head, 128 * head + 128) for head in range(2)]
    query = [halves(unit(activated[0][:, at])[0] * HD**-0.5) for at in lanes]
    key = [halves(unit(activated[1][:, at])[0]) for at in lanes]
    strength = [sigmoid(proj[:, 768 + head : 769 + head]) for head in range(2)]
    source = [halves(b * activated[2][:, at]) for b, at in zip(strength, lanes)]
    systems = [jnp.where(strict, b * dot3(k, k, NT), 0.0) for b, k in zip(strength, key)]
    scores = [halves(jnp.where(tri, dot3(q, k, NT), 0.0)) for q, k in zip(query, key)]
    solved = inverses(systems)
    fresh = [dot3(halves(t), r, NN) for t, r in zip(solved, source)]
    produced = [dot3(p, halves(u), NN) for p, u in zip(scores, fresh)]
    heads = []
    for head in range(2):
        s.solved[layer, head] = solved[head]
        s.fresh[layer, head] = fresh[head]
        s.produced[layer, head] = produced[head]
        out = produced[head]
        scale = lax.rsqrt(jnp.mean(out * out, axis=-1, keepdims=True) + 1e-05)
        heads.append((out * scale * small[layer, 2:3, 0:128]).astype(BF16))
    mixed = jnp.concatenate(heads, axis=1)
    s.att[layer] = dot(places, mixed, TN).astype(BF16).reshape(4, ROWS, 256)


def mixer_backward(s, perm_row, doc_len, layer):
    small = s.small
    grad = s.branch[layer].reshape(PACK, D)
    grad_att = dot(grad, s.wo[layer].reshape(256, D), NT).astype(BF16)
    places = to_places(perm_row)
    grad_att = dot(places, grad_att, NN)
    proj = s.proj[layer].astype(F32)
    offset, same = doc_places(doc_len)
    pres, gates = [], []
    for kind in range(3):
        pre = conv_part(proj[:, 256 * kind : 256 * kind + 256], small, layer, kind, offset)
        pres.append(pre)
        gates.append(sigmoid(pre))
    col, row = masks()
    strict = same & (col > row)
    tri = same & (col >= row)
    gain = small[layer, 2:3, 0:128]
    both = range(2)
    lanes = [slice(128 * head, 128 * head + 128) for head in both]
    acts = [pre * gate for pre, gate in zip(pres, gates)]
    act_q, act_k, value = [[act[:, at] for at in lanes] for act in acts]
    unit_q, unit_k = [unit(a) for a in act_q], [unit(a) for a in act_k]
    query = [halves(q * HD**-0.5) for q, _ in unit_q]
    key = [halves(k) for k, _ in unit_k]
    strength = [sigmoid(proj[:, 768 + head : 769 + head]) for head in both]
    gain_grad = jnp.zeros((1, HD), F32)
    grad_o = []
    for head in both:
        produced = s.produced[layer, head]
        scale = lax.rsqrt(jnp.mean(produced * produced, axis=-1, keepdims=True) + 1e-05)
        given = grad_att[:, lanes[head]]
        weighted = given * gain
        inner = jnp.mean(weighted * produced, axis=-1, keepdims=True)
        grad_o.append(halves(scale * weighted - produced * (scale * scale * scale) * inner))
        gain_grad = gain_grad + jnp.sum(given * produced * scale, axis=0, keepdims=True)
    fresh = [halves(s.fresh[layer, head]) for head in both]
    scores = [halves(jnp.where(tri, dot3(query[h], key[h], NT), 0.0)) for h in both]
    grad_fresh = [halves(dot3(scores[h], grad_o[h], TN)) for h in both]
    gram = [dot3(key[h], key[h], NT) for h in both]
    grad_scores = [halves(jnp.where(tri, dot3(grad_o[h], fresh[h], NT), 0.0)) for h in both]
    grad_source = [dot3(halves(s.solved[layer, h]), grad_fresh[h], TN) for h in both]
    grad_query = [dot3(grad_scores[h], key[h], NN) for h in both]
    grad_system = [
        jnp.where(strict, -dot3(halves(grad_source[h]), fresh[h], NT), 0.0) for h in both
    ]
    grad_key = [dot3(grad_scores[h], query[h], TN) for h in both]
    grad_gram = [halves(strength[h] * grad_system[h]) for h in both]
    grad_key = [
        grad_key[h] + dot3(grad_gram[h], key[h], NN) + dot3(grad_gram[h], key[h], TN) for h in both
    ]
    grads = [[], [], []]
    logit_grads = []
    for h in both:
        grad_strength = jnp.sum(grad_source[h] * value[h], axis=-1, keepdims=True) + jnp.sum(
            grad_system[h] * gram[h], axis=-1, keepdims=True
        )
        logit_grads.append(grad_strength * strength[h] * (1.0 - strength[h]))
        for kind, act, scale, grad in (
            (0, act_q[h], unit_q[h][1], grad_query[h] * HD**-0.5),
            (1, act_k[h], unit_k[h][1], grad_key[h]),
        ):
            along = jnp.sum(act * grad, axis=-1, keepdims=True)
            grads[kind].append(scale * grad - act * (scale * scale * scale) * along)
        grads[2].append(strength[h] * grad_source[h])
    dsmall = s.dsmall.at[layer]
    dsmall[...] = jnp.zeros((16, D), F32)
    dsmall[2:3, 0:128] = gain_grad
    pieces = []
    for kind in range(3):
        pre, gate = pres[kind], gates[kind]
        grad_pre = jnp.concatenate(grads[kind], axis=1) * gate * (1.0 + pre * (1.0 - gate))
        series = proj[:, 256 * kind : 256 * kind + 256]
        total = grad_pre * conv_taps(small, layer, 0, kind)
        dsmall[4 + kind : 5 + kind, 0:256] = jnp.sum(grad_pre * series, axis=0, keepdims=True)
        for tap in range(1, 4):
            kept = jnp.where(offset >= tap, grad_pre, 0.0)
            total = total + shifted(kept, -tap) * conv_taps(small, layer, tap, kind)
            dsmall[4 + tap * 3 + kind : 5 + tap * 3 + kind, 0:256] = jnp.sum(
                kept * shifted(series, tap), axis=0, keepdims=True
            )
        pieces.append(total.astype(BF16))
    lane = lax.broadcasted_iota(jnp.int32, (1, 128), 1)
    pieces.append(
        jnp.where(lane == 0, logit_grads[0], jnp.where(lane == 1, logit_grads[1], 0.0)).astype(BF16)
    )
    grad_proj = jnp.concatenate(pieces, axis=1)
    s.grad_proj[...] = dot(places, grad_proj, TN).astype(BF16).reshape(4, ROWS, QW)


def units(weights, layer, kind):
    return weights[layer, :, :, UNIT * kind : UNIT * kind + UNIT, :].reshape(768, D)


def half_of(ref, layer, half):
    return ref[layer, :, half, :].reshape(PACK // 2, ref.shape[-1])


def put_half(ref, layer, half, value):
    ref[layer, :, half, :] = value.reshape(4, ROWS // 2, ref.shape[-1])


def ffn_forward(s, layer, half):
    normed = half_of(s.normed_ffn, layer, half)
    gate = dot(normed, units(s.wf, layer, 0), NT)
    up = dot(normed, units(s.wf, layer, 1), NT)
    put_half(s.gate, layer, half, gate)
    put_half(s.up, layer, half, up)
    hidden = (gate * sigmoid(gate) * up).astype(BF16)
    return dot(hidden, units(s.wf, layer, 2), NN)


def ffn_backward(s, layer, half):
    grad = half_of(s.outer, layer, half)
    gate, up = half_of(s.gate, layer, half), half_of(s.up, layer, half)
    sig = sigmoid(gate)
    grad_hidden = dot(grad, units(s.wf, layer, 2), NT)
    grad_gate = (grad_hidden * up * sig * (1.0 + gate * (1.0 - sig))).astype(BF16)
    grad_up = (grad_hidden * gate * sig).astype(BF16)
    put_half(s.unit_grads, 0, half, grad_gate)
    put_half(s.unit_grads, 1, half, grad_up)
    put_half(s.unit_grads, 2, half, (gate * sig * up).astype(BF16))
    return dot(grad_gate, units(s.wf, layer, 0), NN) + dot(grad_up, units(s.wf, layer, 1), NN)


def ffn_weights(s, layer, kind):
    right = (s.outer if kind == 2 else s.normed_ffn)[layer].reshape(PACK, D)
    s.dwf[layer, :, :, UNIT * kind : UNIT * kind + UNIT, :] = (
        dot(s.unit_grads[kind].reshape(PACK, 768), right, TN).astype(BF16).reshape(4, 4, UNIT, D)
    )


def mixer_weights(s, layer):
    s.dwo[layer] = (
        dot(s.att[layer].reshape(PACK, 256), s.branch[layer].reshape(PACK, D), TN).astype(BF16).reshape(4, 64, D)
    )
    s.dwq[layer] = (
        dot(s.normed[layer].reshape(PACK, D), s.grad_proj[...].reshape(PACK, QW), TN)
        .astype(BF16)
        .reshape(4, 4, 64, QW)
    )


SCRATCH = [
    ("rows_in", (2, 4, ROWS, D), BF16),
    ("outer", (2, 4, ROWS, D), BF16),
    ("normed_ffn", (2, 4, ROWS, D), BF16),
    ("branch", (2, 4, ROWS, D), BF16),
    ("small", (2, 16, D), F32),
    ("own_q", (64, QW), BF16),
    ("own_f", (3 * UNIT, D), BF16),
    ("raw_ffn", (2, 176, D), BF16),
    ("raw_down", (176, D), BF16),
    ("wq", (2, 4, 4, 64, QW), BF16),
    ("wf", (2, 4, 4, 3 * UNIT, D), BF16),
    ("wo", (2, 4, 64, D), BF16),
    ("dwq", (2, 4, 4, 64, QW), BF16),
    ("dwf", (2, 4, 4, 3 * UNIT, D), BF16),
    ("dwo", (2, 4, 64, D), BF16),
    ("normed", (2, 4, ROWS, D), BF16),
    ("stored", (4, ROWS, QW), BF16),
    ("proj", (2, PACK, QW), BF16),
    ("solved", (2, 2, PACK, PACK), F32),
    ("fresh", (2, 2, PACK, HD), F32),
    ("produced", (2, 2, PACK, HD), F32),
    ("att", (2, 4, ROWS, 256), BF16),
    ("gate", (2, 4, ROWS, 768), F32),
    ("up", (2, 4, ROWS, 768), F32),
    ("unit_grads", (3, 4, ROWS, 768), BF16),
    ("grad_proj", (4, ROWS, QW), BF16),
    ("residual", (2, ROWS, D), F32),
    ("grad_residual", (ROWS, D), F32),
    ("part", (2, 4, ROWS, D), BF16),
    ("landing", (2, 3, ROWS, D), BF16),
    ("final", (2, ROWS, D), BF16),
    ("dsmall", (2, 16, D), F32),
    ("small_sum", (3, 16, D), F32),
    ("small_in", (7, 16, D), F32),
    ("q_in", (2, 3, 4, 32, QW), BF16),
    ("g_in", (3, 4, CUT, D), BF16),
    ("o_in", (2, 3, 64, D), BF16),
    ("q_in2", (2, 3, 32, QW), BF16),
    ("g_in2", (3, CUT, D), BF16),
    ("o_in2", (2, 3, 64, D), BF16),
]
N_SEM = 420


class Refs:
    pass


def pick(rows, columns, first):
    row = lax.broadcasted_iota(jnp.int32, (rows, columns), 0)
    column = lax.broadcasted_iota(jnp.int32, (rows, columns), 1)
    return one_hot(column, row + first)


def pick_columns(count, first):
    row = lax.broadcasted_iota(jnp.int32, (count, 128), 0)
    column = lax.broadcasted_iota(jnp.int32, (count, 128), 1)
    return ((row == first + column) & (column < 2)).astype(F32).astype(BF16)


def program_kernel(*refs):
    (
        block_in,
        cotangent,
        perm_ref,
        doc_ref,
        norm_in,
        w_qkv,
        w_beta,
        conv_w,
        norm_head,
        w_out,
        norm_ffn,
        w_ffn,
        w_down,
    ) = refs[:13]
    rows_out, small_out, q_out, f_out, o_out = refs[13:18]
    s = Refs()
    for (name, _, _), ref in zip(SCRATCH, refs[18:]):
        setattr(s, name, ref)
    send, recv, local, credit = refs[18 + len(SCRATCH) :]
    sems = Semaphores(send, recv)
    core, seq, z, y = place()
    partner = {"section": 1 - core}
    x_peers = [along_x(seq, k) for k in (1, 2, 3)]
    y_peers = [along_y(z, y, k) for k in (1, 2, 3)]
    z_peers = [along_z(z, y, k) for k in (1, 2, 3)]
    perm_row = perm_ref[core]
    perms = (perm_row, [doc_ref[core, 0, k] for k in range(4)])
    x_ref, cot_ref, o_ref = block_in.at[core, 0], cotangent.at[core, 0], w_out.at[0]

    def gather(peers, source, target):
        return Direct(sems, peers, lambda k: source, lambda k: target)

    low, high = pl.ds(0, 32), pl.ds(32, 32)
    f_low, f_high = pl.ds(0, CUT), pl.ds(CUT, 3 * UNIT - CUT)

    def on_core(which):
        return pl.when(core == which)

    def on(which, peers):
        return [{**peer, "section": which} for peer in peers]

    own_q = [
        pltpu.make_async_copy(
            w_qkv.at[0, :, pl.ds(pl.multiple_of(D * kind + 256 * seq, 256), 256)],
            s.own_q.at[:, pl.ds(256 * kind, 256)],
            local.at[kind],
        )
        for kind in range(3)
    ]
    for copy in own_q:
        copy.start()
    own_x = pltpu.make_async_copy(x_ref, s.rows_in.at[0, seq], local.at[3])
    own_cot = pltpu.make_async_copy(cot_ref, s.outer.at[1, seq], local.at[4])
    own_o = pltpu.make_async_copy(o_ref, s.wo.at[1, y], local.at[5])
    own_x.start()
    own_raw = [
        pltpu.make_async_copy(w_ffn.at[0], s.raw_ffn, local.at[12]),
        pltpu.make_async_copy(w_down.at[0], s.raw_down, local.at[13]),
    ]
    for copy in own_raw:
        copy.start()
    own_cot.start()

    greet(
        [partner]
        + [peer for peers in (x_peers, y_peers, z_peers) for c in (0, 1) for peer in on(c, peers)]
    )
    x_gather = gather(x_peers, x_ref, s.rows_in.at[0, seq])
    cot_gather = gather(x_peers, cot_ref, s.outer.at[1, seq])
    pair_small = sems.copy(s.small.at[core], s.small.at[core], partner)
    x_gather.start()

    class Weights:
        def __init__(self, layer):
            self.layer = layer
            wq, wf, wo = s.wq.at[layer], s.wf.at[layer], s.wo.at[layer]
            self.wo = wo
            axes = (y_peers, z_peers)

            def first(source, target, rows):
                return [
                    [
                        sems.copy(source.at[part], target.at[z, y, part], peer)
                        for peer in on(which, axes[which])
                        + ([partner] if which != layer else [])
                    ]
                    for which, part in enumerate(rows)
                ]

            def second(target, rows):
                return [
                    gather(z_peers, target.at[z, :, rows[0]], target.at[z, :, rows[0]]),
                    gather(y_peers, target.at[:, y, rows[1]], target.at[:, y, rows[1]]),
                ]

            def pairs(target, rows):
                pieces = [
                    [target.at[lax.rem(z + 4 - k, 4), :, rows[0]] for k in range(4)],
                    [target.at[:, lax.rem(y + 4 - k, 4), rows[1]] for k in range(4)],
                ]
                return [[sems.copy(piece, piece, partner) for piece in part] for part in pieces]

            q_rows, f_rows = (low, high), (f_low, f_high)
            self.q_one, self.q_two = first(s.own_q, wq, q_rows), second(wq, q_rows)
            self.f_one, self.f_two = first(s.own_f, wf, f_rows), second(wf, f_rows)
            self.pair_q, self.pair_f = pairs(wq, q_rows), pairs(wf, f_rows)
            self.o_one = [sems.copy(o_ref, wo.at[y], peer) for peer in on(1, z_peers)]
            if layer == 0:
                self.o_pair = sems.copy(o_ref, wo.at[y], partner)
            self.o_two = gather(y_peers, wo.at[y], wo.at[y])
            self.pair_o = sems.copy(wo, wo, partner)

        def first_q(self):
            @on_core(self.layer)
            def _():
                for copies in self.q_one:
                    for copy in copies:
                        copy.start()

        def first_f(self):
            @on_core(self.layer)
            def _():
                @pl.when(z == seq)
                def _():
                    for copy in self.o_one:
                        copy.start()
                    if self.layer == 0:
                        self.o_pair.start()
                    else:
                        own_o.start()

                for copies in self.f_one:
                    for copy in copies:
                        copy.start()

        def second_of(self, one, two, pair):
            for which in (0, 1):

                @on_core(which)
                def _():
                    for copy in one[which]:
                        copy.wait_recv()
                    two[which].start()
                    pair[which][0].start()

        def second_q(self):
            self.second_of(self.q_one, self.q_two, self.pair_q)

        def second_f(self):
            self.second_of(self.f_one, self.f_two, self.pair_f)

        def second_o(self):
            @on_core(1)
            def _():
                @pl.when(z == seq)
                def _():
                    if self.layer == 0:
                        self.o_pair.wait_recv()
                    else:
                        own_o.wait()

                for k in range(3):

                    @pl.when(lax.rem(seq + k + 1, 4) == z)
                    def _():
                        self.o_one[k].wait_recv()

                self.o_two.start()

        def third_of(self, two, pair):
            for which in (0, 1):

                @on_core(which)
                def _():
                    for k in range(3):
                        two[which].copies[k].wait_recv()
                        pair[which][k + 1].start()

        def third_q(self):
            self.third_of(self.q_two, self.pair_q)

        def third_f(self):
            self.third_of(self.f_two, self.pair_f)

        def third_o(self):
            @on_core(1)
            def _():
                self.o_two.arrive()
                self.pair_o.start()

        def arrived(self, pair, with_o):
            for which in (0, 1):

                @on_core(1 - which)
                def _():
                    for copy in pair[which]:
                        copy.wait_recv()
                    if with_o and which == 1:
                        self.pair_o.wait_recv()

        def arrived_q(self):
            self.arrived(self.pair_q, True)

        def arrived_f(self):
            self.arrived(self.pair_f, False)

        def sent(self):
            @on_core(self.layer)
            def _():
                for copies in self.q_one + self.f_one:
                    for copy in copies:
                        copy.wait_send()

                @pl.when(z == seq)
                def _():
                    for copy in self.o_one:
                        copy.wait_send()
                    if self.layer == 0:
                        self.o_pair.wait_send()

            for which in (0, 1):

                @on_core(which)
                def _():
                    for ring in (self.q_two[which], self.f_two[which]):
                        ring.sent()
                    for copy in self.pair_q[which] + self.pair_f[which]:
                        copy.wait_send()
                    if which == 1:
                        self.o_two.sent()
                        self.pair_o.wait_send()

    weights = [Weights(0), Weights(1)]

    both_halves = (low, high)

    def start_rows(turn, half, value):
        part, landing = s.part.at[turn % 2], s.landing.at[turn % 2]
        part[:, half, :] = value.astype(BF16).reshape(4, ROWS // 2, D)
        ring = Direct(
            sems,
            x_peers,
            lambda k: part.at[lax.rem(seq + k + 1, 4), half],
            lambda k: landing.at[k, half],
        )
        ring.start()
        return ring

    def rows_total(turn, half, ring):
        ring.arrive()
        total = s.part[turn % 2, seq, half].astype(F32)
        for k in range(3):
            total = total + s.landing[turn % 2, k, half].astype(F32)
        return total

    def send_rows(place_of, half):
        ring = gather(x_peers, place_of.at[seq, half], place_of.at[seq, half])
        ring.start()
        return ring

    def all_sent(rings):
        for ring in rings:
            ring.sent()

    def sum_over(ring, target, landing):
        ring.arrive()
        add_into(target, [landing.at[k] for k in range(3)])

    def scatter(peers, me, part, landing):
        return Direct(
            sems, peers, lambda k: part(lax.rem(me + k + 1, 4)), lambda k: landing.at[k]
        )

    class Gradients:
        def __init__(self, layer):
            self.layer = layer
            dq, df, do = s.dwq.at[layer], s.dwf.at[layer], s.dwo.at[layer]
            lq, lf, lo = s.wq.at[1], s.wf.at[1], s.wo.at[1]
            self.dq, self.df, self.do = dq, df, do
            self.q_in, self.o_in = s.q_in.at[layer], s.o_in.at[layer]
            self.q_in2, self.o_in2 = s.q_in2.at[layer], s.o_in2.at[layer]
            self.lq, self.lf, self.lo = lq, lf, lo
            self.q_rows, self.f_rows = (low, high), (f_low, f_high)

            def pair_f(first, count):
                rows = pl.ds(first, count)
                return sems.copy(df.at[:, :, rows], lf.at[:, :, rows], partner)

            self.pair_f = [
                [pair_f(0, UNIT), pair_f(UNIT, CUT - UNIT)],
                [pair_f(2 * UNIT, UNIT), pair_f(CUT, 2 * UNIT - CUT)],
            ]
            self.pair_q = [sems.copy(dq.at[:, :, half], lq.at[:, :, half], partner) for half in self.q_rows]
            self.pair_o = sems.copy(do, lo, partner)
            def ring_of(me, right, left, part, rows):
                def block(which):
                    return lambda half: s.g_in.at[which, pl.ds(2 * half, 2), rows]

                return RingReduce(sems, me, right, left, part, block(0), block(1), block(2))

            self.f_one = [
                ring_of(
                    z,
                    z_peers[0],
                    z_peers[2],
                    lambda j, half: df.at[j, pl.ds(2 * half, 2), f_low],
                    pl.ds(0, CUT),
                ),
                ring_of(
                    y,
                    y_peers[0],
                    y_peers[2],
                    lambda j, half: df.at[pl.ds(2 * half, 2), j, f_high],
                    pl.ds(0, 3 * UNIT - CUT),
                ),
            ]
            self.f_two = [
                scatter(y_peers, y, lambda j: df.at[z, j, f_low], s.g_in2),
                scatter(z_peers, z, lambda j: df.at[j, y, f_high], s.g_in2.at[:, pl.ds(0, 3 * UNIT - CUT)]),
            ]
            self.q_one = [
                scatter(z_peers, z, lambda j: dq.at[j, :, low], self.q_in),
                scatter(y_peers, y, lambda j: dq.at[:, j, high], self.q_in),
            ]
            self.q_two = [
                scatter(y_peers, y, lambda j: dq.at[z, j, low], self.q_in2),
                scatter(z_peers, z, lambda j: dq.at[j, y, high], self.q_in2),
            ]
            self.o_one = scatter(y_peers, y, lambda j: do.at[j], self.o_in)
            self.o_two = [
                sems.copy(do.at[y], self.o_in2.at[k], along_z(z, y, 3 - k)) for k in range(3)
            ]
            holders = [{**peer, "section": layer} for peer in x_peers]

            def to_holders(which, source, target, index):
                copies = [sems.copy(source, target, peer) for peer in holders]
                if which == layer:
                    return copies, pltpu.make_async_copy(source, target, local.at[index])
                return copies, sems.copy(source, target, partner)

            self.q_three = [
                to_holders(which, dq.at[z, y, half], q_out.at[seq, half], 6)
                for which, half in enumerate(self.q_rows)
            ]
            self.f_three = [
                to_holders(which, df.at[z, y, rows], f_out.at[seq, rows], 7)
                for which, rows in enumerate(self.f_rows)
            ]
            self.o_three = to_holders(1, do.at[y], o_out, 8)

        def free(self, index):
            pl.semaphore_signal(credit.at[index], inc=1, device_id=partner, device_id_type=MESH)

        def taken(self, index):
            pl.semaphore_wait(credit.at[index], 1)

        def hand_f(self, which, index):
            @on_core(1 - which)
            def _():
                self.pair_f[which][index].start()

        def hand_q(self):
            for which in (0, 1):

                @on_core(1 - which)
                def _():
                    self.pair_q[which].start()
                    if which == 1:
                        self.pair_o.start()

        def f_first(self):
            for which, rows in enumerate(self.f_rows):

                @on_core(which)
                def _():
                    for copy in self.pair_f[which]:
                        copy.wait_recv()
                    add_into(self.df.at[:, :, rows], [self.lf.at[:, :, rows]])
                    self.f_one[which].start()

        def q_first(self):
            for which, half in enumerate(self.q_rows):

                @on_core(which)
                def _():
                    self.pair_q[which].wait_recv()
                    add_into(self.dq.at[:, :, half], [self.lq.at[:, :, half]])
                    self.q_one[which].start()
                    if which == 1:
                        self.pair_o.wait_recv()
                        add_into(self.do, [self.lo])
                        self.o_one.start()

        def f_middle(self):
            for which in (0, 1):

                @on_core(which)
                def _():
                    self.f_one[which].middle()

        def f_second(self):
            for which in (0, 1):

                @on_core(which)
                def _():
                    self.f_one[which].total()
                    self.f_two[which].start()

        def q_second(self):
            @on_core(0)
            def _():
                sum_over(self.q_one[0], self.dq.at[z, :, low], self.q_in)
                self.q_two[0].start()

            @on_core(1)
            def _():
                sum_over(self.q_one[1], self.dq.at[:, y, high], self.q_in)
                self.q_two[1].start()
                sum_over(self.o_one, self.do.at[y], self.o_in)
                for k in range(3):

                    @pl.when(lax.rem(z + 3 - k, 4) == seq)
                    def _():
                        self.o_two[k].start()

        def f_third(self):
            for which, rows, landing in ((0, f_low, s.g_in2), (1, f_high, s.g_in2.at[:, pl.ds(0, 3 * UNIT - CUT)])):

                @on_core(which)
                def _():
                    sum_over(self.f_two[which], self.df.at[z, y, rows], landing)

        def f_out(self):
            for which in (0, 1):

                @on_core(which)
                def _():
                    copies, here = self.f_three[which]
                    for copy in copies + [here]:
                        copy.start()

        def q_third(self):
            for which, half in enumerate(self.q_rows):

                @on_core(which)
                def _():
                    sum_over(self.q_two[which], self.dq.at[z, y, half], self.q_in2)
                    if which == 1:

                        @pl.when(z == seq)
                        def _():
                            for k in range(3):
                                self.o_two[k].wait_recv()
                            add_into(self.do.at[y], [self.o_in2.at[k] for k in range(3)])

        def q_out(self):
            for which in (0, 1):

                @on_core(which)
                def _():
                    copies, here = self.q_three[which]
                    for copy in copies + [here]:
                        copy.start()
                    if which == 1:

                        @pl.when(z == seq)
                        def _():
                            copies, here = self.o_three
                            for copy in copies + [here]:
                                copy.start()

        def end(self):
            for which in (0, 1):

                @on_core(which)
                def _():
                    mine = self.layer == which
                    rings = [self.f_one, self.f_two, self.q_one, self.q_two]
                    for ring in rings:
                        ring[which].sent()
                    for copies, here in (self.q_three[which], self.f_three[which]):
                        for copy in copies:
                            copy.wait_send()
                        if mine:
                            here.wait()
                        else:
                            here.wait_send()
                    for copy in self.pair_f[1 - which] + [self.pair_q[1 - which]]:
                        copy.wait_send()
                    if which == 0:
                        self.pair_o.wait_send()
                    else:
                        self.o_one.sent()
                        for k in range(3):

                            @pl.when(lax.rem(z + 3 - k, 4) == seq)
                            def _():
                                self.o_two[k].wait_send()

                        @pl.when(z == seq)
                        def _():
                            copies, here = self.o_three
                            for copy in copies:
                                copy.wait_send()
                            if mine:
                                here.wait()
                            else:
                                here.wait_send()

                    if mine:
                        for source in (0, 1):
                            for copies, here in (self.q_three[source], self.f_three[source]):
                                for copy in copies:
                                    copy.wait_recv()
                                if source != which:
                                    here.wait_recv()
                        copies, here = self.o_three
                        for k in range(3):

                            @pl.when(lax.rem(z + k + 1, 4) == seq)
                            def _():
                                copies[k].wait_recv()

                        if which == 0:

                            @pl.when(z == seq)
                            def _():
                                here.wait_recv()

    grads = [Gradients(0), Gradients(1)]

    logit_columns = dot(w_beta[0], pick_columns(8, 2 * seq), TN)
    s.own_q[:, 768:QW] = logit_columns.astype(BF16)
    for copy in own_q:
        copy.wait()
    weights[0].first_q()

    for which, q_part, f_part in ((0, low, f_low), (1, high, f_high)):

        @on_core(which)
        def _():
            s.wq[which, z, y, q_part] = s.own_q[q_part]

    own_small = s.small.at[core]
    own_small[0:1, :] = norm_in[...]
    own_small[1:2, :] = norm_ffn[...]
    own_small[2:3, 0:HD] = norm_head[...]
    for tap in range(4):
        for part in range(3):
            row = 4 + 3 * tap + part
            own_small[row : row + 1, 0:256] = conv_w[
                0, part, tap : tap + 1, pl.ds(pl.multiple_of(256 * seq, 256), 256)
            ]
    pair_small.start()
    mine_of = pick(UNIT, 176, UNIT * seq)
    for copy in own_raw:
        copy.wait()
    for kind in range(2):
        s.own_f[UNIT * kind : UNIT * kind + UNIT, :] = dot(mine_of, s.raw_ffn[kind], NN).astype(BF16)
    s.own_f[2 * UNIT : 3 * UNIT, :] = dot(mine_of, s.raw_down[...], NN).astype(BF16)
    weights[0].first_f()
    for which, f_part in ((0, f_low), (1, f_high)):

        @on_core(which)
        def _():
            s.wf[which, z, y, f_part] = s.own_f[f_part]

    weights[0].second_q()
    own_x.wait()
    x_gather.arrive()
    pair_small.wait_recv()
    for half in both_halves:
        norm_rows(s, 0, half)
    weights[0].second_o()
    weights[0].third_q()
    weights[0].second_f()
    weights[0].third_o()
    weights[1].first_q()
    weights[1].first_f()
    cot_gather.start()
    incoming = []
    for layer in (0, 1):
        weights[layer].arrived_q()
        for index, half in enumerate(both_halves):
            if layer == 1:
                incoming[index].arrive()
                norm_rows(s, 1, half)
            project(s, layer, half)

        mixer_forward(s, *perms, layer)
        turn = 2 * layer
        reduces = [
            start_rows(turn, half, dot(half_of(s.att, layer, half), s.wo[layer].reshape(256, D), NN))
            for half in both_halves
        ]
        if layer == 0:
            weights[1].second_q()
            weights[0].third_f()
            weights[1].second_o()
            weights[1].second_f()
        gathers = []
        for ring, half in zip(reduces, both_halves):
            total = rows_total(turn, half, ring)
            residual = s.rows_in[layer, seq, half].astype(F32) + total
            s.residual[layer, half] = residual
            s.normed_ffn[layer, seq, half] = (
                residual * rms(residual) * s.small[layer, 1:2, :]
            ).astype(BF16)
            gathers.append(send_rows(s.normed_ffn.at[layer], half))
        all_sent(incoming)

        weights[layer].arrived_f()
        turn = 2 * layer + 1
        more = []
        for ring, half in zip(gathers, both_halves):
            ring.arrive()
            more.append(start_rows(turn, half, ffn_forward(s, layer, half)))
        all_sent(reduces + gathers)
        if layer == 0:
            weights[1].third_q()
            weights[1].third_o()
        incoming = []
        for ring, half in zip(more, both_halves):
            out = (s.residual[layer, half] + rows_total(turn, half, ring)).astype(BF16)
            if layer == 0:
                s.rows_in[1, seq, half] = out
                incoming.append(send_rows(s.rows_in.at[1], half))
            else:
                s.final[0, half] = out
        if layer == 0:
            weights[1].third_f()
        all_sent(more)

    for each in weights:
        each.sent()
    own_cot.wait()
    cot_gather.arrive()
    for layer in (1, 0):
        mine = grads[layer]
        turn = 6 - 2 * layer
        reduces = []
        for index, half in enumerate(both_halves):
            if layer == 0:
                incoming[index].arrive()
            reduces.append(start_rows(turn, half, ffn_backward(s, layer, half)))
        all_sent(incoming)
        mine.free(0)
        if layer == 0:
            mine.free(1)
        ffn_weights(s, layer, 2)
        mine.taken(0)
        mine.hand_f(1, 0)
        ffn_weights(s, layer, 0)
        mine.hand_f(0, 0)
        ffn_weights(s, layer, 1)
        mine.hand_f(0, 1)
        mine.hand_f(1, 1)
        if layer == 0:
            grads[1].f_third()
            grads[1].q_second()
        gathers, gains = [], []
        for ring, half in zip(reduces, both_halves):
            value = s.residual[layer, half]
            grad, gain = rms_back(
                rows_total(turn, half, ring), value, rms(value), s.small[layer, 1:2, :]
            )
            grad = s.outer[layer, seq, half].astype(F32) + grad
            s.grad_residual[half] = grad
            s.branch[layer, seq, half] = grad.astype(BF16)
            gathers.append(send_rows(s.branch.at[layer], half))
            gains.append(gain)
        gain_ffn = gains[0] + gains[1]
        mine.f_first()
        if layer == 0:
            grads[1].q_third()
        for ring in gathers:
            ring.arrive()
        mixer_backward(s, *perms, layer)
        s.dsmall[layer, 1:2, :] = gain_ffn
        all_sent(reduces + gathers)
        mine.f_middle()
        if layer == 0:
            mixer_weights(s, 0)
            mine.taken(1)
            mine.hand_q()

        turn = 7 - 2 * layer
        reduces = [
            start_rows(
                turn,
                half,
                dot(
                    s.grad_proj[:, half, :].reshape(PACK // 2, QW),
                    s.wq[layer].reshape(D, QW),
                    NT,
                ),
            )
            for half in both_halves
        ]
        if layer == 1:
            mine.free(1)
            mixer_weights(s, 1)
            mine.taken(1)
            mine.hand_q()
        else:
            mine.q_first()
        incoming, gains = [], []
        for ring, half in zip(reduces, both_halves):
            value = s.rows_in[layer, seq, half].astype(F32)
            grad, gain = rms_back(
                rows_total(turn, half, ring), value, rms(value), s.small[layer, 0:1, :]
            )
            grad = (s.grad_residual[half] + grad).astype(BF16)
            if layer == 1:
                s.outer[0, seq, half] = grad
                incoming.append(send_rows(s.outer.at[0], half))
            else:
                s.final[1, half] = grad
            gains.append(gain)
        s.dsmall[layer, 0:1, :] = gains[0] + gains[1]
        all_sent(reduces)
        if layer == 1:
            mine.f_second()
            mine.q_first()

    rows_copies = [
        pltpu.make_async_copy(s.final.at[k], rows_out.at[k, core], local.at[9 + k]) for k in (0, 1)
    ]
    pair_rows = [sems.copy(s.final.at[k], rows_out.at[k, core], partner) for k in (0, 1)]
    pair_gains = sems.copy(s.dsmall.at[1 - core], s.small_in.at[0], partner)
    pair_gains.start()
    for copy in rows_copies + pair_rows:
        copy.start()
    small_y = Direct(sems, y_peers, lambda k: s.small_sum.at[0], lambda k: s.small_in.at[1 + k])
    small_z = Direct(sems, z_peers, lambda k: s.small_sum.at[1], lambda k: s.small_in.at[4 + k])
    small_x = gather(x_peers, s.small_sum.at[2], small_out.at[seq])
    small_keep = pltpu.make_async_copy(s.small_sum.at[2], small_out.at[seq], local.at[11])
    grads[1].f_out()
    grads[1].q_out()
    grads[0].f_second()
    pair_gains.wait_recv()
    s.small_sum[0] = s.dsmall[core] + s.small_in[0]
    small_y.start()
    grads[0].q_second()
    grads[0].f_third()
    grads[0].f_out()
    small_y.arrive()
    s.small_sum[1] = s.small_sum[0] + s.small_in[1] + s.small_in[2] + s.small_in[3]
    small_z.start()
    grads[0].q_third()
    grads[0].q_out()
    small_z.arrive()
    s.small_sum[2] = s.small_sum[1] + s.small_in[4] + s.small_in[5] + s.small_in[6]
    small_x.start()
    small_keep.start()
    grads[1].end()
    grads[0].end()
    small_x.arrive()
    for copy in pair_rows:
        copy.wait()
    pair_gains.wait_send()
    for ring in (small_y, small_z, small_x, x_gather, cot_gather):
        ring.sent()
    pair_small.wait_send()
    for copy in rows_copies + [small_keep]:
        copy.wait()


def whole_program(*operands):
    return pl.pallas_call(
        program_kernel,
        out_shape=[
            sds((2, 2, ROWS, D), BF16),
            sds((4, 16, D), F32),
            sds((4, 64, QW), BF16),
            sds((4, 3 * UNIT, D), BF16),
            sds((64, D), BF16),
        ],
        in_specs=[ANY, ANY, VMEM, SMEM, VMEM, ANY, VMEM, VMEM, VMEM, ANY, VMEM, ANY, ANY],
        out_specs=[ANY] * 5,
        scratch_shapes=[pltpu.VMEM(shape, dtype) for _, shape, dtype in SCRATCH]
        + [
            pltpu.SemaphoreType.DMA((N_SEM,)),
            pltpu.SemaphoreType.DMA((N_SEM,)),
            pltpu.SemaphoreType.DMA((14,)),
            pltpu.SemaphoreType.REGULAR((2,)),
        ],
        compiler_params=pltpu.CompilerParams(
            collective_id=1, has_side_effects=True, vmem_limit_bytes=VMEM_BYTES
        ),
        name="layers",
    )(*operands)


def finish_kernel(
    rows,
    small,
    q,
    f,
    o,
    block_out,
    input_grad,
    grad_norm_in,
    grad_qkv,
    grad_beta,
    grad_conv,
    grad_norm_head,
    grad_out,
    grad_norm_ffn,
    grad_ffn,
    grad_down,
):
    block_out[:, 0] = rows[0]
    input_grad[:, 0] = rows[1]
    total = small[0] + small[1] + small[2] + small[3]
    grad_norm_in[...] = total[0:1]
    grad_norm_ffn[...] = total[1:2]
    grad_norm_head[...] = total[2:3, 0:HD]
    grad_out[0] = o[...].astype(F32)
    beta = jnp.zeros((8, 64), F32)
    for seq in range(4):
        lanes = slice(256 * seq, 256 * seq + 256)
        for tap in range(4):
            for part in range(3):
                row = 4 + 3 * tap + part
                grad_conv[0, part, tap : tap + 1, lanes] = small[seq, row : row + 1, 0:256]
        for part in range(3):
            grad_qkv[0, :, D * part + 256 * seq : D * part + 256 * seq + 256] = q[
                seq, :, 256 * part : 256 * part + 256
            ].astype(F32)
        beta = beta + dot(pick_columns(8, 2 * seq), q[seq, :, 768:QW], NT)
    grad_beta[0] = beta
    for kind in range(3):
        whole = f[:, UNIT * kind : UNIT * kind + UNIT, :].reshape(4 * UNIT, D)[:176].astype(F32)
        if kind < 2:
            grad_ffn[0, kind] = whole
        else:
            grad_down[0] = whole


def finish(*operands):
    shapes = [
        ((2, 1, ROWS, D), BF16),
        ((2, 1, ROWS, D), BF16),
        ((1, D), F32),
        ((1, 64, 3 * D), F32),
        ((1, H, 64), F32),
        ((1, 3, 4, D), F32),
        ((1, HD), F32),
        ((1, 64, D), F32),
        ((1, D), F32),
        ((1, 2, 176, D), F32),
        ((1, 176, D), F32),
    ]
    return pl.pallas_call(
        finish_kernel,
        out_shape=[sds(*shape) for shape in shapes],
        in_specs=[VMEM] * 5,
        out_specs=[VMEM] * 11,
        compiler_params=pltpu.CompilerParams(vmem_limit_bytes=VMEM_BYTES),
        name="finish",
    )(*operands)


def local(
    block_in,
    cotangent,
    perm_rows,
    doc_lengths,
    norm_in,
    w_qkv,
    w_beta,
    conv_w,
    norm_head,
    w_out,
    norm_ffn,
    w_ffn,
    w_down,
):
    results = list(finish(
        *whole_program(
            block_in,
            cotangent,
            perm_rows,
            doc_lengths,
            norm_in,
            w_qkv,
            jnp.swapaxes(w_beta, 1, 2),
            jnp.swapaxes(conv_w, 1, 2),
            norm_head,
            w_out,
            norm_ffn,
            jnp.swapaxes(w_ffn, 2, 3),
            w_down,
        )
    ))
    results[4] = jnp.swapaxes(results[4], 1, 2)
    results[5] = jnp.swapaxes(results[5], 1, 2)
    results[9] = jnp.swapaxes(results[9], 2, 3)
    return tuple(results)


def solution(mesh):
    placed = (
        P(None, "fsdp", "seq", None),
        P(None, "fsdp", "seq", None),
        P(None, "fsdp", None),
        P(None, "fsdp", None),
        P("section", None),
        P("section", "fsdp", None),
        P("section", "fsdp", None),
        P("section", None, None, None),
        P("section", None),
        P("section", "fsdp", None),
        P("section", None),
        P("section", None, None, "fsdp"),
        P("section", "fsdp", None),
    )
    return jax.shard_map(
        local,
        mesh=mesh,
        in_specs=placed,
        out_specs=(
            P(None, "fsdp", "seq", None),
            P(None, "fsdp", "seq", None),
            P("section", None),
            P("section", "fsdp", None),
            P("section", "fsdp", None),
            P("section", None, None, None),
            P("section", None),
            P("section", "fsdp", None),
            P("section", None),
            P("section", None, None, "fsdp"),
            P("section", "fsdp", None),
        ),
        check_vma=False,
    )
```

```python
import functools

import jax
import jax.numpy as jnp
from jax import lax
from jax.experimental import pallas as pl
from jax.experimental.pallas import tpu as pltpu
from jax.sharding import PartitionSpec as P

D = 1024
H = 8
HD = 128
PACK = 256
ROWS = 64
UNIT = 48
QW = 896
MESH = pl.DeviceIdType.MESH
F32, BF16 = jnp.float32, jnp.bfloat16
VMEM = pl.BlockSpec(memory_space=pltpu.VMEM)
SMEM = pl.BlockSpec(memory_space=pltpu.SMEM)
ANY = pl.BlockSpec(memory_space=pl.ANY)
VMEM_BYTES = 60 * 1024 * 1024


def sds(shape, dtype):
    return jax.ShapeDtypeStruct(shape, dtype)


def dot(left, right, dims):
    return lax.dot_general(left, right, (dims, ((), ())), preferred_element_type=F32)


NN = ((1,), (0,))
NT = ((1,), (1,))
TN = ((0,), (0,))


def halves(value):
    high = value.astype(BF16)
    return high, (value - high.astype(F32)).astype(BF16)


def dot3(left, right, dims):
    return dot(left[0], right[0], dims) + (
        dot(left[0], right[1], dims) + dot(left[1], right[0], dims)
    )


def place():
    fsdp = lax.axis_index("fsdp")
    return (
        lax.axis_index("section"),
        lax.axis_index("seq"),
        lax.div(fsdp, 4),
        lax.rem(fsdp, 4),
    )


def along_x(seq, step):
    return {"seq": lax.rem(seq + step, 4)}


def along_y(z, y, step):
    return {"fsdp": z * 4 + lax.rem(y + step, 4)}


def along_z(z, y, step):
    return {"fsdp": lax.rem(z + step, 4) * 4 + y}


def greet(peers):
    barrier = pltpu.get_barrier_semaphore()
    for peer in peers:
        pl.semaphore_signal(barrier, inc=1, device_id=peer, device_id_type=MESH)
    pl.semaphore_wait(barrier, len(peers))


def remote(source, target, send, recv, peer):
    return pltpu.make_async_remote_copy(
        src_ref=source,
        dst_ref=target,
        send_sem=send,
        recv_sem=recv,
        device_id=peer,
        device_id_type=MESH,
    )


CUT = 80


class Direct:
    def __init__(self, sems, peers, source, target):
        self.copies = [sems.copy(source(k), target(k), peer) for k, peer in enumerate(peers)]

    def start(self):
        for k in (1, 0, 2):
            self.copies[k].start()

    def arrive(self):
        for copy in self.copies:
            copy.wait_recv()

    def sent(self):
        for copy in self.copies:
            copy.wait_send()


class RingReduce:
    def __init__(self, sems, me, right, left, part, near, from_left, from_right):
        at_right, at_left = lax.rem(me + 1, 4), lax.rem(me + 3, 4)
        opposite = lax.rem(me + 2, 4)
        self.me, self.part, self.near = me, part, near
        self.from_left, self.from_right = from_left, from_right
        self.at_right, self.at_left = at_right, at_left
        self.first = [
            sems.copy(part(opposite, 0), near(0), right),
            sems.copy(part(opposite, 1), near(1), left),
            sems.copy(part(at_right, 1), from_left(1), right),
            sems.copy(part(at_left, 0), from_right(0), left),
        ]
        self.second = [
            sems.copy(part(at_right, 0), from_left(0), right),
            sems.copy(part(at_left, 1), from_right(1), left),
        ]

    def start(self):
        for copy in self.first:
            copy.start()

    def middle(self):
        for half, index in ((0, self.at_right), (1, self.at_left)):
            self.first[half].wait_recv()
            add_into(self.part(index, half), [self.near(half)])
            self.second[half].start()

    def total(self):
        for copy in self.first[2:] + self.second:
            copy.wait_recv()
        for half in (0, 1):
            add_into(self.part(self.me, half), [self.from_left(half), self.from_right(half)])

    def sent(self):
        for copy in self.first + self.second:
            copy.wait_send()


class Semaphores:
    def __init__(self, send, recv):
        self.send, self.recv, self.used = send, recv, 0

    def copy(self, source, target, peer):
        index = self.used
        self.used += 1
        return remote(source, target, self.send.at[index], self.recv.at[index], peer)


def add_into(target, others):
    shape = target.shape
    if len(shape) == 2:
        value = target[...].astype(F32)
        for other in others:
            value = value + other[...].astype(F32)
        target[...] = value.astype(target.dtype)
        return

    def body(index, carry):
        add_into(target.at[index], [other.at[index] for other in others])
        return carry

    lax.fori_loop(0, shape[0], body, 0)


def rms(value):
    return lax.rsqrt(jnp.mean(value * value, axis=-1, keepdims=True) + 1e-06)


def rms_back(grad, value, scale, gain):
    weighted = grad * gain
    inner = jnp.mean(weighted * value, axis=-1, keepdims=True)
    return (
        scale * weighted - value * (scale * scale * scale) * inner,
        jnp.sum(grad * value * scale, axis=0, keepdims=True),
    )


def shifted(value, step):
    rows = value.shape[0]
    filler = jnp.zeros((abs(step), value.shape[1]), value.dtype)
    if step > 0:
        return jnp.concatenate([filler, value[: rows - step]], axis=0)
    return jnp.concatenate([value[-step:], filler], axis=0)


def doc_places(doc_len):
    col = lax.broadcasted_iota(jnp.int32, (PACK, 1), 0)
    row = lax.broadcasted_iota(jnp.int32, (1, PACK), 1)
    start_col, start_row = jnp.zeros_like(col), jnp.zeros_like(row)
    end = 0
    for doc in range(4):
        end = end + doc_len[doc]
        start_col = jnp.where(col >= end, end, start_col)
        start_row = jnp.where(row >= end, end, start_row)
    return col - start_col, start_col == start_row


def one_hot(column, row):
    return (column == row).astype(F32).astype(BF16)


def sigmoid(value):
    return 1.0 / (1.0 + jnp.exp(-value))


def conv_taps(small_ref, layer, tap, part):
    return small_ref[layer, 4 + tap * 3 + part : 5 + tap * 3 + part, 0:256]


def conv_part(series, small_ref, layer, part, offset):
    total = series * conv_taps(small_ref, layer, 0, part)
    for tap in range(1, 4):
        moved = jnp.where(offset >= tap, shifted(series, tap), 0.0)
        total = total + moved * conv_taps(small_ref, layer, tap, part)
    return total


def unit(value):
    scale = lax.rsqrt(jnp.sum(value * value, axis=-1, keepdims=True) + 1e-06)
    return value * scale, scale


def inverses(systems):
    col, row = masks()
    apart = col ^ row
    identity = jnp.where(col == row, 1.0, 0.0)
    rough = [(identity - jnp.where(apart == 1, system, 0.0)).astype(BF16) for system in systems]
    for level in range(1, 8):
        mask = (apart >> level) == 1
        corner = [jnp.where(mask, system, 0.0).astype(BF16) for system in systems]
        inner = [dot(c, r, NN).astype(BF16) for c, r in zip(corner, rough)]
        rough = [r - dot(r, i, NN).astype(BF16) for r, i in zip(rough, inner)]
    split = [halves(system) for system in systems]
    left = [
        identity - r.astype(F32) - (dot(high, r, NN) + dot(low, r, NN))
        for r, (high, low) in zip(rough, split)
    ]
    return [r.astype(F32) + dot(r, rest.astype(BF16), NN) for r, rest in zip(rough, left)]


def masks():
    col = lax.broadcasted_iota(jnp.int32, (PACK, PACK), 0)
    row = lax.broadcasted_iota(jnp.int32, (PACK, PACK), 1)
    return col, row


def to_places(perm_row):
    return one_hot(lax.broadcasted_iota(jnp.int32, (PACK, 1), 0), perm_row)


def norm_rows(s, layer, half):
    x = s.rows_in[layer, :, half, :].reshape(PACK // 2, D).astype(F32)
    x = (x * rms(x) * s.small[layer, 0:1, :]).astype(BF16)
    s.normed[layer, :, half, :] = x.reshape(4, ROWS // 2, D)


def project_whole(s, layer):
    normed = s.normed[layer].reshape(PACK, D)
    proj = dot(normed, s.wq[layer].reshape(D, QW), NN).astype(BF16)
    s.stored[...] = proj.reshape(4, ROWS, QW)


def project(s, layer, half):
    normed = s.normed[layer, :, half, :].reshape(PACK // 2, D)
    proj = dot(normed, s.wq[layer].reshape(D, QW), NN).astype(BF16)
    s.stored[:, half, :] = proj.reshape(4, ROWS // 2, QW)


def mixer_forward(s, perm_row, doc_len, layer):
    small = s.small
    places = to_places(perm_row)
    proj = dot(places, s.stored[...].reshape(PACK, QW), NN)
    s.proj[layer] = proj.astype(BF16)
    offset, same = doc_places(doc_len)
    activated = []
    for kind in range(3):
        pre = conv_part(proj[:, 256 * kind : 256 * kind + 256], small, layer, kind, offset)
        activated.append(pre * sigmoid(pre))
    col, row = masks()
    strict = same & (col > row)
    tri = same & (col >= row)
    lanes = [slice(128 * head, 128 * head + 128) for head in range(2)]
    query = [halves(unit(activated[0][:, at])[0] * HD**-0.5) for at in lanes]
    key = [halves(unit(activated[1][:, at])[0]) for at in lanes]
    strength = [sigmoid(proj[:, 768 + head : 769 + head]) for head in range(2)]
    source = [halves(b * activated[2][:, at]) for b, at in zip(strength, lanes)]
    systems = [jnp.where(strict, b * dot3(k, k, NT), 0.0) for b, k in zip(strength, key)]
    scores = [halves(jnp.where(tri, dot3(q, k, NT), 0.0)) for q, k in zip(query, key)]
    solved = inverses(systems)
    fresh = [dot3(halves(t), r, NN) for t, r in zip(solved, source)]
    produced = [dot3(p, halves(u), NN) for p, u in zip(scores, fresh)]
    heads = []
    for head in range(2):
        s.solved[layer, head] = solved[head]
        s.fresh[layer, head] = fresh[head]
        s.produced[layer, head] = produced[head]
        out = produced[head]
        scale = lax.rsqrt(jnp.mean(out * out, axis=-1, keepdims=True) + 1e-05)
        heads.append((out * scale * small[layer, 2:3, 0:128]).astype(BF16))
    mixed = jnp.concatenate(heads, axis=1)
    s.att[layer] = dot(places, mixed, TN).astype(BF16).reshape(4, ROWS, 256)


def mixer_backward(s, perm_row, doc_len, layer):
    small = s.small
    grad = s.branch[layer].reshape(PACK, D)
    grad_att = dot(grad, s.wo[layer].reshape(256, D), NT).astype(BF16)
    places = to_places(perm_row)
    grad_att = dot(places, grad_att, NN)
    proj = s.proj[layer].astype(F32)
    offset, same = doc_places(doc_len)
    pres, gates = [], []
    for kind in range(3):
        pre = conv_part(proj[:, 256 * kind : 256 * kind + 256], small, layer, kind, offset)
        pres.append(pre)
        gates.append(sigmoid(pre))
    col, row = masks()
    strict = same & (col > row)
    tri = same & (col >= row)
    gain = small[layer, 2:3, 0:128]
    both = range(2)
    lanes = [slice(128 * head, 128 * head + 128) for head in both]
    acts = [pre * gate for pre, gate in zip(pres, gates)]
    act_q, act_k, value = [[act[:, at] for at in lanes] for act in acts]
    unit_q, unit_k = [unit(a) for a in act_q], [unit(a) for a in act_k]
    query = [halves(q * HD**-0.5) for q, _ in unit_q]
    key = [halves(k) for k, _ in unit_k]
    strength = [sigmoid(proj[:, 768 + head : 769 + head]) for head in both]
    gain_grad = jnp.zeros((1, HD), F32)
    grad_o = []
    for head in both:
        produced = s.produced[layer, head]
        scale = lax.rsqrt(jnp.mean(produced * produced, axis=-1, keepdims=True) + 1e-05)
        given = grad_att[:, lanes[head]]
        weighted = given * gain
        inner = jnp.mean(weighted * produced, axis=-1, keepdims=True)
        grad_o.append(halves(scale * weighted - produced * (scale * scale * scale) * inner))
        gain_grad = gain_grad + jnp.sum(given * produced * scale, axis=0, keepdims=True)
    fresh = [halves(s.fresh[layer, head]) for head in both]
    scores = [halves(jnp.where(tri, dot3(query[h], key[h], NT), 0.0)) for h in both]
    grad_fresh = [halves(dot3(scores[h], grad_o[h], TN)) for h in both]
    gram = [dot3(key[h], key[h], NT) for h in both]
    grad_scores = [halves(jnp.where(tri, dot3(grad_o[h], fresh[h], NT), 0.0)) for h in both]
    grad_source = [dot3(halves(s.solved[layer, h]), grad_fresh[h], TN) for h in both]
    grad_query = [dot(grad_scores[h][0], key[h][0], NN) for h in both]
    grad_system = [
        jnp.where(strict, -dot3(halves(grad_source[h]), fresh[h], NT), 0.0) for h in both
    ]
    grad_key = [dot(grad_scores[h][0], query[h][0], TN) for h in both]
    grad_gram = [(strength[h] * grad_system[h]).astype(BF16) for h in both]
    grad_key = [
        grad_key[h] + dot(grad_gram[h], key[h][0], NN) + dot(grad_gram[h], key[h][0], TN)
        for h in both
    ]
    grads = [[], [], []]
    logit_grads = []
    for h in both:
        grad_strength = jnp.sum(grad_source[h] * value[h], axis=-1, keepdims=True) + jnp.sum(
            grad_system[h] * gram[h], axis=-1, keepdims=True
        )
        logit_grads.append(grad_strength * strength[h] * (1.0 - strength[h]))
        for kind, act, scale, grad in (
            (0, act_q[h], unit_q[h][1], grad_query[h] * HD**-0.5),
            (1, act_k[h], unit_k[h][1], grad_key[h]),
        ):
            along = jnp.sum(act * grad, axis=-1, keepdims=True)
            grads[kind].append(scale * grad - act * (scale * scale * scale) * along)
        grads[2].append(strength[h] * grad_source[h])
    dsmall = s.dsmall.at[layer]
    dsmall[...] = jnp.zeros((8, D), F32)
    dsmall[2:3, 0:128] = gain_grad
    pieces = []
    for kind in range(3):
        pre, gate = pres[kind], gates[kind]
        grad_pre = jnp.concatenate(grads[kind], axis=1) * gate * (1.0 + pre * (1.0 - gate))
        series = proj[:, 256 * kind : 256 * kind + 256]
        total = grad_pre * conv_taps(small, layer, 0, kind)
        dsmall[3 + kind : 4 + kind, 0:256] = jnp.sum(grad_pre * series, axis=0, keepdims=True)
        for tap in range(1, 4):
            kept = jnp.where(offset >= tap, grad_pre, 0.0)
            total = total + shifted(kept, -tap) * conv_taps(small, layer, tap, kind)
            dsmall[3 + kind : 4 + kind, 256 * tap : 256 * tap + 256] = jnp.sum(
                kept * shifted(series, tap), axis=0, keepdims=True
            )
        pieces.append(total.astype(BF16))
    lane = lax.broadcasted_iota(jnp.int32, (1, 128), 1)
    pieces.append(
        jnp.where(lane == 0, logit_grads[0], jnp.where(lane == 1, logit_grads[1], 0.0)).astype(BF16)
    )
    grad_proj = jnp.concatenate(pieces, axis=1)
    s.grad_proj[...] = dot(places, grad_proj, TN).astype(BF16).reshape(4, ROWS, QW)


def units(weights, layer, kind):
    return weights[layer, :, :, UNIT * kind : UNIT * kind + UNIT, :].reshape(768, D)


def half_of(ref, layer, half):
    return ref[layer, :, half, :].reshape(PACK // 2, ref.shape[-1])


def put_half(ref, layer, half, value):
    ref[layer, :, half, :] = value.reshape(4, ROWS // 2, ref.shape[-1])


def ffn_forward(s, layer, half):
    normed = half_of(s.normed_ffn, layer, half)
    gate = dot(normed, units(s.wf, layer, 0), NT)
    up = dot(normed, units(s.wf, layer, 1), NT)
    put_half(s.gate, layer, half, gate)
    put_half(s.up, layer, half, up)
    hidden = (gate * sigmoid(gate) * up).astype(BF16)
    return dot(hidden, units(s.wf, layer, 2), NN)


def ffn_backward(s, layer, half):
    grad = half_of(s.outer, layer, half)
    gate, up = half_of(s.gate, layer, half), half_of(s.up, layer, half)
    sig = sigmoid(gate)
    grad_hidden = dot(grad, units(s.wf, layer, 2), NT)
    grad_gate = (grad_hidden * up * sig * (1.0 + gate * (1.0 - sig))).astype(BF16)
    grad_up = (grad_hidden * gate * sig).astype(BF16)
    put_half(s.unit_grads, 0, half, grad_gate)
    put_half(s.unit_grads, 1, half, grad_up)
    put_half(s.unit_grads, 2, half, (gate * sig * up).astype(BF16))
    return dot(grad_gate, units(s.wf, layer, 0), NN) + dot(grad_up, units(s.wf, layer, 1), NN)


def ffn_weights(s, layer, kind):
    right = (s.outer if kind == 2 else s.normed_ffn)[layer].reshape(PACK, D)
    s.dwf[layer, :, :, UNIT * kind : UNIT * kind + UNIT, :] = (
        dot(s.unit_grads[kind].reshape(PACK, 768), right, TN).astype(BF16).reshape(4, 4, UNIT, D)
    )


def mixer_weights(s, layer):
    s.dwo[layer] = (
        dot(s.att[layer].reshape(PACK, 256), s.branch[layer].reshape(PACK, D), TN).astype(BF16).reshape(4, 64, D)
    )
    s.dwq[layer] = (
        dot(s.normed[layer].reshape(PACK, D), s.grad_proj[...].reshape(PACK, QW), TN)
        .astype(BF16)
        .reshape(4, 4, 64, QW)
    )


SCRATCH = [
    ("rows_in", (2, 4, ROWS, D), BF16),
    ("outer", (2, 4, ROWS, D), BF16),
    ("normed_ffn", (2, 4, ROWS, D), BF16),
    ("branch", (2, 4, ROWS, D), BF16),
    ("small", (2, 16, D), F32),
    ("own_q", (64, QW), BF16),
    ("own_f", (3 * UNIT, D), BF16),
    ("raw_ffn", (2, 176, D), BF16),
    ("raw_down", (176, D), BF16),
    ("wq", (2, 4, 4, 64, QW), BF16),
    ("wf", (2, 4, 4, 3 * UNIT, D), BF16),
    ("wo", (2, 4, 64, D), BF16),
    ("dwq", (2, 4, 4, 64, QW), BF16),
    ("dwf", (2, 4, 4, 3 * UNIT, D), BF16),
    ("dwo", (2, 4, 64, D), BF16),
    ("normed", (2, 4, ROWS, D), BF16),
    ("stored", (4, ROWS, QW), BF16),
    ("proj", (2, PACK, QW), BF16),
    ("solved", (2, 2, PACK, PACK), F32),
    ("fresh", (2, 2, PACK, HD), F32),
    ("produced", (2, 2, PACK, HD), F32),
    ("att", (2, 4, ROWS, 256), BF16),
    ("gate", (2, 4, ROWS, 768), F32),
    ("up", (2, 4, ROWS, 768), F32),
    ("unit_grads", (3, 4, ROWS, 768), BF16),
    ("grad_proj", (4, ROWS, QW), BF16),
    ("residual", (2, ROWS, D), F32),
    ("grad_residual", (ROWS, D), F32),
    ("part", (2, 4, ROWS, D), BF16),
    ("landing", (2, 3, ROWS, D), BF16),
    ("final", (2, ROWS, D), BF16),
    ("dsmall", (2, 8, D), F32),
    ("small_sum", (3, 8, D), F32),
    ("small_in", (7, 8, D), F32),
    ("q_in", (2, 3, 4, 32, QW), BF16),
    ("g_in", (3, 4, CUT, D), BF16),
    ("o_in", (2, 3, 64, D), BF16),
    ("q_in2", (2, 3, 32, QW), BF16),
    ("g_in2", (3, CUT, D), BF16),
    ("o_in2", (2, 3, 64, D), BF16),
]
N_SEM = 420


class Refs:
    pass


def pick(rows, columns, first):
    row = lax.broadcasted_iota(jnp.int32, (rows, columns), 0)
    column = lax.broadcasted_iota(jnp.int32, (rows, columns), 1)
    return one_hot(column, row + first)


def pick_columns(count, first):
    row = lax.broadcasted_iota(jnp.int32, (count, 128), 0)
    column = lax.broadcasted_iota(jnp.int32, (count, 128), 1)
    return ((row == first + column) & (column < 2)).astype(F32).astype(BF16)


def program_kernel(*refs):
    (
        block_in,
        cotangent,
        perm_ref,
        doc_ref,
        norm_in,
        w_qkv,
        w_beta,
        conv_w,
        norm_head,
        w_out,
        norm_ffn,
        w_ffn,
        w_down,
    ) = refs[:13]
    rows_out, small_out, q_out, f_out, o_out = refs[13:18]
    s = Refs()
    for (name, _, _), ref in zip(SCRATCH, refs[18:]):
        setattr(s, name, ref)
    send, recv, local, credit = refs[18 + len(SCRATCH) :]
    sems = Semaphores(send, recv)
    core, seq, z, y = place()
    partner = {"section": 1 - core}
    x_peers = [along_x(seq, k) for k in (1, 2, 3)]
    y_peers = [along_y(z, y, k) for k in (1, 2, 3)]
    z_peers = [along_z(z, y, k) for k in (1, 2, 3)]
    perm_row = perm_ref[core]
    perms = (perm_row, [doc_ref[core, 0, k] for k in range(4)])
    x_ref, cot_ref, o_ref = block_in.at[core, 0], cotangent.at[core, 0], w_out.at[0]

    def gather(peers, source, target):
        return Direct(sems, peers, lambda k: source, lambda k: target)

    low, high = pl.ds(0, 32), pl.ds(32, 32)
    f_low, f_high = pl.ds(0, CUT), pl.ds(CUT, 3 * UNIT - CUT)

    def on_core(which):
        return pl.when(core == which)

    def on(which, peers):
        return [{**peer, "section": which} for peer in peers]

    own_q = [
        pltpu.make_async_copy(
            w_qkv.at[0, :, pl.ds(pl.multiple_of(D * kind + 256 * seq, 256), 256)],
            s.own_q.at[:, pl.ds(256 * kind, 256)],
            local.at[kind],
        )
        for kind in range(3)
    ]
    for copy in own_q:
        copy.start()
    own_x = pltpu.make_async_copy(x_ref, s.rows_in.at[0, seq], local.at[3])
    own_cot = pltpu.make_async_copy(cot_ref, s.outer.at[1, seq], local.at[4])
    own_o = pltpu.make_async_copy(o_ref, s.wo.at[1, y], local.at[5])
    own_x.start()
    own_raw = [
        pltpu.make_async_copy(w_ffn.at[0], s.raw_ffn, local.at[12]),
        pltpu.make_async_copy(w_down.at[0], s.raw_down, local.at[13]),
    ]
    for copy in own_raw:
        copy.start()
    own_cot.start()

    greet(
        [partner]
        + [peer for peers in (x_peers, y_peers, z_peers) for c in (0, 1) for peer in on(c, peers)]
    )
    x_gather = gather(x_peers, x_ref, s.rows_in.at[0, seq])
    cot_gather = gather(x_peers, cot_ref, s.outer.at[1, seq])
    pair_small = sems.copy(s.small.at[core], s.small.at[core], partner)
    x_gather.start()

    class Weights:
        def __init__(self, layer):
            self.layer = layer
            wq, wf, wo = s.wq.at[layer], s.wf.at[layer], s.wo.at[layer]
            self.wo = wo
            axes = (y_peers, z_peers)

            def first(source, target, rows):
                return [
                    [
                        sems.copy(source.at[part], target.at[z, y, part], peer)
                        for peer in on(which, axes[which])
                        + ([partner] if which != layer else [])
                    ]
                    for which, part in enumerate(rows)
                ]

            def second(target, rows):
                return [
                    gather(z_peers, target.at[z, :, rows[0]], target.at[z, :, rows[0]]),
                    gather(y_peers, target.at[:, y, rows[1]], target.at[:, y, rows[1]]),
                ]

            def pairs(target, rows):
                pieces = [
                    [target.at[lax.rem(z + 4 - k, 4), :, rows[0]] for k in range(4)],
                    [target.at[:, lax.rem(y + 4 - k, 4), rows[1]] for k in range(4)],
                ]
                return [[sems.copy(piece, piece, partner) for piece in part] for part in pieces]

            q_rows, f_rows = (low, high), (f_low, f_high)
            self.q_one, self.q_two = first(s.own_q, wq, q_rows), second(wq, q_rows)
            self.f_one, self.f_two = first(s.own_f, wf, f_rows), second(wf, f_rows)
            self.pair_q, self.pair_f = pairs(wq, q_rows), pairs(wf, f_rows)
            self.o_one = [sems.copy(o_ref, wo.at[y], peer) for peer in on(1, z_peers)]
            if layer == 0:
                self.o_pair = sems.copy(o_ref, wo.at[y], partner)
            self.o_two = gather(y_peers, wo.at[y], wo.at[y])
            self.pair_o = sems.copy(wo, wo, partner)

        def first_q(self):
            @on_core(self.layer)
            def _():
                for copies in self.q_one:
                    for copy in copies:
                        copy.start()

        def first_f(self):
            @on_core(self.layer)
            def _():
                @pl.when(z == seq)
                def _():
                    for copy in self.o_one:
                        copy.start()
                    if self.layer == 0:
                        self.o_pair.start()
                    else:
                        own_o.start()

                for copies in self.f_one:
                    for copy in copies:
                        copy.start()

        def second_of(self, one, two, pair):
            for which in (0, 1):

                @on_core(which)
                def _():
                    for copy in one[which]:
                        copy.wait_recv()
                    two[which].start()
                    pair[which][0].start()

        def second_q(self):
            self.second_of(self.q_one, self.q_two, self.pair_q)

        def second_f(self):
            self.second_of(self.f_one, self.f_two, self.pair_f)

        def second_o(self):
            @on_core(1)
            def _():
                @pl.when(z == seq)
                def _():
                    if self.layer == 0:
                        self.o_pair.wait_recv()
                    else:
                        own_o.wait()

                for k in range(3):

                    @pl.when(lax.rem(seq + k + 1, 4) == z)
                    def _():
                        self.o_one[k].wait_recv()

                self.o_two.start()

        def third_of(self, two, pair):
            for which in (0, 1):

                @on_core(which)
                def _():
                    for k in (0, 2, 1):
                        two[which].copies[k].wait_recv()
                        pair[which][k + 1].start()

        def third_q(self):
            self.third_of(self.q_two, self.pair_q)

        def third_f(self):
            self.third_of(self.f_two, self.pair_f)

        def third_o(self):
            @on_core(1)
            def _():
                self.o_two.arrive()
                self.pair_o.start()

        def arrived(self, pair, with_o):
            for which in (0, 1):

                @on_core(1 - which)
                def _():
                    for copy in pair[which]:
                        copy.wait_recv()
                    if with_o and which == 1:
                        self.pair_o.wait_recv()

        def arrived_q(self):
            self.arrived(self.pair_q, True)

        def arrived_f(self):
            self.arrived(self.pair_f, False)

        def sent(self):
            @on_core(self.layer)
            def _():
                for copies in self.q_one + self.f_one:
                    for copy in copies:
                        copy.wait_send()

                @pl.when(z == seq)
                def _():
                    for copy in self.o_one:
                        copy.wait_send()
                    if self.layer == 0:
                        self.o_pair.wait_send()

            for which in (0, 1):

                @on_core(which)
                def _():
                    for ring in (self.q_two[which], self.f_two[which]):
                        ring.sent()
                    for copy in self.pair_q[which] + self.pair_f[which]:
                        copy.wait_send()
                    if which == 1:
                        self.o_two.sent()
                        self.pair_o.wait_send()

    weights = [Weights(0), Weights(1)]

    both_halves = (low, high)

    def start_rows(turn, half, value):
        part, landing = s.part.at[turn % 2], s.landing.at[turn % 2]
        part[:, half, :] = value.astype(BF16).reshape(4, ROWS // 2, D)
        ring = Direct(
            sems,
            x_peers,
            lambda k: part.at[lax.rem(seq + k + 1, 4), half],
            lambda k: landing.at[k, half],
        )
        ring.start()
        return ring

    def rows_total(turn, half, ring):
        ring.arrive()
        total = s.part[turn % 2, seq, half].astype(F32)
        for k in range(3):
            total = total + s.landing[turn % 2, k, half].astype(F32)
        return total

    def send_rows(place_of, half):
        ring = gather(x_peers, place_of.at[seq, half], place_of.at[seq, half])
        ring.start()
        return ring

    def all_sent(rings):
        for ring in rings:
            ring.sent()

    def sum_over(ring, target, landing):
        ring.arrive()
        add_into(target, [landing.at[k] for k in range(3)])

    def scatter(peers, me, part, landing):
        return Direct(
            sems, peers, lambda k: part(lax.rem(me + k + 1, 4)), lambda k: landing.at[k]
        )

    class Gradients:
        def __init__(self, layer):
            self.layer = layer
            dq, df, do = s.dwq.at[layer], s.dwf.at[layer], s.dwo.at[layer]
            lq, lf, lo = s.wq.at[1], s.wf.at[1], s.wo.at[1]
            self.dq, self.df, self.do = dq, df, do
            self.q_in, self.o_in = s.q_in.at[layer], s.o_in.at[layer]
            self.q_in2, self.o_in2 = s.q_in2.at[layer], s.o_in2.at[layer]
            self.lq, self.lf, self.lo = lq, lf, lo
            self.q_rows, self.f_rows = (low, high), (f_low, f_high)

            def pair_f(first, count):
                rows = pl.ds(first, count)
                return sems.copy(df.at[:, :, rows], lf.at[:, :, rows], partner)

            self.pair_f = [
                [pair_f(0, UNIT), pair_f(UNIT, CUT - UNIT)],
                [pair_f(2 * UNIT, UNIT), pair_f(CUT, 2 * UNIT - CUT)],
            ]
            self.pair_q = [sems.copy(dq.at[:, :, half], lq.at[:, :, half], partner) for half in self.q_rows]
            self.pair_o = sems.copy(do, lo, partner)
            def ring_of(me, right, left, part, rows):
                def block(which):
                    return lambda half: s.g_in.at[which, pl.ds(2 * half, 2), rows]

                return RingReduce(sems, me, right, left, part, block(0), block(1), block(2))

            self.f_one = [
                ring_of(
                    z,
                    z_peers[0],
                    z_peers[2],
                    lambda j, half: df.at[j, pl.ds(2 * half, 2), f_low],
                    pl.ds(0, CUT),
                ),
                ring_of(
                    y,
                    y_peers[0],
                    y_peers[2],
                    lambda j, half: df.at[pl.ds(2 * half, 2), j, f_high],
                    pl.ds(0, 3 * UNIT - CUT),
                ),
            ]
            self.f_two = [
                scatter(y_peers, y, lambda j: df.at[z, j, f_low], s.g_in2),
                scatter(z_peers, z, lambda j: df.at[j, y, f_high], s.g_in2.at[:, pl.ds(0, 3 * UNIT - CUT)]),
            ]
            self.q_one = [
                scatter(z_peers, z, lambda j: dq.at[j, :, low], self.q_in),
                scatter(y_peers, y, lambda j: dq.at[:, j, high], self.q_in),
            ]
            self.q_two = [
                scatter(y_peers, y, lambda j: dq.at[z, j, low], self.q_in2),
                scatter(z_peers, z, lambda j: dq.at[j, y, high], self.q_in2),
            ]
            self.o_one = scatter(y_peers, y, lambda j: do.at[j], self.o_in)
            self.o_two = [
                sems.copy(do.at[y], self.o_in2.at[k], along_z(z, y, 3 - k)) for k in range(3)
            ]
            holders = [{**peer, "section": layer} for peer in x_peers]

            def to_holders(which, source, target, index):
                copies = [sems.copy(source, target, peer) for peer in holders]
                if which == layer:
                    return copies, pltpu.make_async_copy(source, target, local.at[index])
                return copies, sems.copy(source, target, partner)

            self.q_three = [
                to_holders(which, dq.at[z, y, half], q_out.at[seq, half], 6)
                for which, half in enumerate(self.q_rows)
            ]
            self.f_three = [
                to_holders(which, df.at[z, y, rows], f_out.at[seq, rows], 7)
                for which, rows in enumerate(self.f_rows)
            ]
            self.o_three = to_holders(1, do.at[y], o_out, 8)

        def free(self, index):
            pl.semaphore_signal(credit.at[index], inc=1, device_id=partner, device_id_type=MESH)

        def taken(self, index):
            pl.semaphore_wait(credit.at[index], 1)

        def hand_f(self, which, index):
            @on_core(1 - which)
            def _():
                self.pair_f[which][index].start()

        def hand_q(self):
            for which in (0, 1):

                @on_core(1 - which)
                def _():
                    self.pair_q[which].start()
                    if which == 1:
                        self.pair_o.start()

        def f_first(self):
            for which, rows in enumerate(self.f_rows):

                @on_core(which)
                def _():
                    for copy in self.pair_f[which]:
                        copy.wait_recv()
                    add_into(self.df.at[:, :, rows], [self.lf.at[:, :, rows]])
                    self.f_one[which].start()

        def q_first(self):
            for which, half in enumerate(self.q_rows):

                @on_core(which)
                def _():
                    self.pair_q[which].wait_recv()
                    add_into(self.dq.at[:, :, half], [self.lq.at[:, :, half]])
                    self.q_one[which].start()
                    if which == 1:
                        self.pair_o.wait_recv()
                        add_into(self.do, [self.lo])
                        self.o_one.start()

        def f_middle(self):
            for which in (0, 1):

                @on_core(which)
                def _():
                    self.f_one[which].middle()

        def f_second(self):
            for which in (0, 1):

                @on_core(which)
                def _():
                    self.f_one[which].total()
                    self.f_two[which].start()

        def q_second(self):
            @on_core(0)
            def _():
                sum_over(self.q_one[0], self.dq.at[z, :, low], self.q_in)
                self.q_two[0].start()

            @on_core(1)
            def _():
                sum_over(self.q_one[1], self.dq.at[:, y, high], self.q_in)
                self.q_two[1].start()
                sum_over(self.o_one, self.do.at[y], self.o_in)
                for k in range(3):

                    @pl.when(lax.rem(z + 3 - k, 4) == seq)
                    def _():
                        self.o_two[k].start()

        def f_third(self):
            for which, rows, landing in ((0, f_low, s.g_in2), (1, f_high, s.g_in2.at[:, pl.ds(0, 3 * UNIT - CUT)])):

                @on_core(which)
                def _():
                    sum_over(self.f_two[which], self.df.at[z, y, rows], landing)

        def f_out(self):
            for which in (0, 1):

                @on_core(which)
                def _():
                    copies, here = self.f_three[which]
                    for copy in copies + [here]:
                        copy.start()

        def q_third(self):
            for which, half in enumerate(self.q_rows):

                @on_core(which)
                def _():
                    sum_over(self.q_two[which], self.dq.at[z, y, half], self.q_in2)
                    if which == 1:

                        @pl.when(z == seq)
                        def _():
                            for k in range(3):
                                self.o_two[k].wait_recv()
                            add_into(self.do.at[y], [self.o_in2.at[k] for k in range(3)])

        def q_out(self):
            for which in (0, 1):

                @on_core(which)
                def _():
                    copies, here = self.q_three[which]
                    for copy in copies + [here]:
                        copy.start()
                    if which == 1:

                        @pl.when(z == seq)
                        def _():
                            copies, here = self.o_three
                            for copy in copies + [here]:
                                copy.start()

        def end(self):
            for which in (0, 1):

                @on_core(which)
                def _():
                    mine = self.layer == which
                    rings = [self.f_one, self.f_two, self.q_one, self.q_two]
                    for ring in rings:
                        ring[which].sent()
                    for copies, here in (self.q_three[which], self.f_three[which]):
                        for copy in copies:
                            copy.wait_send()
                        if mine:
                            here.wait()
                        else:
                            here.wait_send()
                    for copy in self.pair_f[1 - which] + [self.pair_q[1 - which]]:
                        copy.wait_send()
                    if which == 0:
                        self.pair_o.wait_send()
                    else:
                        self.o_one.sent()
                        for k in range(3):

                            @pl.when(lax.rem(z + 3 - k, 4) == seq)
                            def _():
                                self.o_two[k].wait_send()

                        @pl.when(z == seq)
                        def _():
                            copies, here = self.o_three
                            for copy in copies:
                                copy.wait_send()
                            if mine:
                                here.wait()
                            else:
                                here.wait_send()

                    if mine:
                        for source in (0, 1):
                            for copies, here in (self.q_three[source], self.f_three[source]):
                                for copy in copies:
                                    copy.wait_recv()
                                if source != which:
                                    here.wait_recv()
                        copies, here = self.o_three
                        for k in range(3):

                            @pl.when(lax.rem(z + k + 1, 4) == seq)
                            def _():
                                copies[k].wait_recv()

                        if which == 0:

                            @pl.when(z == seq)
                            def _():
                                here.wait_recv()

    grads = [Gradients(0), Gradients(1)]

    logit_columns = dot(w_beta[0], pick_columns(8, 2 * seq), TN)
    s.own_q[:, 768:QW] = logit_columns.astype(BF16)
    for copy in own_q:
        copy.wait()
    weights[0].first_q()

    for which, q_part, f_part in ((0, low, f_low), (1, high, f_high)):

        @on_core(which)
        def _():
            s.wq[which, z, y, q_part] = s.own_q[q_part]

    own_small = s.small.at[core]
    own_small[0:1, :] = norm_in[...]
    own_small[1:2, :] = norm_ffn[...]
    own_small[2:3, 0:HD] = norm_head[...]
    for tap in range(4):
        for part in range(3):
            row = 4 + 3 * tap + part
            own_small[row : row + 1, 0:256] = conv_w[
                0, part, tap : tap + 1, pl.ds(pl.multiple_of(256 * seq, 256), 256)
            ]
    pair_small.start()
    mine_of = pick(UNIT, 176, UNIT * seq)
    for copy in own_raw:
        copy.wait()
    for kind in range(2):
        s.own_f[UNIT * kind : UNIT * kind + UNIT, :] = dot(mine_of, s.raw_ffn[kind], NN).astype(BF16)
    s.own_f[2 * UNIT : 3 * UNIT, :] = dot(mine_of, s.raw_down[...], NN).astype(BF16)
    weights[0].first_f()
    for which, f_part in ((0, f_low), (1, f_high)):

        @on_core(which)
        def _():
            s.wf[which, z, y, f_part] = s.own_f[f_part]

    weights[0].second_q()
    own_x.wait()
    x_gather.arrive()
    pair_small.wait_recv()
    for half in both_halves:
        norm_rows(s, 0, half)
    weights[0].second_o()
    weights[0].third_q()
    weights[0].second_f()
    weights[0].third_o()
    weights[1].first_q()
    weights[1].first_f()
    cot_gather.start()
    incoming = []
    for layer in (0, 1):
        weights[layer].arrived_q()
        if layer == 0:
            project_whole(s, 0)
        else:
            for index, half in enumerate(both_halves):
                incoming[index].arrive()
                norm_rows(s, 1, half)
                project(s, 1, half)

        mixer_forward(s, *perms, layer)
        turn = 2 * layer
        reduces = [
            start_rows(turn, half, dot(half_of(s.att, layer, half), s.wo[layer].reshape(256, D), NN))
            for half in both_halves
        ]
        if layer == 0:
            weights[1].second_q()
            weights[0].third_f()
            weights[1].second_o()
            weights[1].second_f()
        gathers = []
        for ring, half in zip(reduces, both_halves):
            total = rows_total(turn, half, ring)
            residual = s.rows_in[layer, seq, half].astype(F32) + total
            s.residual[layer, half] = residual
            s.normed_ffn[layer, seq, half] = (
                residual * rms(residual) * s.small[layer, 1:2, :]
            ).astype(BF16)
            gathers.append(send_rows(s.normed_ffn.at[layer], half))
        all_sent(incoming)

        weights[layer].arrived_f()
        turn = 2 * layer + 1
        more = []
        for ring, half in zip(gathers, both_halves):
            ring.arrive()
            more.append(start_rows(turn, half, ffn_forward(s, layer, half)))
        all_sent(reduces + gathers)
        if layer == 0:
            weights[1].third_q()
            weights[1].third_o()
        incoming = []
        for ring, half in zip(more, both_halves):
            out = (s.residual[layer, half] + rows_total(turn, half, ring)).astype(BF16)
            if layer == 0:
                s.rows_in[1, seq, half] = out
                incoming.append(send_rows(s.rows_in.at[1], half))
            else:
                s.final[0, half] = out
        if layer == 0:
            weights[1].third_f()
        all_sent(more)

    for each in weights:
        each.sent()
    own_cot.wait()
    cot_gather.arrive()
    for layer in (1, 0):
        mine = grads[layer]
        turn = 6 - 2 * layer
        reduces = []
        for index, half in enumerate(both_halves):
            if layer == 0:
                incoming[index].arrive()
            reduces.append(start_rows(turn, half, ffn_backward(s, layer, half)))
        all_sent(incoming)
        mine.free(0)
        if layer == 0:
            mine.free(1)
        ffn_weights(s, layer, 2)
        mine.taken(0)
        mine.hand_f(1, 0)
        ffn_weights(s, layer, 0)
        mine.hand_f(0, 0)
        ffn_weights(s, layer, 1)
        mine.hand_f(0, 1)
        mine.hand_f(1, 1)
        if layer == 0:
            grads[1].f_third()
            grads[1].q_second()
        gathers, gains = [], []
        for ring, half in zip(reduces, both_halves):
            value = s.residual[layer, half]
            grad, gain = rms_back(
                rows_total(turn, half, ring), value, rms(value), s.small[layer, 1:2, :]
            )
            grad = s.outer[layer, seq, half].astype(F32) + grad
            s.grad_residual[half] = grad
            s.branch[layer, seq, half] = grad.astype(BF16)
            gathers.append(send_rows(s.branch.at[layer], half))
            gains.append(gain)
        gain_ffn = gains[0] + gains[1]
        mine.f_first()
        if layer == 0:
            grads[1].q_third()
        for ring in gathers:
            ring.arrive()
        mixer_backward(s, *perms, layer)
        s.dsmall[layer, 1:2, :] = gain_ffn
        all_sent(reduces + gathers)
        mine.f_middle()
        if layer == 0:
            mixer_weights(s, 0)
            mine.taken(1)
            mine.hand_q()

        turn = 7 - 2 * layer
        reduces = [
            start_rows(
                turn,
                half,
                dot(
                    s.grad_proj[:, half, :].reshape(PACK // 2, QW),
                    s.wq[layer].reshape(D, QW),
                    NT,
                ),
            )
            for half in both_halves
        ]
        if layer == 1:
            mine.free(1)
            mixer_weights(s, 1)
            mine.taken(1)
            mine.hand_q()
        else:
            mine.q_first()
        incoming, gains = [], []
        for ring, half in zip(reduces, both_halves):
            value = s.rows_in[layer, seq, half].astype(F32)
            grad, gain = rms_back(
                rows_total(turn, half, ring), value, rms(value), s.small[layer, 0:1, :]
            )
            grad = (s.grad_residual[half] + grad).astype(BF16)
            if layer == 1:
                s.outer[0, seq, half] = grad
                incoming.append(send_rows(s.outer.at[0], half))
            else:
                s.final[1, half] = grad
            gains.append(gain)
        s.dsmall[layer, 0:1, :] = gains[0] + gains[1]
        all_sent(reduces)
        if layer == 1:
            mine.f_second()
            mine.q_first()

    rows_copies = [
        pltpu.make_async_copy(s.final.at[k], rows_out.at[k, core], local.at[9 + k]) for k in (0, 1)
    ]
    pair_rows = [sems.copy(s.final.at[k], rows_out.at[k, core], partner) for k in (0, 1)]
    pair_gains = sems.copy(s.dsmall.at[1 - core], s.small_in.at[0], partner)
    pair_gains.start()
    for copy in rows_copies + pair_rows:
        copy.start()
    small_y = Direct(sems, y_peers, lambda k: s.small_sum.at[0], lambda k: s.small_in.at[1 + k])
    small_z = Direct(sems, z_peers, lambda k: s.small_sum.at[1], lambda k: s.small_in.at[4 + k])
    small_x = gather(x_peers, s.small_sum.at[2], small_out.at[seq])
    small_keep = pltpu.make_async_copy(s.small_sum.at[2], small_out.at[seq], local.at[11])
    grads[1].f_out()
    grads[1].q_out()
    grads[0].f_second()
    pair_gains.wait_recv()
    s.small_sum[0] = s.dsmall[core] + s.small_in[0]
    small_y.start()
    grads[0].q_second()
    grads[0].f_third()
    grads[0].f_out()
    small_y.arrive()
    s.small_sum[1] = s.small_sum[0] + s.small_in[1] + s.small_in[2] + s.small_in[3]
    small_z.start()
    grads[0].q_third()
    grads[0].q_out()
    small_z.arrive()
    s.small_sum[2] = s.small_sum[1] + s.small_in[4] + s.small_in[5] + s.small_in[6]
    small_x.start()
    small_keep.start()
    grads[1].end()
    grads[0].end()
    small_x.arrive()
    for copy in pair_rows:
        copy.wait()
    pair_gains.wait_send()
    for ring in (small_y, small_z, small_x, x_gather, cot_gather):
        ring.sent()
    pair_small.wait_send()
    for copy in rows_copies + [small_keep]:
        copy.wait()


def whole_program(*operands):
    return pl.pallas_call(
        program_kernel,
        out_shape=[
            sds((2, 2, ROWS, D), BF16),
            sds((4, 8, D), F32),
            sds((4, 64, QW), BF16),
            sds((4, 3 * UNIT, D), BF16),
            sds((64, D), BF16),
        ],
        in_specs=[ANY, ANY, VMEM, SMEM, VMEM, ANY, VMEM, VMEM, VMEM, ANY, VMEM, ANY, ANY],
        out_specs=[ANY] * 5,
        scratch_shapes=[pltpu.VMEM(shape, dtype) for _, shape, dtype in SCRATCH]
        + [
            pltpu.SemaphoreType.DMA((N_SEM,)),
            pltpu.SemaphoreType.DMA((N_SEM,)),
            pltpu.SemaphoreType.DMA((14,)),
            pltpu.SemaphoreType.REGULAR((2,)),
        ],
        compiler_params=pltpu.CompilerParams(
            collective_id=1, has_side_effects=True, vmem_limit_bytes=VMEM_BYTES
        ),
        name="layers",
    )(*operands)


def finish_kernel(
    rows,
    small,
    q,
    f,
    o,
    block_out,
    input_grad,
    grad_norm_in,
    grad_qkv,
    grad_beta,
    grad_conv,
    grad_norm_head,
    grad_out,
    grad_norm_ffn,
    grad_ffn,
    grad_down,
):
    block_out[:, 0] = rows[0]
    input_grad[:, 0] = rows[1]
    total = small[0] + small[1] + small[2] + small[3]
    grad_norm_in[...] = total[0:1]
    grad_norm_ffn[...] = total[1:2]
    grad_norm_head[...] = total[2:3, 0:HD]
    grad_out[0] = o[...].astype(F32)
    beta = jnp.zeros((8, 64), F32)
    for seq in range(4):
        lanes = slice(256 * seq, 256 * seq + 256)
        for tap in range(4):
            for part in range(3):
                grad_conv[0, part, tap : tap + 1, lanes] = small[
                    seq, 3 + part : 4 + part, 256 * tap : 256 * tap + 256
                ]
        for part in range(3):
            grad_qkv[0, :, D * part + 256 * seq : D * part + 256 * seq + 256] = q[
                seq, :, 256 * part : 256 * part + 256
            ].astype(F32)
        beta = beta + dot(pick_columns(8, 2 * seq), q[seq, :, 768:QW], NT)
    grad_beta[0] = beta
    for kind in range(3):
        whole = f[:, UNIT * kind : UNIT * kind + UNIT, :].reshape(4 * UNIT, D)[:176].astype(F32)
        if kind < 2:
            grad_ffn[0, kind] = whole
        else:
            grad_down[0] = whole


def finish(*operands):
    shapes = [
        ((2, 1, ROWS, D), BF16),
        ((2, 1, ROWS, D), BF16),
        ((1, D), F32),
        ((1, 64, 3 * D), F32),
        ((1, H, 64), F32),
        ((1, 3, 4, D), F32),
        ((1, HD), F32),
        ((1, 64, D), F32),
        ((1, D), F32),
        ((1, 2, 176, D), F32),
        ((1, 176, D), F32),
    ]
    return pl.pallas_call(
        finish_kernel,
        out_shape=[sds(*shape) for shape in shapes],
        in_specs=[VMEM] * 5,
        out_specs=[VMEM] * 11,
        compiler_params=pltpu.CompilerParams(vmem_limit_bytes=VMEM_BYTES),
        name="finish",
    )(*operands)


def local(
    block_in,
    cotangent,
    perm_rows,
    doc_lengths,
    norm_in,
    w_qkv,
    w_beta,
    conv_w,
    norm_head,
    w_out,
    norm_ffn,
    w_ffn,
    w_down,
):
    results = list(finish(
        *whole_program(
            block_in,
            cotangent,
            perm_rows,
            doc_lengths,
            norm_in,
            w_qkv,
            jnp.swapaxes(w_beta, 1, 2),
            jnp.swapaxes(conv_w, 1, 2),
            norm_head,
            w_out,
            norm_ffn,
            jnp.swapaxes(w_ffn, 2, 3),
            w_down,
        )
    ))
    results[4] = jnp.swapaxes(results[4], 1, 2)
    results[5] = jnp.swapaxes(results[5], 1, 2)
    results[9] = jnp.swapaxes(results[9], 2, 3)
    return tuple(results)


def solution(mesh):
    placed = (
        P(None, "fsdp", "seq", None),
        P(None, "fsdp", "seq", None),
        P(None, "fsdp", None),
        P(None, "fsdp", None),
        P("section", None),
        P("section", "fsdp", None),
        P("section", "fsdp", None),
        P("section", None, None, None),
        P("section", None),
        P("section", "fsdp", None),
        P("section", None),
        P("section", None, None, "fsdp"),
        P("section", "fsdp", None),
    )
    return jax.shard_map(
        local,
        mesh=mesh,
        in_specs=placed,
        out_specs=(
            P(None, "fsdp", "seq", None),
            P(None, "fsdp", "seq", None),
            P("section", None),
            P("section", "fsdp", None),
            P("section", "fsdp", None),
            P("section", None, None, None),
            P("section", None),
            P("section", "fsdp", None),
            P("section", None),
            P("section", None, None, "fsdp"),
            P("section", "fsdp", None),
        ),
        check_vma=False,
    )
```

```python
import functools

import jax
import jax.numpy as jnp
from jax import lax
from jax.experimental import pallas as pl
from jax.experimental.pallas import tpu as pltpu
from jax.sharding import PartitionSpec as P

D = 1024
H = 8
HD = 128
PACK = 256
ROWS = 64
UNIT = 48
QW = 896
MESH = pl.DeviceIdType.MESH
F32, BF16 = jnp.float32, jnp.bfloat16
VMEM = pl.BlockSpec(memory_space=pltpu.VMEM)
SMEM = pl.BlockSpec(memory_space=pltpu.SMEM)
ANY = pl.BlockSpec(memory_space=pl.ANY)
VMEM_BYTES = 60 * 1024 * 1024


def sds(shape, dtype):
    return jax.ShapeDtypeStruct(shape, dtype)


def dot(left, right, dims):
    return lax.dot_general(left, right, (dims, ((), ())), preferred_element_type=F32)


NN = ((1,), (0,))
NT = ((1,), (1,))
TN = ((0,), (0,))


def halves(value):
    high = value.astype(BF16)
    return high, (value - high.astype(F32)).astype(BF16)


def dot3(left, right, dims):
    return dot(left[0], right[0], dims) + (
        dot(left[0], right[1], dims) + dot(left[1], right[0], dims)
    )


def place():
    fsdp = lax.axis_index("fsdp")
    return (
        lax.axis_index("section"),
        lax.axis_index("seq"),
        lax.div(fsdp, 4),
        lax.rem(fsdp, 4),
    )


def along_x(seq, step):
    return {"seq": lax.rem(seq + step, 4)}


def along_y(z, y, step):
    return {"fsdp": z * 4 + lax.rem(y + step, 4)}


def along_z(z, y, step):
    return {"fsdp": lax.rem(z + step, 4) * 4 + y}


def greet(peers):
    barrier = pltpu.get_barrier_semaphore()
    for peer in peers:
        pl.semaphore_signal(barrier, inc=1, device_id=peer, device_id_type=MESH)
    pl.semaphore_wait(barrier, len(peers))


def remote(source, target, send, recv, peer):
    return pltpu.make_async_remote_copy(
        src_ref=source,
        dst_ref=target,
        send_sem=send,
        recv_sem=recv,
        device_id=peer,
        device_id_type=MESH,
    )


CUT = 80


class Direct:
    def __init__(self, sems, peers, source, target):
        self.copies = [sems.copy(source(k), target(k), peer) for k, peer in enumerate(peers)]

    def start(self):
        for k in (1, 0, 2):
            self.copies[k].start()

    def arrive(self):
        for copy in self.copies:
            copy.wait_recv()

    def sent(self):
        for copy in self.copies:
            copy.wait_send()


class RingReduce:
    def __init__(self, sems, me, right, left, part, near, from_left, from_right):
        at_right, at_left = lax.rem(me + 1, 4), lax.rem(me + 3, 4)
        opposite = lax.rem(me + 2, 4)
        self.me, self.part, self.near = me, part, near
        self.from_left, self.from_right = from_left, from_right
        self.at_right, self.at_left = at_right, at_left
        self.first = [
            sems.copy(part(opposite, 0), near(0), right),
            sems.copy(part(opposite, 1), near(1), left),
            sems.copy(part(at_right, 1), from_left(1), right),
            sems.copy(part(at_left, 0), from_right(0), left),
        ]
        self.second = [
            sems.copy(part(at_right, 0), from_left(0), right),
            sems.copy(part(at_left, 1), from_right(1), left),
        ]

    def start(self):
        for copy in self.first:
            copy.start()

    def middle(self):
        for half, index in ((0, self.at_right), (1, self.at_left)):
            self.first[half].wait_recv()
            add_into(self.part(index, half), [self.near(half)])
            self.second[half].start()

    def total(self):
        for copy in self.first[2:] + self.second:
            copy.wait_recv()
        for half in (0, 1):
            add_into(self.part(self.me, half), [self.from_left(half), self.from_right(half)])

    def sent(self):
        for copy in self.first + self.second:
            copy.wait_send()


class Semaphores:
    def __init__(self, send, recv):
        self.send, self.recv, self.used = send, recv, 0

    def copy(self, source, target, peer):
        index = self.used
        self.used += 1
        return remote(source, target, self.send.at[index], self.recv.at[index], peer)


def add_into(target, others):
    shape = target.shape
    if len(shape) == 2:
        value = target[...].astype(F32)
        for other in others:
            value = value + other[...].astype(F32)
        target[...] = value.astype(target.dtype)
        return

    def body(index, carry):
        add_into(target.at[index], [other.at[index] for other in others])
        return carry

    lax.fori_loop(0, shape[0], body, 0)


def rms(value):
    return lax.rsqrt(jnp.mean(value * value, axis=-1, keepdims=True) + 1e-06)


def rms_back(grad, value, scale, gain):
    weighted = grad * gain
    inner = jnp.mean(weighted * value, axis=-1, keepdims=True)
    return (
        scale * weighted - value * (scale * scale * scale) * inner,
        jnp.sum(grad * value * scale, axis=0, keepdims=True),
    )


def shifted(value, step):
    rows = value.shape[0]
    filler = jnp.zeros((abs(step), value.shape[1]), value.dtype)
    if step > 0:
        return jnp.concatenate([filler, value[: rows - step]], axis=0)
    return jnp.concatenate([value[-step:], filler], axis=0)


def doc_places(doc_len):
    col = lax.broadcasted_iota(jnp.int32, (PACK, 1), 0)
    row = lax.broadcasted_iota(jnp.int32, (1, PACK), 1)
    start_col, start_row = jnp.zeros_like(col), jnp.zeros_like(row)
    end = 0
    for doc in range(4):
        end = end + doc_len[doc]
        start_col = jnp.where(col >= end, end, start_col)
        start_row = jnp.where(row >= end, end, start_row)
    return col - start_col, start_col == start_row


def one_hot(column, row):
    return (column == row).astype(F32).astype(BF16)


def sigmoid(value):
    return 1.0 / (1.0 + jnp.exp(-value))


def conv_taps(small_ref, layer, tap, part):
    return small_ref[layer, 4 + tap * 3 + part : 5 + tap * 3 + part, 0:256]


def conv_part(series, small_ref, layer, part, offset):
    total = series * conv_taps(small_ref, layer, 0, part)
    for tap in range(1, 4):
        moved = jnp.where(offset >= tap, shifted(series, tap), 0.0)
        total = total + moved * conv_taps(small_ref, layer, tap, part)
    return total


def unit(value):
    scale = lax.rsqrt(jnp.sum(value * value, axis=-1, keepdims=True) + 1e-06)
    return value * scale, scale


def inverses(systems):
    col, row = masks()
    apart = col ^ row
    identity = jnp.where(col == row, 1.0, 0.0)
    rough = [(identity - jnp.where(apart == 1, system, 0.0)).astype(BF16) for system in systems]
    for level in range(1, 8):
        mask = (apart >> level) == 1
        corner = [jnp.where(mask, system, 0.0).astype(BF16) for system in systems]
        inner = [dot(c, r, NN).astype(BF16) for c, r in zip(corner, rough)]
        rough = [r - dot(r, i, NN).astype(BF16) for r, i in zip(rough, inner)]
    split = [halves(system) for system in systems]
    left = [
        identity - r.astype(F32) - (dot(high, r, NN) + dot(low, r, NN))
        for r, (high, low) in zip(rough, split)
    ]
    return [r.astype(F32) + dot(r, rest.astype(BF16), NN) for r, rest in zip(rough, left)]


def masks():
    col = lax.broadcasted_iota(jnp.int32, (PACK, PACK), 0)
    row = lax.broadcasted_iota(jnp.int32, (PACK, PACK), 1)
    return col, row


def to_places(perm_row):
    return one_hot(lax.broadcasted_iota(jnp.int32, (PACK, 1), 0), perm_row)


def norm_rows(s, layer, half):
    x = s.rows_in[layer, :, half, :].reshape(PACK // 2, D).astype(F32)
    x = (x * rms(x) * s.small[layer, 0:1, :]).astype(BF16)
    s.normed[layer, :, half, :] = x.reshape(4, ROWS // 2, D)


def project_whole(s, layer):
    normed = s.normed[layer].reshape(PACK, D)
    proj = dot(normed, s.wq[layer].reshape(D, QW), NN).astype(BF16)
    s.stored[...] = proj.reshape(4, ROWS, QW)


def project(s, layer, half):
    normed = s.normed[layer, :, half, :].reshape(PACK // 2, D)
    proj = dot(normed, s.wq[layer].reshape(D, QW), NN).astype(BF16)
    s.stored[:, half, :] = proj.reshape(4, ROWS // 2, QW)


def mixer_forward(s, perm_row, doc_len, layer):
    small = s.small
    places = to_places(perm_row)
    proj = dot(places, s.stored[...].reshape(PACK, QW), NN)
    s.proj[layer] = proj.astype(BF16)
    offset, same = doc_places(doc_len)
    activated = []
    for kind in range(3):
        pre = conv_part(proj[:, 256 * kind : 256 * kind + 256], small, layer, kind, offset)
        activated.append(pre * sigmoid(pre))
    col, row = masks()
    strict = same & (col > row)
    tri = same & (col >= row)
    lanes = [slice(128 * head, 128 * head + 128) for head in range(2)]
    query = [halves(unit(activated[0][:, at])[0] * HD**-0.5) for at in lanes]
    key = [halves(unit(activated[1][:, at])[0]) for at in lanes]
    strength = [sigmoid(proj[:, 768 + head : 769 + head]) for head in range(2)]
    source = [halves(b * activated[2][:, at]) for b, at in zip(strength, lanes)]
    systems = [jnp.where(strict, b * dot3(k, k, NT), 0.0) for b, k in zip(strength, key)]
    scores = [halves(jnp.where(tri, dot3(q, k, NT), 0.0)) for q, k in zip(query, key)]
    solved = inverses(systems)
    fresh = [dot3(halves(t), r, NN) for t, r in zip(solved, source)]
    produced = [dot3(p, halves(u), NN) for p, u in zip(scores, fresh)]
    heads = []
    for head in range(2):
        s.solved[layer, head] = solved[head]
        s.fresh[layer, head] = fresh[head]
        s.produced[layer, head] = produced[head]
        out = produced[head]
        scale = lax.rsqrt(jnp.mean(out * out, axis=-1, keepdims=True) + 1e-05)
        heads.append((out * scale * small[layer, 2:3, 0:128]).astype(BF16))
    mixed = jnp.concatenate(heads, axis=1)
    s.att[layer] = dot(places, mixed, TN).astype(BF16).reshape(4, ROWS, 256)


def mixer_backward(s, perm_row, doc_len, layer):
    small = s.small
    grad = s.branch[layer].reshape(PACK, D)
    grad_att = dot(grad, s.wo[layer].reshape(256, D), NT).astype(BF16)
    places = to_places(perm_row)
    grad_att = dot(places, grad_att, NN)
    proj = s.proj[layer].astype(F32)
    offset, same = doc_places(doc_len)
    pres, gates = [], []
    for kind in range(3):
        pre = conv_part(proj[:, 256 * kind : 256 * kind + 256], small, layer, kind, offset)
        pres.append(pre)
        gates.append(sigmoid(pre))
    col, row = masks()
    strict = same & (col > row)
    tri = same & (col >= row)
    gain = small[layer, 2:3, 0:128]
    both = range(2)
    lanes = [slice(128 * head, 128 * head + 128) for head in both]
    acts = [pre * gate for pre, gate in zip(pres, gates)]
    act_q, act_k, value = [[act[:, at] for at in lanes] for act in acts]
    unit_q, unit_k = [unit(a) for a in act_q], [unit(a) for a in act_k]
    query = [halves(q * HD**-0.5) for q, _ in unit_q]
    key = [halves(k) for k, _ in unit_k]
    strength = [sigmoid(proj[:, 768 + head : 769 + head]) for head in both]
    gain_grad = jnp.zeros((1, HD), F32)
    grad_o = []
    for head in both:
        produced = s.produced[layer, head]
        scale = lax.rsqrt(jnp.mean(produced * produced, axis=-1, keepdims=True) + 1e-05)
        given = grad_att[:, lanes[head]]
        weighted = given * gain
        inner = jnp.mean(weighted * produced, axis=-1, keepdims=True)
        grad_o.append(halves(scale * weighted - produced * (scale * scale * scale) * inner))
        gain_grad = gain_grad + jnp.sum(given * produced * scale, axis=0, keepdims=True)
    fresh = [halves(s.fresh[layer, head]) for head in both]
    scores = [
        jnp.where(tri, dot(query[h][0], key[h][0], NT), 0.0).astype(BF16) for h in both
    ]
    grad_fresh = [halves(dot(scores[h], grad_o[h][0], TN)) for h in both]
    gram = [dot3(key[h], key[h], NT) for h in both]
    grad_scores = [
        jnp.where(tri, dot(grad_o[h][0], fresh[h][0], NT), 0.0).astype(BF16) for h in both
    ]
    grad_source = [dot3(halves(s.solved[layer, h]), grad_fresh[h], TN) for h in both]
    grad_query = [dot(grad_scores[h], key[h][0], NN) for h in both]
    grad_system = [
        jnp.where(strict, -dot3(halves(grad_source[h]), fresh[h], NT), 0.0) for h in both
    ]
    grad_key = [dot(grad_scores[h], query[h][0], TN) for h in both]
    grad_gram = [(strength[h] * grad_system[h]).astype(BF16) for h in both]
    grad_key = [
        grad_key[h] + dot(grad_gram[h], key[h][0], NN) + dot(grad_gram[h], key[h][0], TN)
        for h in both
    ]
    grads = [[], [], []]
    logit_grads = []
    for h in both:
        grad_strength = jnp.sum(grad_source[h] * value[h], axis=-1, keepdims=True) + jnp.sum(
            grad_system[h] * gram[h], axis=-1, keepdims=True
        )
        logit_grads.append(grad_strength * strength[h] * (1.0 - strength[h]))
        for kind, act, scale, grad in (
            (0, act_q[h], unit_q[h][1], grad_query[h] * HD**-0.5),
            (1, act_k[h], unit_k[h][1], grad_key[h]),
        ):
            along = jnp.sum(act * grad, axis=-1, keepdims=True)
            grads[kind].append(scale * grad - act * (scale * scale * scale) * along)
        grads[2].append(strength[h] * grad_source[h])
    dsmall = s.dsmall.at[layer]
    dsmall[...] = jnp.zeros((8, D), F32)
    dsmall[2:3, 0:128] = gain_grad
    pieces = []
    for kind in range(3):
        pre, gate = pres[kind], gates[kind]
        grad_pre = jnp.concatenate(grads[kind], axis=1) * gate * (1.0 + pre * (1.0 - gate))
        series = proj[:, 256 * kind : 256 * kind + 256]
        total = grad_pre * conv_taps(small, layer, 0, kind)
        dsmall[3 + kind : 4 + kind, 0:256] = jnp.sum(grad_pre * series, axis=0, keepdims=True)
        for tap in range(1, 4):
            kept = jnp.where(offset >= tap, grad_pre, 0.0)
            total = total + shifted(kept, -tap) * conv_taps(small, layer, tap, kind)
            dsmall[3 + kind : 4 + kind, 256 * tap : 256 * tap + 256] = jnp.sum(
                kept * shifted(series, tap), axis=0, keepdims=True
            )
        pieces.append(total.astype(BF16))
    lane = lax.broadcasted_iota(jnp.int32, (1, 128), 1)
    pieces.append(
        jnp.where(lane == 0, logit_grads[0], jnp.where(lane == 1, logit_grads[1], 0.0)).astype(BF16)
    )
    grad_proj = jnp.concatenate(pieces, axis=1)
    s.grad_proj[...] = dot(places, grad_proj, TN).astype(BF16).reshape(4, ROWS, QW)


def units(weights, layer, kind):
    return weights[layer, :, :, UNIT * kind : UNIT * kind + UNIT, :].reshape(768, D)


def half_of(ref, layer, half):
    return ref[layer, :, half, :].reshape(PACK // 2, ref.shape[-1])


def put_half(ref, layer, half, value):
    ref[layer, :, half, :] = value.reshape(4, ROWS // 2, ref.shape[-1])


def ffn_forward(s, layer, half):
    normed = half_of(s.normed_ffn, layer, half)
    gate = dot(normed, units(s.wf, layer, 0), NT)
    up = dot(normed, units(s.wf, layer, 1), NT)
    put_half(s.gate, layer, half, gate)
    put_half(s.up, layer, half, up)
    hidden = (gate * sigmoid(gate) * up).astype(BF16)
    return dot(hidden, units(s.wf, layer, 2), NN)


def ffn_backward(s, layer, half):
    grad = half_of(s.outer, layer, half)
    gate, up = half_of(s.gate, layer, half), half_of(s.up, layer, half)
    sig = sigmoid(gate)
    grad_hidden = dot(grad, units(s.wf, layer, 2), NT)
    grad_gate = (grad_hidden * up * sig * (1.0 + gate * (1.0 - sig))).astype(BF16)
    grad_up = (grad_hidden * gate * sig).astype(BF16)
    put_half(s.unit_grads, 0, half, grad_gate)
    put_half(s.unit_grads, 1, half, grad_up)
    put_half(s.unit_grads, 2, half, (gate * sig * up).astype(BF16))
    return dot(grad_gate, units(s.wf, layer, 0), NN) + dot(grad_up, units(s.wf, layer, 1), NN)


def ffn_weights(s, layer, kind):
    right = (s.outer if kind == 2 else s.normed_ffn)[layer].reshape(PACK, D)
    s.dwf[layer, :, :, UNIT * kind : UNIT * kind + UNIT, :] = (
        dot(s.unit_grads[kind].reshape(PACK, 768), right, TN).astype(BF16).reshape(4, 4, UNIT, D)
    )


def mixer_weights(s, layer):
    s.dwo[layer] = (
        dot(s.att[layer].reshape(PACK, 256), s.branch[layer].reshape(PACK, D), TN).astype(BF16).reshape(4, 64, D)
    )
    s.dwq[layer] = (
        dot(s.normed[layer].reshape(PACK, D), s.grad_proj[...].reshape(PACK, QW), TN)
        .astype(BF16)
        .reshape(4, 4, 64, QW)
    )


SCRATCH = [
    ("rows_in", (2, 4, ROWS, D), BF16),
    ("outer", (2, 4, ROWS, D), BF16),
    ("normed_ffn", (2, 4, ROWS, D), BF16),
    ("branch", (2, 4, ROWS, D), BF16),
    ("small", (2, 16, D), F32),
    ("own_q", (64, QW), BF16),
    ("own_f", (3 * UNIT, D), BF16),
    ("raw_ffn", (2, 176, D), BF16),
    ("raw_down", (176, D), BF16),
    ("wq", (2, 4, 4, 64, QW), BF16),
    ("wf", (2, 4, 4, 3 * UNIT, D), BF16),
    ("wo", (2, 4, 64, D), BF16),
    ("dwq", (2, 4, 4, 64, QW), BF16),
    ("dwf", (2, 4, 4, 3 * UNIT, D), BF16),
    ("dwo", (2, 4, 64, D), BF16),
    ("normed", (2, 4, ROWS, D), BF16),
    ("stored", (4, ROWS, QW), BF16),
    ("proj", (2, PACK, QW), BF16),
    ("solved", (2, 2, PACK, PACK), F32),
    ("fresh", (2, 2, PACK, HD), F32),
    ("produced", (2, 2, PACK, HD), F32),
    ("att", (2, 4, ROWS, 256), BF16),
    ("gate", (2, 4, ROWS, 768), F32),
    ("up", (2, 4, ROWS, 768), F32),
    ("unit_grads", (3, 4, ROWS, 768), BF16),
    ("grad_proj", (4, ROWS, QW), BF16),
    ("residual", (2, ROWS, D), F32),
    ("grad_residual", (ROWS, D), F32),
    ("part", (2, 4, ROWS, D), BF16),
    ("landing", (2, 3, ROWS, D), BF16),
    ("final", (2, ROWS, D), BF16),
    ("dsmall", (2, 8, D), F32),
    ("small_sum", (3, 8, D), F32),
    ("small_in", (7, 8, D), F32),
    ("q_in", (2, 3, 4, 32, QW), BF16),
    ("g_in", (3, 4, CUT, D), BF16),
    ("o_in", (2, 3, 64, D), BF16),
    ("q_in2", (2, 3, 32, QW), BF16),
    ("g_in2", (3, CUT, D), BF16),
    ("o_in2", (2, 3, 64, D), BF16),
]
N_SEM = 420


class Refs:
    pass


def pick(rows, columns, first):
    row = lax.broadcasted_iota(jnp.int32, (rows, columns), 0)
    column = lax.broadcasted_iota(jnp.int32, (rows, columns), 1)
    return one_hot(column, row + first)


def pick_columns(count, first):
    row = lax.broadcasted_iota(jnp.int32, (count, 128), 0)
    column = lax.broadcasted_iota(jnp.int32, (count, 128), 1)
    return ((row == first + column) & (column < 2)).astype(F32).astype(BF16)


def program_kernel(*refs):
    (
        block_in,
        cotangent,
        perm_ref,
        doc_ref,
        norm_in,
        w_qkv,
        w_beta,
        conv_w,
        norm_head,
        w_out,
        norm_ffn,
        w_ffn,
        w_down,
    ) = refs[:13]
    rows_out, small_out, q_out, f_out, o_out = refs[13:18]
    s = Refs()
    for (name, _, _), ref in zip(SCRATCH, refs[18:]):
        setattr(s, name, ref)
    send, recv, local, credit = refs[18 + len(SCRATCH) :]
    sems = Semaphores(send, recv)
    core, seq, z, y = place()
    partner = {"section": 1 - core}
    x_peers = [along_x(seq, k) for k in (1, 2, 3)]
    y_peers = [along_y(z, y, k) for k in (1, 2, 3)]
    z_peers = [along_z(z, y, k) for k in (1, 2, 3)]
    perm_row = perm_ref[core]
    perms = (perm_row, [doc_ref[core, 0, k] for k in range(4)])
    x_ref, cot_ref, o_ref = block_in.at[core, 0], cotangent.at[core, 0], w_out.at[0]

    def gather(peers, source, target):
        return Direct(sems, peers, lambda k: source, lambda k: target)

    low, high = pl.ds(0, 32), pl.ds(32, 32)
    f_low, f_high = pl.ds(0, CUT), pl.ds(CUT, 3 * UNIT - CUT)

    def on_core(which):
        return pl.when(core == which)

    def on(which, peers):
        return [{**peer, "section": which} for peer in peers]

    own_q = [
        pltpu.make_async_copy(
            w_qkv.at[0, :, pl.ds(pl.multiple_of(D * kind + 256 * seq, 256), 256)],
            s.own_q.at[:, pl.ds(256 * kind, 256)],
            local.at[kind],
        )
        for kind in range(3)
    ]
    for copy in own_q:
        copy.start()
    own_x = pltpu.make_async_copy(x_ref, s.rows_in.at[0, seq], local.at[3])
    own_cot = pltpu.make_async_copy(cot_ref, s.outer.at[1, seq], local.at[4])
    own_o = pltpu.make_async_copy(o_ref, s.wo.at[1, y], local.at[5])
    own_x.start()
    own_raw = [
        pltpu.make_async_copy(w_ffn.at[0], s.raw_ffn, local.at[12]),
        pltpu.make_async_copy(w_down.at[0], s.raw_down, local.at[13]),
    ]
    for copy in own_raw:
        copy.start()
    own_cot.start()

    greet(
        [partner]
        + [peer for peers in (x_peers, y_peers, z_peers) for c in (0, 1) for peer in on(c, peers)]
    )
    x_gather = gather(x_peers, x_ref, s.rows_in.at[0, seq])
    cot_gather = gather(x_peers, cot_ref, s.outer.at[1, seq])
    pair_small = sems.copy(s.small.at[core], s.small.at[core], partner)
    x_gather.start()

    class Weights:
        def __init__(self, layer):
            self.layer = layer
            wq, wf, wo = s.wq.at[layer], s.wf.at[layer], s.wo.at[layer]
            self.wo = wo
            axes = (y_peers, z_peers)

            def first(source, target, rows):
                return [
                    [
                        sems.copy(source.at[part], target.at[z, y, part], peer)
                        for peer in on(which, axes[which])
                        + ([partner] if which != layer else [])
                    ]
                    for which, part in enumerate(rows)
                ]

            def second(target, rows):
                return [
                    gather(z_peers, target.at[z, :, rows[0]], target.at[z, :, rows[0]]),
                    gather(y_peers, target.at[:, y, rows[1]], target.at[:, y, rows[1]]),
                ]

            def pairs(target, rows):
                pieces = [
                    [target.at[lax.rem(z + 4 - k, 4), :, rows[0]] for k in range(4)],
                    [target.at[:, lax.rem(y + 4 - k, 4), rows[1]] for k in range(4)],
                ]
                return [[sems.copy(piece, piece, partner) for piece in part] for part in pieces]

            q_rows, f_rows = (low, high), (f_low, f_high)
            self.q_one, self.q_two = first(s.own_q, wq, q_rows), second(wq, q_rows)
            self.f_one, self.f_two = first(s.own_f, wf, f_rows), second(wf, f_rows)
            self.pair_q, self.pair_f = pairs(wq, q_rows), pairs(wf, f_rows)
            self.o_one = [sems.copy(o_ref, wo.at[y], peer) for peer in on(1, z_peers)]
            if layer == 0:
                self.o_pair = sems.copy(o_ref, wo.at[y], partner)
            self.o_two = gather(y_peers, wo.at[y], wo.at[y])
            self.pair_o = sems.copy(wo, wo, partner)

        def first_q(self):
            @on_core(self.layer)
            def _():
                for copies in self.q_one:
                    for copy in copies:
                        copy.start()

        def first_f(self):
            @on_core(self.layer)
            def _():
                @pl.when(z == seq)
                def _():
                    for copy in self.o_one:
                        copy.start()
                    if self.layer == 0:
                        self.o_pair.start()
                    else:
                        own_o.start()

                for copies in self.f_one:
                    for copy in copies:
                        copy.start()

        def second_of(self, one, two, pair):
            for which in (0, 1):

                @on_core(which)
                def _():
                    for copy in one[which]:
                        copy.wait_recv()
                    two[which].start()
                    pair[which][0].start()

        def second_q(self):
            self.second_of(self.q_one, self.q_two, self.pair_q)

        def second_f(self):
            self.second_of(self.f_one, self.f_two, self.pair_f)

        def second_o(self):
            @on_core(1)
            def _():
                @pl.when(z == seq)
                def _():
                    if self.layer == 0:
                        self.o_pair.wait_recv()
                    else:
                        own_o.wait()

                for k in range(3):

                    @pl.when(lax.rem(seq + k + 1, 4) == z)
                    def _():
                        self.o_one[k].wait_recv()

                self.o_two.start()

        def third_of(self, two, pair):
            for which in (0, 1):

                @on_core(which)
                def _():
                    for k in (0, 2, 1):
                        two[which].copies[k].wait_recv()
                        pair[which][k + 1].start()

        def third_q(self):
            self.third_of(self.q_two, self.pair_q)

        def third_f(self):
            self.third_of(self.f_two, self.pair_f)

        def third_o(self):
            @on_core(1)
            def _():
                self.o_two.arrive()
                self.pair_o.start()

        def arrived(self, pair, with_o):
            for which in (0, 1):

                @on_core(1 - which)
                def _():
                    for copy in pair[which]:
                        copy.wait_recv()
                    if with_o and which == 1:
                        self.pair_o.wait_recv()

        def arrived_q(self):
            self.arrived(self.pair_q, True)

        def arrived_f(self):
            self.arrived(self.pair_f, False)

        def sent(self):
            @on_core(self.layer)
            def _():
                for copies in self.q_one + self.f_one:
                    for copy in copies:
                        copy.wait_send()

                @pl.when(z == seq)
                def _():
                    for copy in self.o_one:
                        copy.wait_send()
                    if self.layer == 0:
                        self.o_pair.wait_send()

            for which in (0, 1):

                @on_core(which)
                def _():
                    for ring in (self.q_two[which], self.f_two[which]):
                        ring.sent()
                    for copy in self.pair_q[which] + self.pair_f[which]:
                        copy.wait_send()
                    if which == 1:
                        self.o_two.sent()
                        self.pair_o.wait_send()

    weights = [Weights(0), Weights(1)]

    both_halves = (low, high)

    def start_rows(turn, half, value):
        part, landing = s.part.at[turn % 2], s.landing.at[turn % 2]
        part[:, half, :] = value.astype(BF16).reshape(4, ROWS // 2, D)
        ring = Direct(
            sems,
            x_peers,
            lambda k: part.at[lax.rem(seq + k + 1, 4), half],
            lambda k: landing.at[k, half],
        )
        ring.start()
        return ring

    def rows_total(turn, half, ring):
        ring.arrive()
        total = s.part[turn % 2, seq, half].astype(F32)
        for k in range(3):
            total = total + s.landing[turn % 2, k, half].astype(F32)
        return total

    def send_rows(place_of, half):
        ring = gather(x_peers, place_of.at[seq, half], place_of.at[seq, half])
        ring.start()
        return ring

    def all_sent(rings):
        for ring in rings:
            ring.sent()

    def sum_over(ring, target, landing):
        ring.arrive()
        add_into(target, [landing.at[k] for k in range(3)])

    def scatter(peers, me, part, landing):
        return Direct(
            sems, peers, lambda k: part(lax.rem(me + k + 1, 4)), lambda k: landing.at[k]
        )

    class Gradients:
        def __init__(self, layer):
            self.layer = layer
            dq, df, do = s.dwq.at[layer], s.dwf.at[layer], s.dwo.at[layer]
            lq, lf, lo = s.wq.at[1], s.wf.at[1], s.wo.at[1]
            self.dq, self.df, self.do = dq, df, do
            self.q_in, self.o_in = s.q_in.at[layer], s.o_in.at[layer]
            self.q_in2, self.o_in2 = s.q_in2.at[layer], s.o_in2.at[layer]
            self.lq, self.lf, self.lo = lq, lf, lo
            self.q_rows, self.f_rows = (low, high), (f_low, f_high)

            def pair_f(first, count):
                rows = pl.ds(first, count)
                return sems.copy(df.at[:, :, rows], lf.at[:, :, rows], partner)

            self.pair_f = [
                [pair_f(0, UNIT), pair_f(UNIT, CUT - UNIT)],
                [pair_f(2 * UNIT, UNIT), pair_f(CUT, 2 * UNIT - CUT)],
            ]
            self.pair_q = [sems.copy(dq.at[:, :, half], lq.at[:, :, half], partner) for half in self.q_rows]
            self.pair_o = sems.copy(do, lo, partner)
            def ring_of(me, right, left, part, rows):
                def block(which):
                    return lambda half: s.g_in.at[which, pl.ds(2 * half, 2), rows]

                return RingReduce(sems, me, right, left, part, block(0), block(1), block(2))

            self.f_one = [
                ring_of(
                    z,
                    z_peers[0],
                    z_peers[2],
                    lambda j, half: df.at[j, pl.ds(2 * half, 2), f_low],
                    pl.ds(0, CUT),
                ),
                ring_of(
                    y,
                    y_peers[0],
                    y_peers[2],
                    lambda j, half: df.at[pl.ds(2 * half, 2), j, f_high],
                    pl.ds(0, 3 * UNIT - CUT),
                ),
            ]
            self.f_two = [
                scatter(y_peers, y, lambda j: df.at[z, j, f_low], s.g_in2),
                scatter(z_peers, z, lambda j: df.at[j, y, f_high], s.g_in2.at[:, pl.ds(0, 3 * UNIT - CUT)]),
            ]
            self.q_one = [
                scatter(z_peers, z, lambda j: dq.at[j, :, low], self.q_in),
                scatter(y_peers, y, lambda j: dq.at[:, j, high], self.q_in),
            ]
            self.q_two = [
                scatter(y_peers, y, lambda j: dq.at[z, j, low], self.q_in2),
                scatter(z_peers, z, lambda j: dq.at[j, y, high], self.q_in2),
            ]
            self.o_one = scatter(y_peers, y, lambda j: do.at[j], self.o_in)
            self.o_two = [
                sems.copy(do.at[y], self.o_in2.at[k], along_z(z, y, 3 - k)) for k in range(3)
            ]
            holders = [{**peer, "section": layer} for peer in x_peers]

            def to_holders(which, source, target, index):
                copies = [sems.copy(source, target, peer) for peer in holders]
                if which == layer:
                    return copies, pltpu.make_async_copy(source, target, local.at[index])
                return copies, sems.copy(source, target, partner)

            self.q_three = [
                to_holders(which, dq.at[z, y, half], q_out.at[seq, half], 6)
                for which, half in enumerate(self.q_rows)
            ]
            self.f_three = [
                to_holders(which, df.at[z, y, rows], f_out.at[seq, rows], 7)
                for which, rows in enumerate(self.f_rows)
            ]
            self.o_three = to_holders(1, do.at[y], o_out, 8)

        def free(self, index):
            pl.semaphore_signal(credit.at[index], inc=1, device_id=partner, device_id_type=MESH)

        def taken(self, index):
            pl.semaphore_wait(credit.at[index], 1)

        def hand_f(self, which, index):
            @on_core(1 - which)
            def _():
                self.pair_f[which][index].start()

        def hand_q(self):
            for which in (0, 1):

                @on_core(1 - which)
                def _():
                    self.pair_q[which].start()
                    if which == 1:
                        self.pair_o.start()

        def f_first(self):
            for which, rows in enumerate(self.f_rows):

                @on_core(which)
                def _():
                    for copy in self.pair_f[which]:
                        copy.wait_recv()
                    add_into(self.df.at[:, :, rows], [self.lf.at[:, :, rows]])
                    self.f_one[which].start()

        def q_first(self):
            for which, half in enumerate(self.q_rows):

                @on_core(which)
                def _():
                    self.pair_q[which].wait_recv()
                    add_into(self.dq.at[:, :, half], [self.lq.at[:, :, half]])
                    self.q_one[which].start()
                    if which == 1:
                        self.pair_o.wait_recv()
                        add_into(self.do, [self.lo])
                        self.o_one.start()

        def f_middle(self):
            for which in (0, 1):

                @on_core(which)
                def _():
                    self.f_one[which].middle()

        def f_second(self):
            for which in (0, 1):

                @on_core(which)
                def _():
                    self.f_one[which].total()
                    self.f_two[which].start()

        def q_second(self):
            @on_core(0)
            def _():
                sum_over(self.q_one[0], self.dq.at[z, :, low], self.q_in)
                self.q_two[0].start()

            @on_core(1)
            def _():
                sum_over(self.q_one[1], self.dq.at[:, y, high], self.q_in)
                self.q_two[1].start()
                sum_over(self.o_one, self.do.at[y], self.o_in)
                for k in range(3):

                    @pl.when(lax.rem(z + 3 - k, 4) == seq)
                    def _():
                        self.o_two[k].start()

        def f_third(self):
            for which, rows, landing in ((0, f_low, s.g_in2), (1, f_high, s.g_in2.at[:, pl.ds(0, 3 * UNIT - CUT)])):

                @on_core(which)
                def _():
                    sum_over(self.f_two[which], self.df.at[z, y, rows], landing)

        def f_out(self):
            for which in (0, 1):

                @on_core(which)
                def _():
                    copies, here = self.f_three[which]
                    for copy in copies + [here]:
                        copy.start()

        def q_third(self):
            for which, half in enumerate(self.q_rows):

                @on_core(which)
                def _():
                    sum_over(self.q_two[which], self.dq.at[z, y, half], self.q_in2)

        def q_out(self):
            for which in (0, 1):

                @on_core(which)
                def _():
                    copies, here = self.q_three[which]
                    for copy in copies + [here]:
                        copy.start()
                    if which == 1:

                        @pl.when(z == seq)
                        def _():
                            for k in range(3):
                                self.o_two[k].wait_recv()
                            add_into(self.do.at[y], [self.o_in2.at[k] for k in range(3)])
                            copies, here = self.o_three
                            for copy in copies + [here]:
                                copy.start()

        def end(self):
            for which in (0, 1):

                @on_core(which)
                def _():
                    mine = self.layer == which
                    rings = [self.f_one, self.f_two, self.q_one, self.q_two]
                    for ring in rings:
                        ring[which].sent()
                    for copies, here in (self.q_three[which], self.f_three[which]):
                        for copy in copies:
                            copy.wait_send()
                        if mine:
                            here.wait()
                        else:
                            here.wait_send()
                    for copy in self.pair_f[1 - which] + [self.pair_q[1 - which]]:
                        copy.wait_send()
                    if which == 0:
                        self.pair_o.wait_send()
                    else:
                        self.o_one.sent()
                        for k in range(3):

                            @pl.when(lax.rem(z + 3 - k, 4) == seq)
                            def _():
                                self.o_two[k].wait_send()

                        @pl.when(z == seq)
                        def _():
                            copies, here = self.o_three
                            for copy in copies:
                                copy.wait_send()
                            if mine:
                                here.wait()
                            else:
                                here.wait_send()

                    if mine:
                        for source in (0, 1):
                            for copies, here in (self.q_three[source], self.f_three[source]):
                                for copy in copies:
                                    copy.wait_recv()
                                if source != which:
                                    here.wait_recv()
                        copies, here = self.o_three
                        for k in range(3):

                            @pl.when(lax.rem(z + k + 1, 4) == seq)
                            def _():
                                copies[k].wait_recv()

                        if which == 0:

                            @pl.when(z == seq)
                            def _():
                                here.wait_recv()

    grads = [Gradients(0), Gradients(1)]

    logit_columns = dot(w_beta[0], pick_columns(8, 2 * seq), TN)
    s.own_q[:, 768:QW] = logit_columns.astype(BF16)
    for copy in own_q:
        copy.wait()
    weights[0].first_q()

    for which, q_part, f_part in ((0, low, f_low), (1, high, f_high)):

        @on_core(which)
        def _():
            s.wq[which, z, y, q_part] = s.own_q[q_part]

    own_small = s.small.at[core]
    own_small[0:1, :] = norm_in[...]
    own_small[1:2, :] = norm_ffn[...]
    own_small[2:3, 0:HD] = norm_head[...]
    for tap in range(4):
        for part in range(3):
            row = 4 + 3 * tap + part
            own_small[row : row + 1, 0:256] = conv_w[
                0, part, tap : tap + 1, pl.ds(pl.multiple_of(256 * seq, 256), 256)
            ]
    pair_small.start()
    mine_of = pick(UNIT, 176, UNIT * seq)
    for copy in own_raw:
        copy.wait()
    for kind in range(2):
        s.own_f[UNIT * kind : UNIT * kind + UNIT, :] = dot(mine_of, s.raw_ffn[kind], NN).astype(BF16)
    s.own_f[2 * UNIT : 3 * UNIT, :] = dot(mine_of, s.raw_down[...], NN).astype(BF16)
    weights[0].first_f()
    for which, f_part in ((0, f_low), (1, f_high)):

        @on_core(which)
        def _():
            s.wf[which, z, y, f_part] = s.own_f[f_part]

    weights[0].second_q()
    own_x.wait()
    x_gather.arrive()
    pair_small.wait_recv()
    for half in both_halves:
        norm_rows(s, 0, half)
    weights[0].second_o()
    weights[0].third_q()
    weights[0].second_f()
    weights[0].third_o()
    weights[1].first_q()
    weights[1].first_f()
    cot_gather.start()
    incoming = []
    for layer in (0, 1):
        weights[layer].arrived_q()
        if layer == 0:
            project_whole(s, 0)
        else:
            for index, half in enumerate(both_halves):
                incoming[index].arrive()
                norm_rows(s, 1, half)
                project(s, 1, half)

        mixer_forward(s, *perms, layer)
        turn = 2 * layer
        reduces = [
            start_rows(turn, half, dot(half_of(s.att, layer, half), s.wo[layer].reshape(256, D), NN))
            for half in both_halves
        ]
        if layer == 0:
            weights[1].second_q()
            weights[0].third_f()
            weights[1].second_o()
            weights[1].second_f()
        gathers = []
        for ring, half in zip(reduces, both_halves):
            total = rows_total(turn, half, ring)
            residual = s.rows_in[layer, seq, half].astype(F32) + total
            s.residual[layer, half] = residual
            s.normed_ffn[layer, seq, half] = (
                residual * rms(residual) * s.small[layer, 1:2, :]
            ).astype(BF16)
            gathers.append(send_rows(s.normed_ffn.at[layer], half))
        all_sent(incoming)

        weights[layer].arrived_f()
        turn = 2 * layer + 1
        more = []
        for ring, half in zip(gathers, both_halves):
            ring.arrive()
            more.append(start_rows(turn, half, ffn_forward(s, layer, half)))
        all_sent(reduces + gathers)
        if layer == 0:
            weights[1].third_q()
            weights[1].third_o()
        incoming = []
        for ring, half in zip(more, both_halves):
            out = (s.residual[layer, half] + rows_total(turn, half, ring)).astype(BF16)
            if layer == 0:
                s.rows_in[1, seq, half] = out
                incoming.append(send_rows(s.rows_in.at[1], half))
            else:
                s.final[0, half] = out
        if layer == 0:
            weights[1].third_f()
        all_sent(more)

    for each in weights:
        each.sent()
    own_cot.wait()
    cot_gather.arrive()
    for layer in (1, 0):
        mine = grads[layer]
        turn = 6 - 2 * layer
        reduces = []
        for index, half in enumerate(both_halves):
            if layer == 0:
                incoming[index].arrive()
            reduces.append(start_rows(turn, half, ffn_backward(s, layer, half)))
        all_sent(incoming)
        mine.free(0)
        if layer == 0:
            mine.free(1)
        ffn_weights(s, layer, 2)
        mine.taken(0)
        mine.hand_f(1, 0)
        ffn_weights(s, layer, 0)
        mine.hand_f(0, 0)
        ffn_weights(s, layer, 1)
        mine.hand_f(0, 1)
        mine.hand_f(1, 1)
        if layer == 0:
            grads[1].f_third()
            grads[1].q_second()
        gathers, gains = [], []
        for ring, half in zip(reduces, both_halves):
            value = s.residual[layer, half]
            grad, gain = rms_back(
                rows_total(turn, half, ring), value, rms(value), s.small[layer, 1:2, :]
            )
            grad = s.outer[layer, seq, half].astype(F32) + grad
            s.grad_residual[half] = grad
            s.branch[layer, seq, half] = grad.astype(BF16)
            gathers.append(send_rows(s.branch.at[layer], half))
            gains.append(gain)
        gain_ffn = gains[0] + gains[1]
        mine.f_first()
        if layer == 0:
            grads[1].q_third()
        for ring in gathers:
            ring.arrive()
        mixer_backward(s, *perms, layer)
        s.dsmall[layer, 1:2, :] = gain_ffn
        all_sent(reduces + gathers)
        mine.f_middle()
        if layer == 0:
            mixer_weights(s, 0)
            mine.taken(1)
            mine.hand_q()

        turn = 7 - 2 * layer
        reduces = [
            start_rows(
                turn,
                half,
                dot(
                    s.grad_proj[:, half, :].reshape(PACK // 2, QW),
                    s.wq[layer].reshape(D, QW),
                    NT,
                ),
            )
            for half in both_halves
        ]
        if layer == 1:
            mine.free(1)
            mixer_weights(s, 1)
            mine.taken(1)
            mine.hand_q()
        else:
            mine.q_first()
        incoming, gains = [], []
        for ring, half in zip(reduces, both_halves):
            value = s.rows_in[layer, seq, half].astype(F32)
            grad, gain = rms_back(
                rows_total(turn, half, ring), value, rms(value), s.small[layer, 0:1, :]
            )
            grad = (s.grad_residual[half] + grad).astype(BF16)
            if layer == 1:
                s.outer[0, seq, half] = grad
                incoming.append(send_rows(s.outer.at[0], half))
            else:
                s.final[1, half] = grad
            gains.append(gain)
        s.dsmall[layer, 0:1, :] = gains[0] + gains[1]
        all_sent(reduces)
        if layer == 1:
            mine.f_second()
            mine.q_first()

    rows_copies = [
        pltpu.make_async_copy(s.final.at[k], rows_out.at[k, core], local.at[9 + k]) for k in (0, 1)
    ]
    pair_rows = [sems.copy(s.final.at[k], rows_out.at[k, core], partner) for k in (0, 1)]
    pair_gains = sems.copy(s.dsmall.at[1 - core], s.small_in.at[0], partner)
    pair_gains.start()
    for copy in rows_copies + pair_rows:
        copy.start()
    small_y = Direct(sems, y_peers, lambda k: s.small_sum.at[0], lambda k: s.small_in.at[1 + k])
    small_z = Direct(sems, z_peers, lambda k: s.small_sum.at[1], lambda k: s.small_in.at[4 + k])
    small_x = gather(x_peers, s.small_sum.at[2], small_out.at[seq])
    small_keep = pltpu.make_async_copy(s.small_sum.at[2], small_out.at[seq], local.at[11])
    grads[1].f_out()
    grads[1].q_out()
    grads[0].f_second()
    pair_gains.wait_recv()
    s.small_sum[0] = s.dsmall[core] + s.small_in[0]
    small_y.start()
    grads[0].q_second()
    grads[0].f_third()
    grads[0].f_out()
    small_y.arrive()
    s.small_sum[1] = s.small_sum[0] + s.small_in[1] + s.small_in[2] + s.small_in[3]
    small_z.start()
    grads[0].q_third()
    grads[0].q_out()
    small_z.arrive()
    s.small_sum[2] = s.small_sum[1] + s.small_in[4] + s.small_in[5] + s.small_in[6]
    small_x.start()
    small_keep.start()
    grads[1].end()
    grads[0].end()
    small_x.arrive()
    for copy in pair_rows:
        copy.wait()
    pair_gains.wait_send()
    for ring in (small_y, small_z, small_x, x_gather, cot_gather):
        ring.sent()
    pair_small.wait_send()
    for copy in rows_copies + [small_keep]:
        copy.wait()


def whole_program(*operands):
    return pl.pallas_call(
        program_kernel,
        out_shape=[
            sds((2, 2, ROWS, D), BF16),
            sds((4, 8, D), F32),
            sds((4, 64, QW), BF16),
            sds((4, 3 * UNIT, D), BF16),
            sds((64, D), BF16),
        ],
        in_specs=[ANY, ANY, VMEM, SMEM, VMEM, ANY, VMEM, VMEM, VMEM, ANY, VMEM, ANY, ANY],
        out_specs=[ANY] * 5,
        scratch_shapes=[pltpu.VMEM(shape, dtype) for _, shape, dtype in SCRATCH]
        + [
            pltpu.SemaphoreType.DMA((N_SEM,)),
            pltpu.SemaphoreType.DMA((N_SEM,)),
            pltpu.SemaphoreType.DMA((14,)),
            pltpu.SemaphoreType.REGULAR((2,)),
        ],
        compiler_params=pltpu.CompilerParams(
            collective_id=1, has_side_effects=True, vmem_limit_bytes=VMEM_BYTES
        ),
        name="layers",
    )(*operands)


def finish_kernel(
    rows,
    small,
    q,
    f,
    o,
    block_out,
    input_grad,
    grad_norm_in,
    grad_qkv,
    grad_beta,
    grad_conv,
    grad_norm_head,
    grad_out,
    grad_norm_ffn,
    grad_ffn,
    grad_down,
):
    block_out[:, 0] = rows[0]
    input_grad[:, 0] = rows[1]
    total = small[0] + small[1] + small[2] + small[3]
    grad_norm_in[...] = total[0:1]
    grad_norm_ffn[...] = total[1:2]
    grad_norm_head[...] = total[2:3, 0:HD]
    grad_out[0] = o[...].astype(F32)
    beta = jnp.zeros((8, 64), F32)
    for seq in range(4):
        lanes = slice(256 * seq, 256 * seq + 256)
        for tap in range(4):
            for part in range(3):
                grad_conv[0, part, tap : tap + 1, lanes] = small[
                    seq, 3 + part : 4 + part, 256 * tap : 256 * tap + 256
                ]
        for part in range(3):
            grad_qkv[0, :, D * part + 256 * seq : D * part + 256 * seq + 256] = q[
                seq, :, 256 * part : 256 * part + 256
            ].astype(F32)
        beta = beta + dot(pick_columns(8, 2 * seq), q[seq, :, 768:QW], NT)
    grad_beta[0] = beta
    for kind in range(3):
        whole = f[:, UNIT * kind : UNIT * kind + UNIT, :].reshape(4 * UNIT, D)[:176].astype(F32)
        if kind < 2:
            grad_ffn[0, kind] = whole
        else:
            grad_down[0] = whole


def finish(*operands):
    shapes = [
        ((2, 1, ROWS, D), BF16),
        ((2, 1, ROWS, D), BF16),
        ((1, D), F32),
        ((1, 64, 3 * D), F32),
        ((1, H, 64), F32),
        ((1, 3, 4, D), F32),
        ((1, HD), F32),
        ((1, 64, D), F32),
        ((1, D), F32),
        ((1, 2, 176, D), F32),
        ((1, 176, D), F32),
    ]
    return pl.pallas_call(
        finish_kernel,
        out_shape=[sds(*shape) for shape in shapes],
        in_specs=[VMEM] * 5,
        out_specs=[VMEM] * 11,
        compiler_params=pltpu.CompilerParams(vmem_limit_bytes=VMEM_BYTES),
        name="finish",
    )(*operands)


def local(
    block_in,
    cotangent,
    perm_rows,
    doc_lengths,
    norm_in,
    w_qkv,
    w_beta,
    conv_w,
    norm_head,
    w_out,
    norm_ffn,
    w_ffn,
    w_down,
):
    results = list(finish(
        *whole_program(
            block_in,
            cotangent,
            perm_rows,
            doc_lengths,
            norm_in,
            w_qkv,
            jnp.swapaxes(w_beta, 1, 2),
            jnp.swapaxes(conv_w, 1, 2),
            norm_head,
            w_out,
            norm_ffn,
            jnp.swapaxes(w_ffn, 2, 3),
            w_down,
        )
    ))
    results[4] = jnp.swapaxes(results[4], 1, 2)
    results[5] = jnp.swapaxes(results[5], 1, 2)
    results[9] = jnp.swapaxes(results[9], 2, 3)
    return tuple(results)


def solution(mesh):
    placed = (
        P(None, "fsdp", "seq", None),
        P(None, "fsdp", "seq", None),
        P(None, "fsdp", None),
        P(None, "fsdp", None),
        P("section", None),
        P("section", "fsdp", None),
        P("section", "fsdp", None),
        P("section", None, None, None),
        P("section", None),
        P("section", "fsdp", None),
        P("section", None),
        P("section", None, None, "fsdp"),
        P("section", "fsdp", None),
    )
    return jax.shard_map(
        local,
        mesh=mesh,
        in_specs=placed,
        out_specs=(
            P(None, "fsdp", "seq", None),
            P(None, "fsdp", "seq", None),
            P("section", None),
            P("section", "fsdp", None),
            P("section", "fsdp", None),
            P("section", None, None, None),
            P("section", None),
            P("section", "fsdp", None),
            P("section", None),
            P("section", None, None, "fsdp"),
            P("section", "fsdp", None),
        ),
        check_vma=False,
    )
```
